128 devices in a mesh: head: 4 (over x), inner: 8 (over y, z_hi), outer: 4 (over z_lo, core).
Axes of the slice: x: 4, y: 4, z: 4 (z_hi: 2, z_lo: 2; z = z_hi * 2 + z_lo), core: 2. Of those that a mesh axis runs over, the one named last changes fastest.
Arguments:
- query_rows: bfloat16 [32, 4, 128, 1024], P(('inner', 'outer'), 'head'), may hold values from -6 to 6
- key_rows: bfloat16 [32, 4, 128, 256], P(('inner', 'outer'), 'head'), may hold values from -6 to 6
- value_rows: bfloat16 [32, 4, 128, 256], P(('inner', 'outer'), 'head'), may hold values from -6 to 6
- out_grad: bfloat16 [32, 4, 128, 1024], P(('inner', 'outer'), 'head'), may hold values from -6 to 6
- lengths: int32 [4], replicated, may hold values from 1 to 12288, 16384 in all
Outputs:
- attended: bfloat16 [32, 4, 128, 1024], P(('inner', 'outer'), 'head')
- query_grad: bfloat16 [32, 4, 128, 1024], P(('inner', 'outer'), 'head')
- key_grad: bfloat16 [32, 4, 128, 256], P(('inner', 'outer'), 'head')
- value_grad: bfloat16 [32, 4, 128, 256], P(('inner', 'outer'), 'head')
The draws below stay inside these ranges and needn't reach their ends.
Inputs may be any that keep to these rules, and one draw needn't show every extreme that they name: The 4 lengths sum to 16384; the largest is exactly 12288.
All inputs are finite; a program needn't handle non-finite values.
Results may differ from the reference program's by a relative error of at most 0.03.
Values may be sent and summed in bfloat16 or wider, within the bound.
No kernel may reach another device: no remote copies, remote signals or barrier semaphores. Data moves between devices by JAX's collectives and lax.ppermute only.
A program may use at most 64 MiB of HBM per device.

```python
import math
import jax
import jax.numpy as jnp
import numpy as np
from jax import lax

HEADS = 8
KV_HEADS = 2
HD = 128
TOK_DEV = 128
SLOTS = 4
NCTX = 32
SEQ = 16384
DOCS = 4
DOC_MOST = 12288


def draw_query_rows(key, part):
    key = jax.random.fold_in(key, 3)
    slot_total = SEQ // (NCTX * TOK_DEV)
    shape = (NCTX, slot_total, TOK_DEV, HEADS * HD)
    base = jnp.clip(jax.random.normal(key, shape, jnp.float32), -6.0, 6.0)
    return base.astype(jnp.bfloat16)


def draw_key_rows(key, part):
    key = jax.random.fold_in(key, 4)
    slot_total = SEQ // (NCTX * TOK_DEV)
    shape = (NCTX, slot_total, TOK_DEV, KV_HEADS * HD)
    base = jnp.clip(jax.random.normal(key, shape, jnp.float32), -6.0, 6.0)
    return base.astype(jnp.bfloat16)


def block_levels(rng, dims, shards, smallest, largest):
    gain, own = 1.0, jax.random.fold_in(rng, 6)
    for dim, shards_of in shards:
        draws = jnp.exp(jax.random.uniform(jax.random.fold_in(own, dim), (shards_of,), jnp.float32, smallest / len(shards), largest / len(shards)))
        gain = gain * jnp.repeat(draws, dims[dim] // shards_of).reshape([-1 if axis == dim else 1 for axis in range(len(dims))])
    return gain


def length_profile(number_of, total, most, skew):
    weights = [(1 << 20) // math.isqrt(rank ** skew) + 1 for rank in range(2, number_of + 1)]
    surplus, given = total - most - (number_of - 1), [1] * (number_of - 1)
    while surplus > 0:
        movable = [i for i in range(number_of - 1) if given[i] < most]
        pool, left = sum([weights[i] for i in movable]), surplus
        for i in movable:
            extra = min(most - given[i], max(1, left * weights[i] // pool), surplus)
            given[i] = given[i] + extra
            surplus = surplus - extra
    return np.array([most] + given)


def ragged_sizes(stream_key, count, total, bound, slope):
    if count == 2:
        one = jax.random.randint(stream_key, (), max(1, total - bound), min(bound, total - 1) + 1)
        return jnp.stack([one, total - one])
    tallies = jnp.asarray(length_profile(count, total, bound, slope), jnp.int32)
    pairs = (count - 1) // 2
    giver, receiver = tallies[1:1 + 2 * pairs:2], tallies[2:2 + 2 * pairs:2]
    slack = jnp.minimum(giver - 1, bound - receiver)
    moved = jax.random.randint(jax.random.fold_in(stream_key, 1), (pairs,), 0, 1 << 20) % (slack + 1)
    tallies = tallies.at[1:1 + 2 * pairs:2].set(giver - moved).at[2:2 + 2 * pairs:2].set(receiver + moved)
    return tallies[jax.random.permutation(jax.random.fold_in(stream_key, 2), count)]


def normal_values(key, dims, deviation, bound, pieces=(), kind=jnp.bfloat16):
    factor_of = block_levels(key, dims, pieces, -0.22, 0.18) if pieces else 1.0
    entries = jax.random.normal(key, dims, jnp.float32) * deviation * factor_of
    return jnp.minimum(jnp.maximum(entries, -bound), bound).astype(kind)


def setup_inputs(seed: int = 0) -> dict:
    keys = jax.random.split(jax.random.key(seed), 6)
    query_rows = draw_query_rows(jax.random.fold_in(keys[5], 71), 0)
    key_rows = draw_key_rows(jax.random.fold_in(keys[5], 71), 0)
    value_rows = normal_values(keys[2], (NCTX, SLOTS, TOK_DEV, KV_HEADS * HD), 1.0, 6.0, ((0, 32), (1, 4)))
    out_grad = normal_values(keys[3], (NCTX, SLOTS, TOK_DEV, HEADS * HD), 1.0, 6.0, ((0, 32), (1, 4)))
    lengths = ragged_sizes(keys[4], DOCS, SEQ, DOC_MOST, 2).astype(jnp.int32)
    return {"query_rows": query_rows, "key_rows": key_rows, "value_rows": value_rows, "out_grad": out_grad, "lengths": lengths}


neg_large = -1.0e30


def doc_starts(lengths, positions):
    doc_ends = jnp.cumsum(lengths).astype(jnp.int32)
    picked = jnp.where(doc_ends[None, :] <= positions[:, None], lengths[None, :], 0)
    return jnp.sum(picked, axis=1).astype(jnp.int32)


def reference(query_rows, key_rows, value_rows, out_grad, lengths):
    softmax_scale = HD ** -0.5
    group_size = HEADS // KV_HEADS
    per_slot = HEADS // SLOTS
    run_count = group_size // per_slot
    queries = query_rows.reshape(SEQ, KV_HEADS, group_size, HD)
    grads_in = out_grad.reshape(SEQ, KV_HEADS, group_size, HD)
    block_rows = math.gcd(512, SEQ)
    block_count = SEQ // block_rows
    window = ((DOC_MOST + block_rows - 2) // block_rows + 1) * block_rows
    margin = window - block_rows
    keys_padded = jnp.concatenate([jnp.zeros((margin, KV_HEADS, HD), jnp.bfloat16), key_rows.reshape(SEQ, KV_HEADS, HD)], axis=0)
    values_padded = jnp.concatenate([jnp.zeros((margin, KV_HEADS, HD), jnp.bfloat16), value_rows.reshape(SEQ, KV_HEADS, HD)], axis=0)
    positions = jnp.arange(SEQ, dtype=jnp.int32)
    starts = doc_starts(lengths, positions)

    def visit(totals, block_index):
        key_total, value_total = totals
        first = (block_index * block_rows).astype(jnp.int32)
        query_block = lax.dynamic_slice_in_dim(queries, first, block_rows, 0).astype(jnp.float32)
        grad_block = lax.dynamic_slice_in_dim(grads_in, first, block_rows, 0).astype(jnp.float32)
        key_window = lax.dynamic_slice_in_dim(keys_padded, first, window, 0).astype(jnp.float32)
        value_window = lax.dynamic_slice_in_dim(values_padded, first, window, 0).astype(jnp.float32)
        query_pos = first + jnp.arange(block_rows, dtype=jnp.int32)
        query_start = lax.dynamic_slice_in_dim(starts, first, block_rows, 0)
        key_pos = first - margin + jnp.arange(window, dtype=jnp.int32)
        visible = ((key_pos[None, :] <= query_pos[:, None]) & (key_pos[None, :] >= query_start[:, None]))[:, None, None, :]
        scores = jnp.einsum("qgjd,kgd->qgjk", query_block, key_window) * softmax_scale
        row_max = jnp.max(jnp.where(visible, scores, neg_large), axis=-1, keepdims=True)
        row_total = jnp.sum(jnp.where(visible, jnp.exp(scores - row_max), 0.0), axis=-1, keepdims=True)
        log_total = row_max + jnp.log(row_total)
        weights = jnp.where(visible, jnp.exp(scores - log_total), 0.0)
        attended = jnp.einsum("qgjk,kgd->qgjd", weights, value_window, precision=lax.Precision.HIGHEST).astype(jnp.bfloat16)
        attended_wide = lax.optimization_barrier(attended).astype(jnp.float32)
        row_delta = jnp.sum(grad_block * attended_wide, axis=-1, keepdims=True)
        weight_grad = jnp.einsum("qgjd,kgd->qgjk", grad_block, value_window)
        score_grad = lax.optimization_barrier((weights * (weight_grad - row_delta)).astype(jnp.bfloat16)).astype(jnp.float32)
        query_grad = (softmax_scale * jnp.einsum("qgjk,kgd->qgjd", score_grad, key_window)).astype(jnp.bfloat16)
        rounded_weights = lax.optimization_barrier(weights.astype(jnp.bfloat16)).astype(jnp.float32)
        key_part = jnp.einsum("qgjk,qgjd->kgjd", score_grad, query_block)
        key_part = jnp.sum(key_part.reshape(window, KV_HEADS, run_count, per_slot, HD), axis=3)
        value_part = jnp.einsum("qgjk,qgjd->kgjd", rounded_weights, grad_block)
        value_part = jnp.sum(value_part.reshape(window, KV_HEADS, run_count, per_slot, HD), axis=3)
        key_total = lax.dynamic_update_slice_in_dim(key_total, lax.dynamic_slice_in_dim(key_total, first, window, 0) + key_part, first, 0)
        value_total = lax.dynamic_update_slice_in_dim(value_total, lax.dynamic_slice_in_dim(value_total, first, window, 0) + value_part, first, 0)
        return (key_total, value_total), (attended, query_grad)

    zero_total = jnp.zeros((SEQ + margin, KV_HEADS, run_count, HD), jnp.float32)
    totals, outputs = lax.scan(visit, (zero_total, zero_total), jnp.arange(block_count, dtype=jnp.int32))
    key_total, value_total = totals
    attended, query_grad = outputs
    key_runs = lax.optimization_barrier((softmax_scale * key_total[margin:]).astype(jnp.bfloat16)).astype(jnp.float32)
    value_runs = lax.optimization_barrier(value_total[margin:].astype(jnp.bfloat16)).astype(jnp.float32)
    key_grad = jnp.sum(key_runs, axis=2).astype(jnp.bfloat16).reshape(NCTX, SLOTS, TOK_DEV, KV_HEADS * HD)
    value_grad = jnp.sum(value_runs, axis=2).astype(jnp.bfloat16).reshape(NCTX, SLOTS, TOK_DEV, KV_HEADS * HD)
    attended = attended.reshape(NCTX, SLOTS, TOK_DEV, HEADS * HD)
    query_grad = query_grad.reshape(NCTX, SLOTS, TOK_DEV, HEADS * HD)
    return attended, query_grad, key_grad, value_grad
```

```python
import jax
import jax.numpy as jnp
from jax import lax
from jax.experimental import pallas as pl
from jax.experimental.pallas import tpu as pltpu
from jax.sharding import PartitionSpec as P

HD = 128
NEG = -1.0e30
KT = 256
LOG2E = 1.4426950408889634
SC2 = HD ** -0.5 * LOG2E
VMEM_MIB = 48
FW = 4
BW = 4


def nt(a, b):
    return lax.dot_general(a, b, (((1,), (1,)), ((), ())), preferred_element_type=jnp.float32)


def nn(a, b):
    return jnp.dot(a, b, preferred_element_type=jnp.float32)


def heads_to_rows(block):
    return jnp.concatenate([block[:, h * HD:(h + 1) * HD] for h in range(4)], axis=0)


def visible(c, half, pos_ref):
    r = lax.broadcasted_iota(jnp.int32, (KT, 1), 0)
    kpos = c * 512 + (r // 64) * 128 + half * 64 + r % 64
    return (kpos <= pos_ref[0, 0:1, :]) & (kpos >= pos_ref[0, 1:2, :])


def walk(bounds_ref, a, step, width):
    lo, mid, hi = bounds_ref[a, 0], bounds_ref[a, 1], bounds_ref[a, 2]
    count = (hi - lo + width) // width
    base = hi + 1 - count * width
    masked = jnp.minimum((mid - base + width - 1) // width, count - 1)

    @pl.loop(0, masked)
    def _(n):
        step(base + n * width, True)

    @pl.loop(masked, count - 1)
    def _(n):
        step(base + n * width, False)

    step(hi + 1 - width, True)


def fwd_kernel(bounds_ref, pos_ref, qd_ref, kv_ref, ot_ref, st_ref, vt, m_ref, l_ref, acc):
    a = pl.program_id(0)
    half = bounds_ref[0, 3]

    @pl.when(a == 0)
    def _():
        @pl.loop(0, vt.shape[0])
        def _(c):
            vt[c] = kv_ref[c, :, HD:].T

    rows = qd_ref[:, 0].reshape(64, 1024)
    q = heads_to_rows(rows[:, :512])
    m_ref[...] = jnp.full_like(m_ref, NEG)
    l_ref[...] = jnp.zeros_like(l_ref)
    acc[...] = jnp.zeros_like(acc)

    def step(c0, masked):
        tiles = [jnp.maximum(c0 + i, 0) if masked else c0 + i for i in range(FW)]
        s = [nt(kv_ref[c, :, :HD], q) * SC2 for c in tiles]
        if masked:
            vis = [visible(c0 + i, half, pos_ref) for i in range(FW)]
            s = [jnp.where(w, x, NEG) for w, x in zip(vis, s)]
        m_old = m_ref[...]
        m_new = m_old
        for x in s:
            m_new = jnp.maximum(m_new, jnp.max(x, axis=0, keepdims=True))
        p = [jnp.exp2(x - m_new) for x in s]
        if masked:
            p = [jnp.where(w, x, 0.0) for w, x in zip(vis, p)]
        alpha = jnp.exp2(m_old - m_new)
        m_ref[...] = m_new
        total = l_ref[...] * alpha
        out = acc[...] * alpha
        for c, x in zip(tiles, p):
            total = total + jnp.sum(x, axis=0, keepdims=True)
            out = out + nn(vt[c], x.astype(jnp.bfloat16))
        l_ref[...] = total
        acc[...] = out

    walk(bounds_ref, a, step, FW)
    dot = heads_to_rows(rows[:, 512:]).astype(jnp.float32).T
    o = acc[...]
    ot_ref[0] = o
    st_ref[0, 0:1, :] = m_ref[...]
    st_ref[0, 1:2, :] = l_ref[...]
    st_ref[0, 2:3, :] = jnp.sum(dot * o, axis=0, keepdims=True)


def bwd_kernel(bounds_ref, pos_ref, st_ref, other_ref, qd_ref, kv_ref, ot_ref, oq_ref, dkv_ref, kt, dq, dk, dv):
    a = pl.program_id(0)
    half = bounds_ref[0, 3]

    @pl.when(a == 0)
    def _():
        dk[...] = jnp.zeros_like(dk)
        dv[...] = jnp.zeros_like(dv)

        @pl.loop(0, kt.shape[0])
        def _(c):
            kt[c] = kv_ref[c, :, :HD].T

    rows = qd_ref[:, 0].reshape(64, 1024)
    q = heads_to_rows(rows[:, :512])
    do = heads_to_rows(rows[:, 512:])
    dq[...] = jnp.zeros_like(dq)
    own_max, other_max = st_ref[0, 0:1, :], other_ref[0, 0:1, :]
    top = jnp.maximum(own_max, other_max)
    own, oth = jnp.exp2(own_max - top), jnp.exp2(other_max - top)
    total = own * st_ref[0, 1:2, :] + oth * other_ref[0, 1:2, :]
    lse2 = top + jnp.log2(total)
    delta = (own * st_ref[0, 2:3, :] + oth * other_ref[0, 2:3, :]) / total

    def step(c0, masked):
        part = None
        for i in range(BW):
            c = jnp.maximum(c0 + i, 0) if masked else c0 + i
            s = nt(kv_ref[c, :, :HD], q) * SC2
            p = jnp.exp2(s - lse2)
            if masked:
                p = jnp.where(visible(c0 + i, half, pos_ref), p, 0.0)
            dp = nt(kv_ref[c, :, HD:], do)
            ds = (p * (dp - delta)).astype(jnp.bfloat16)
            dv[c] += nn(p.astype(jnp.bfloat16), do)
            dk[c] += nn(ds, q)
            x = nn(kt[c], ds)
            part = x if part is None else part + x
        dq[...] += part

    walk(bounds_ref, a, step, BW)
    ob = (ot_ref[0] * (own / total)).T.astype(jnp.bfloat16)
    qb = (dq[...] * HD ** -0.5).T.astype(jnp.bfloat16)
    for h in range(4):
        oq_ref[:, 0, :, h * HD:(h + 1) * HD] = ob[h * 64:(h + 1) * 64].reshape(4, 16, HD)
        oq_ref[:, 0, :, 512 + h * HD:512 + (h + 1) * HD] = qb[h * 64:(h + 1) * 64].reshape(4, 16, HD)

    @pl.when(a == pl.num_programs(0) - 1)
    def _():
        @pl.loop(0, kt.shape[0])
        def _(c):
            dkv_ref[c, :, :HD] = (dk[c] * HD ** -0.5).astype(jnp.bfloat16)
            dkv_ref[c, :, HD:] = dv[c].astype(jnp.bfloat16)


def fwd(bounds, pos, qd, kv):
    nt_ = kv.shape[0]
    const = lambda a, b: (0, 0, 0)
    return pl.pallas_call(
        fwd_kernel,
        grid_spec=pltpu.PrefetchScalarGridSpec(
            num_scalar_prefetch=1, grid=(8,),
            in_specs=[pl.BlockSpec((1, 2, 256), lambda a, b: (a, 0, 0)),
                      pl.BlockSpec((4, 1, 16, 1024), lambda a, b: (0, a, 0, 0)),
                      pl.BlockSpec((nt_, KT, 2 * HD), const)],
            out_specs=[pl.BlockSpec((1, HD, 256), lambda a, b: (a, 0, 0)),
                       pl.BlockSpec((1, 8, 256), lambda a, b: (a, 0, 0))],
            scratch_shapes=[pltpu.VMEM((nt_, HD, KT), jnp.bfloat16), pltpu.VMEM((1, 256), jnp.float32),
                            pltpu.VMEM((1, 256), jnp.float32), pltpu.VMEM((HD, 256), jnp.float32)]),
        out_shape=[jax.ShapeDtypeStruct((8, HD, 256), jnp.float32), jax.ShapeDtypeStruct((8, 8, 256), jnp.float32)],
        compiler_params=pltpu.CompilerParams(vmem_limit_bytes=VMEM_MIB << 20),
        name="fwd",
    )(bounds, pos, qd, kv)


def bwd(bounds, pos, st, other, qd, kv, ot):
    nt_ = kv.shape[0]
    const = lambda a, b: (0, 0, 0)
    return pl.pallas_call(
        bwd_kernel,
        grid_spec=pltpu.PrefetchScalarGridSpec(
            num_scalar_prefetch=1, grid=(8,),
            in_specs=[pl.BlockSpec((1, 2, 256), lambda a, b: (a, 0, 0)),
                      pl.BlockSpec((1, 8, 256), lambda a, b: (a, 0, 0)),
                      pl.BlockSpec((1, 8, 256), lambda a, b: (a, 0, 0)),
                      pl.BlockSpec((4, 1, 16, 1024), lambda a, b: (0, a, 0, 0)),
                      pl.BlockSpec((nt_, KT, 2 * HD), const),
                      pl.BlockSpec((1, HD, 256), lambda a, b: (a, 0, 0))],
            out_specs=[pl.BlockSpec((4, 1, 16, 1024), lambda a, b: (0, a, 0, 0)),
                       pl.BlockSpec((nt_, KT, 2 * HD), const)],
            scratch_shapes=[pltpu.VMEM((nt_, HD, KT), jnp.bfloat16), pltpu.VMEM((HD, 256), jnp.float32),
                            pltpu.VMEM((nt_, KT, HD), jnp.float32), pltpu.VMEM((nt_, KT, HD), jnp.float32)]),
        out_shape=[jax.ShapeDtypeStruct((4, 8, 16, 1024), jnp.bfloat16), jax.ShapeDtypeStruct((nt_, KT, 2 * HD), jnp.bfloat16)],
        compiler_params=pltpu.CompilerParams(vmem_limit_bytes=VMEM_MIB << 20),
        name="bwd",
    )(bounds, pos, st, other, qd, kv, ot)


def plan(lengths, b, ap, half):
    a = jnp.arange(8, dtype=jnp.int32)[:, None, None]
    x = jnp.arange(4, dtype=jnp.int32)[None, :, None]
    t = jnp.arange(16, dtype=jnp.int32)[None, None, :]
    pos = (128 * (16 * a + 4 * b + x) + 16 * ap + t).reshape(8, 64)
    ends = jnp.cumsum(lengths)
    start = jnp.sum(jnp.where(ends[None, None, :] <= pos[:, :, None], lengths, 0), axis=-1)
    hi = 4 * jnp.arange(8, dtype=jnp.int32) + b
    lo = jnp.minimum(start[:, 0] // 512, hi)
    mid = jnp.clip((start[:, -1] + 511) // 512, lo, hi)
    bounds = jnp.stack([lo, mid, hi, jnp.full_like(lo, 1) * half], axis=1)
    rows = jnp.stack([jnp.tile(pos, (1, 4)), jnp.tile(start, (1, 4))], axis=1)
    return bounds.astype(jnp.int32), rows.astype(jnp.int32)


def on_device(query_rows, key_rows, value_rows, out_grad, lengths):
    bf = jnp.bfloat16
    x, ap, b = lax.axis_index("head"), lax.axis_index("inner"), lax.axis_index("outer")
    bounds, pos = plan(lengths, b, ap, x % 2)

    def by_group(rows):
        return rows.reshape(8, 16, 2, 512).transpose(2, 0, 1, 3)

    qd = jnp.concatenate([by_group(query_rows), by_group(out_grad)], axis=-1)
    qd = jnp.broadcast_to(qd[:, None], (2, 2, 8, 16, 1024)).reshape(32, 16, 1024)

    def by_half(rows):
        return rows.reshape(2, 64, 2, HD).transpose(2, 0, 1, 3).reshape(4, 64, HD)

    kv = jnp.concatenate([by_half(key_rows), by_half(value_rows)], axis=-1)
    kv = lax.all_to_all(kv, "head", 0, 0, tiled=True).reshape(KT, 2 * HD)
    kv = lax.all_gather(kv, ("inner", "outer"))
    qd = lax.all_to_all(qd, ("head", "inner"), 0, 0, tiled=True).reshape(4, 8, 16, 1024)
    ot, st = fwd(bounds, pos, qd, kv)
    other = lax.ppermute(st, "head", [(0, 1), (1, 0), (2, 3), (3, 2)])
    oq, dkv = bwd(bounds, pos, st, other, qd, kv, ot)
    dkv = lax.all_to_all(dkv, ("inner", "outer"), 0, 0, tiled=True)
    dkv = jnp.sum(dkv.astype(jnp.float32), axis=0).astype(bf).reshape(4, 64, 2 * HD)
    dkv = lax.all_to_all(dkv, "head", 0, 0, tiled=True).reshape(2, 2, 64, 2, HD)
    dkv = dkv.transpose(3, 1, 2, 0, 4).reshape(2, 1, 1, 128, 2 * HD)
    oq = lax.all_to_all(oq.reshape(32, 16, 1024), ("head", "inner"), 0, 0, tiled=True)
    oq = oq.reshape(2, 2, 128, 2, 512).astype(jnp.float32)
    oq = (oq[:, 0] + oq[:, 1]).astype(bf).transpose(2, 1, 0, 3).reshape(2, 1, 1, 128, 1024)
    return oq[0], oq[1], dkv[0], dkv[1]


def solution(mesh):
    placed = P(("inner", "outer"), "head", None, None)
    return jax.shard_map(
        on_device,
        mesh=mesh,
        in_specs=(placed, placed, placed, placed, P()),
        out_specs=(placed, placed, placed, placed),
        check_vma=False,
    )
```

```python
import jax
import jax.numpy as jnp
from jax import lax
from jax.experimental import pallas as pl
from jax.experimental.pallas import tpu as pltpu
from jax.sharding import Mesh
from jax.sharding import PartitionSpec as P

HD = 128
NEG = -1.0e30
SCALE = HD ** -0.5
SC2 = SCALE * 1.4426950408889634
QT = 16
KP = 16
LIST = 160
bf16, f32, i32 = jnp.bfloat16, jnp.float32, jnp.int32
VMEM = pl.BlockSpec(memory_space=pltpu.VMEM)
SMEM = pl.BlockSpec(memory_space=pltpu.SMEM)


def nt(a, b):
    return lax.dot_general(a, b, (((1,), (1,)), ((), ())), preferred_element_type=f32)


def nn(a, b):
    return jnp.dot(a, b, preferred_element_type=f32)


def head_rows(ref, n, first):
    block = ref[:, n].reshape(64, ref.shape[-1])
    return jnp.concatenate([block[:, first + h * HD:first + (h + 1) * HD] for h in range(4)], axis=0)


def list_steps(plan_ref, plain, edge):
    def outer(d, counts):
        def inner(n, counts):
            a, b = counts
            p = n - d
            plain[a] = n * 256 + p
            edge[b] = n * 256 + p
            is_plain = ((p >= plan_ref[1, n]) & (d > 0)).astype(i32)
            is_live = (p >= plan_ref[0, n]).astype(i32)
            return a + is_plain, b + is_live * (1 - is_plain)

        return lax.fori_loop(d, QT, inner, counts)

    counts = lax.fori_loop(0, QT, outer, (jnp.int32(0), jnp.int32(0)))
    for i in range(8):
        plain[counts[0] + i] = QT * 256
        edge[counts[1] + i] = QT * 256
    return counts


def unpack(steps, t):
    word = steps[t]
    return word // 256, word % 256


def visible(p, n, offset, pos_ref):
    r = lax.broadcasted_iota(i32, (256, 1), 0)
    kpos = p * 1024 + (r // 32) * 128 + offset + r % 32
    return (kpos <= pos_ref[n, 0:1, :]) & (kpos >= pos_ref[n, 1:2, :])


def keys_at(ref, p):
    return ref[pl.ds(pl.multiple_of(p * 256, 256), 256), :]


def lanes_at(ref, p):
    return ref[:, pl.ds(pl.multiple_of(p * 256, 256), 256)]


def sort_keys(core, own_ref, oth_ref, first, put):
    @pl.loop(0, KP)
    def _(m):
        own = own_ref[:, m].reshape(128, 2 * HD)[:, first:first + HD]
        oth = oth_ref[:, m].reshape(128, 2 * HD)[:, first:first + HD]
        put(2 * m + core, own)
        put(2 * m + 1 - core, oth)


def put_rows(ref):
    def put(c, rows):
        ref[pl.ds(pl.multiple_of(c * 128, 128), 128), :] = rows
    return put


def put_lanes(ref):
    def put(c, rows):
        ref[:, pl.ds(pl.multiple_of(c * 128, 128), 128)] = rows.T
    return put


def fwd_kernel(plan_ref, pos_ref, qd_ref, own_ref, oth_ref, ot_ref, st_ref,
               q_s, k_s, vt, m_s, l_s, acc, s_buf, p_buf, a_buf, plain, edge):
    core, offset = plan_ref[2, 0], plan_ref[2, 1]
    counts = list_steps(plan_ref, plain, edge)
    sort_keys(core, own_ref, oth_ref, 0, put_rows(k_s))
    sort_keys(core, own_ref, oth_ref, HD, put_lanes(vt))

    @pl.loop(0, QT)
    def _(n):
        q_s[n] = head_rows(qd_ref, n, 0)
    q_s[QT] = jnp.zeros((256, HD), bf16)
    m_s[...] = jnp.full_like(m_s, NEG)
    l_s[...] = jnp.zeros_like(l_s)
    acc[...] = jnp.zeros_like(acc)

    def run(steps, count, masked):
        def score(t, buf):
            n, p = unpack(steps, t)
            s = nt(keys_at(k_s, p), q_s[n]) * SC2
            if masked:
                s = jnp.where(visible(p, n, offset, pos_ref), s, 2 * NEG)
            s_buf[buf] = s

        def soften(t, buf):
            n, _ = unpack(steps, t)
            s = s_buf[buf]
            old = m_s[n]
            new = jnp.maximum(old, jnp.max(s, axis=0, keepdims=True))
            w = jnp.exp2(s - new)
            alpha = jnp.exp2(old - new)
            m_s[n] = new
            l_s[n] = l_s[n] * alpha + jnp.sum(w, axis=0, keepdims=True)
            a_buf[buf] = alpha
            p_buf[buf] = w.astype(bf16)

        def gather(t, buf):
            n, p = unpack(steps, t)
            acc[n] = acc[n] * a_buf[buf] + nn(lanes_at(vt, p), p_buf[buf])

        p_buf[2] = jnp.zeros((256, 256), bf16)
        p_buf[3] = jnp.zeros((256, 256), bf16)
        a_buf[2] = jnp.ones((1, 256), f32)
        a_buf[3] = jnp.ones((1, 256), f32)
        score(0, 0)
        score(1, 1)
        trips = (count + 3) // 4

        @pl.loop(0, trips)
        def _(i):
            t = 4 * i
            for half in (0, 2):
                cur, nxt = half, 2 - half
                for k in (0, 1):
                    score(t + half + 2 + k, nxt + k)
                for k in (0, 1):
                    gather(jnp.maximum(t + half - 2 + k, 0), nxt + k)
                for k in (0, 1):
                    soften(t + half + k, cur + k)

        last = jnp.maximum(4 * trips - 2, 0)
        gather(last, 2)
        gather(last + 1, 3)

    run(plain, counts[0], False)
    run(edge, counts[1], True)

    @pl.loop(0, QT)
    def _(n):
        o = acc[n]
        ot_ref[n] = o
        st_ref[n, 0:1, :] = m_s[n]
        st_ref[n, 1:2, :] = l_s[n]
        st_ref[n, 2:3, :] = jnp.sum(head_rows(qd_ref, n, 512).astype(f32).T * o, axis=0, keepdims=True)


def bwd_kernel(plan_ref, pos_ref, st0_ref, st1_ref, st2_ref, st3_ref, qd_ref, own_ref, oth_ref, ot_ref,
               oq_ref, down_ref, doth_ref,
               q_s, do_s, k_s, v_s, kt, lse_s, delta_s, w_s, dq, dk, dv, s_buf, dp_buf, p_buf, ds_buf, plain, edge):
    core, offset = plan_ref[2, 0], plan_ref[2, 1]
    counts = list_steps(plan_ref, plain, edge)
    sort_keys(core, own_ref, oth_ref, 0, put_rows(k_s))
    sort_keys(core, own_ref, oth_ref, HD, put_rows(v_s))
    sort_keys(core, own_ref, oth_ref, 0, put_lanes(kt))
    refs = (st0_ref, st1_ref, st2_ref, st3_ref)

    @pl.loop(0, QT)
    def _(n):
        q_s[n] = head_rows(qd_ref, n, 0)
        do_s[n] = head_rows(qd_ref, n, 512)
        top = refs[0][n, 0:1, :]
        for ref in refs[1:]:
            top = jnp.maximum(top, ref[n, 0:1, :])
        share = [jnp.exp2(ref[n, 0:1, :] - top) for ref in refs]
        total = sum(w * ref[n, 1:2, :] for w, ref in zip(share, refs))
        lse_s[n] = top + jnp.log2(total)
        delta_s[n] = sum(w * ref[n, 2:3, :] for w, ref in zip(share, refs)) / total
        w_s[n] = share[0] / total
    q_s[QT] = jnp.zeros((256, HD), bf16)
    do_s[QT] = jnp.zeros((256, HD), bf16)
    lse_s[QT] = jnp.zeros((1, 256), f32)
    delta_s[QT] = jnp.zeros((1, 256), f32)
    dq[...] = jnp.zeros_like(dq)
    dk[...] = jnp.zeros_like(dk)
    dv[...] = jnp.zeros_like(dv)

    def run(steps, count, masked):
        def score(t, buf):
            n, p = unpack(steps, t)
            s = nt(keys_at(k_s, p), q_s[n]) * SC2
            if masked:
                s = jnp.where(visible(p, n, offset, pos_ref), s, NEG)
            s_buf[buf] = s
            dp_buf[buf] = nt(keys_at(v_s, p), do_s[n])

        def soften(t, buf):
            n, _ = unpack(steps, t)
            w = jnp.exp2(s_buf[buf] - lse_s[n])
            p_buf[buf] = w.astype(bf16)
            ds_buf[buf] = (w * (dp_buf[buf] - delta_s[n])).astype(bf16)

        def gather(t, buf):
            n, p = unpack(steps, t)
            rows = pl.ds(pl.multiple_of(p * 256, 256), 256)
            ds = ds_buf[buf]
            dv[rows, :] += nn(p_buf[buf], do_s[n])
            dk[rows, :] += nn(ds, q_s[n])
            dq[n] += nn(lanes_at(kt, p), ds)

        for buf in (2, 3):
            p_buf[buf] = jnp.zeros((256, 256), bf16)
            ds_buf[buf] = jnp.zeros((256, 256), bf16)
        score(0, 0)
        score(1, 1)
        trips = (count + 3) // 4

        @pl.loop(0, trips)
        def _(i):
            t = 4 * i
            for half in (0, 2):
                cur, nxt = half, 2 - half
                for k in (0, 1):
                    score(t + half + 2 + k, nxt + k)
                for k in (0, 1):
                    gather(jnp.maximum(t + half - 2 + k, 0), nxt + k)
                for k in (0, 1):
                    soften(t + half + k, cur + k)

        last = jnp.maximum(4 * trips - 2, 0)
        gather(last, 2)
        gather(last + 1, 3)

    run(plain, counts[0], False)
    run(edge, counts[1], True)

    @pl.loop(0, QT)
    def _(n):
        ob = (ot_ref[n] * w_s[n]).T.astype(bf16)
        qb = (dq[n] * SCALE).T.astype(bf16)
        for h in range(4):
            oq_ref[:, n, :, h * HD:(h + 1) * HD] = ob[h * 64:(h + 1) * 64].reshape(4, 16, HD)
            oq_ref[:, n, :, 512 + h * HD:512 + (h + 1) * HD] = qb[h * 64:(h + 1) * 64].reshape(4, 16, HD)

    @pl.loop(0, KP)
    def _(m):
        for ref, c in ((down_ref, 2 * m + core), (doth_ref, 2 * m + 1 - core)):
            rows = pl.ds(pl.multiple_of(c * 128, 128), 128)
            ref[:, m, :, :HD] = (dk[rows, :] * SCALE).astype(bf16).reshape(4, 32, HD)
            ref[:, m, :, HD:] = dv[rows, :].astype(bf16).reshape(4, 32, HD)


def fwd(plan, pos, qd, own, oth):
    return pl.pallas_call(
        fwd_kernel,
        in_specs=[SMEM, VMEM, VMEM, VMEM, VMEM],
        out_specs=[VMEM, VMEM],
        scratch_shapes=[
            pltpu.VMEM((QT + 1, 256, HD), bf16), pltpu.VMEM((KP * 256, HD), bf16), pltpu.VMEM((HD, KP * 256), bf16),
            pltpu.VMEM((QT + 1, 1, 256), f32), pltpu.VMEM((QT + 1, 1, 256), f32), pltpu.VMEM((QT + 1, HD, 256), f32),
            pltpu.VMEM((4, 256, 256), f32), pltpu.VMEM((4, 256, 256), bf16), pltpu.VMEM((4, 1, 256), f32),
            pltpu.SMEM((LIST,), i32), pltpu.SMEM((LIST,), i32),
        ],
        out_shape=[jax.ShapeDtypeStruct((QT, HD, 256), f32), jax.ShapeDtypeStruct((QT, 4, 256), f32)],
        compiler_params=pltpu.CompilerParams(vmem_limit_bytes=40 << 20),
        name="fwd",
    )(plan, pos, qd, own, oth)


def bwd(plan, pos, sts, qd, own, oth, ot):
    half = jax.ShapeDtypeStruct((4, KP, 32, 2 * HD), bf16)
    return pl.pallas_call(
        bwd_kernel,
        in_specs=[SMEM] + [VMEM] * 9,
        out_specs=[VMEM] * 3,
        scratch_shapes=[
            pltpu.VMEM((QT + 1, 256, HD), bf16), pltpu.VMEM((QT + 1, 256, HD), bf16),
            pltpu.VMEM((KP * 256, HD), bf16), pltpu.VMEM((KP * 256, HD), bf16), pltpu.VMEM((HD, KP * 256), bf16),
            pltpu.VMEM((QT + 1, 1, 256), f32), pltpu.VMEM((QT + 1, 1, 256), f32), pltpu.VMEM((QT + 1, 1, 256), f32),
            pltpu.VMEM((QT + 1, HD, 256), f32), pltpu.VMEM((KP * 256, HD), f32), pltpu.VMEM((KP * 256, HD), f32),
            pltpu.VMEM((4, 256, 256), f32), pltpu.VMEM((4, 256, 256), f32),
            pltpu.VMEM((4, 256, 256), bf16), pltpu.VMEM((4, 256, 256), bf16),
            pltpu.SMEM((LIST,), i32), pltpu.SMEM((LIST,), i32),
        ],
        out_shape=[jax.ShapeDtypeStruct((4, QT, 16, 1024), bf16), half, half],
        compiler_params=pltpu.CompilerParams(vmem_limit_bytes=48 << 20),
        name="bwd",
    )(plan, pos, *sts, qd, own, oth, ot)


def make_plan(lengths, core, u, j):
    n = jnp.arange(QT + 1, dtype=i32)[:, None, None]
    x = jnp.arange(4, dtype=i32)[None, :, None]
    t = jnp.arange(16, dtype=i32)[None, None, :]
    pos = (512 * (2 * n + core) + 128 * x + 16 * u + t).reshape(QT + 1, 64)
    ends = jnp.cumsum(lengths)
    start = jnp.sum(jnp.where(ends[None, None, :] <= pos[:, :, None], lengths, 0), axis=-1)
    low = start[:QT, 0] // 1024
    plain = (start[:QT, -1] + 1023) // 1024
    extra = jnp.zeros((QT,), i32).at[0].set(core).at[1].set(32 * j)
    plan = jnp.stack([low, plain, extra]).astype(i32)
    rows = jnp.stack([jnp.tile(pos, (1, 4)), jnp.tile(start, (1, 4))], axis=1)
    return plan, rows.astype(i32)


PLANE = ("head", "inner", "zl")


def on_device(query_rows, key_rows, value_rows, out_grad, lengths):
    j, u, g, core = (lax.axis_index(name) for name in ("head", "inner", "zl", "core"))
    plan, pos = make_plan(lengths, core, u, j)
    swap = [(0, 1), (1, 0)]

    def send_keys(rows):
        return rows.reshape(4, 32, 2, HD).transpose(0, 2, 1, 3)

    kv = jnp.concatenate([send_keys(key_rows), send_keys(value_rows)], axis=-1)
    kv = jnp.broadcast_to(kv[:, None], (4, 8, 2, 32, 2 * HD)).reshape(64, 32, 2 * HD)
    own = lax.all_to_all(kv, PLANE, 0, 0, tiled=True)
    oth = lax.ppermute(own, "core", swap)

    def send_rows(rows):
        return rows.reshape(8, 16, 2, 512).transpose(0, 2, 1, 3)

    qd = jnp.concatenate([send_rows(query_rows), send_rows(out_grad)], axis=-1)
    qd = jnp.broadcast_to(qd[None], (4, 8, 2, 16, 1024)).reshape(64, 16, 1024)
    qd = lax.all_to_all(qd, PLANE, 0, 0, tiled=True).reshape(4, QT, 16, 1024)
    own, oth = own.reshape(4, KP, 32, 2 * HD), oth.reshape(4, KP, 32, 2 * HD)
    ot, st = fwd(plan, pos, qd, own, oth)
    sts = [st] + [lax.ppermute(st, "head", [(i, (i + k) % 4) for i in range(4)]) for k in (1, 2, 3)]
    oq, down, doth = bwd(plan, pos, sts, qd, own, oth, ot)
    other = lax.ppermute(doth, "core", swap)
    dkv = (down.astype(f32) + other.astype(f32)).astype(bf16).reshape(64, 32, 2 * HD)
    dkv = lax.all_to_all(dkv, PLANE, 0, 0, tiled=True).reshape(4, 8, 2, 32, 2, HD)
    dkv = jnp.sum(dkv.astype(f32), axis=1).astype(bf16)
    dkv = dkv.transpose(3, 0, 2, 1, 4).reshape(2, 1, 1, 128, 2 * HD)
    oq = lax.all_to_all(oq.reshape(64, 16, 1024), PLANE, 0, 0, tiled=True).reshape(4, 8, 2, 16, 2, 512)
    oq = jnp.sum(oq.astype(f32), axis=0).astype(bf16)
    oq = oq.transpose(3, 0, 2, 1, 4).reshape(2, 1, 1, 128, 1024)
    return oq[0], oq[1], dkv[0], dkv[1]


def solution(mesh):
    finer = Mesh(mesh.devices.reshape(4, 8, 2, 2), ("head", "inner", "zl", "core"))
    placed = P(("inner", "zl", "core"), "head", None, None)
    return jax.shard_map(
        on_device,
        mesh=finer,
        in_specs=(placed, placed, placed, placed, P()),
        out_specs=(placed, placed, placed, placed),
        check_vma=False,
    )
```

```python
import jax
import jax.numpy as jnp
from jax import lax
from jax.experimental import pallas as pl
from jax.experimental.pallas import tpu as pltpu
from jax.sharding import Mesh
from jax.sharding import PartitionSpec as P

HD = 128
NEG = -1.0e30
SCALE = HD ** -0.5
SC2 = SCALE * 1.4426950408889634
QT = 16
KP = 16
LIST = 160
WIDE = 1536
bf16, f32, i32 = jnp.bfloat16, jnp.float32, jnp.int32
VMEM = pl.BlockSpec(memory_space=pltpu.VMEM)
SMEM = pl.BlockSpec(memory_space=pltpu.SMEM)


def nt(a, b):
    return lax.dot_general(a, b, (((1,), (1,)), ((), ())), preferred_element_type=f32)


def nn(a, b):
    return jnp.dot(a, b, preferred_element_type=f32)


def row_tile(ref, n, first):
    n = jnp.minimum(n, QT - 1)
    return jnp.concatenate([ref[:, n, :, first + h * HD:first + (h + 1) * HD].reshape(64, HD) for h in range(4)], axis=0)


def key_tile(own_ref, oth_ref, p, first):
    parts = [own_ref[:, p, :, 1024 + 256 * h + first:1024 + 256 * h + first + HD].reshape(64, HD) for h in (0, 1)]
    parts += [oth_ref[:, p, :, 256 * h + first:256 * h + first + HD].reshape(64, HD) for h in (0, 1)]
    return jnp.concatenate(parts, axis=0)


def unpack(steps, kind, t):
    word = steps[kind, t]
    return lax.shift_right_logical(word, 8), word & 255


def mask_scores(s, n, p, pos_ref, kpos_ref, low):
    kpos = kpos_ref[...]
    kpos = jnp.concatenate([kpos, kpos], axis=1)
    first = p * 1024
    seen = (kpos <= pos_ref[n, 0:1, :] - first) & (kpos >= pos_ref[n, 1:2, :] - first)
    return jnp.where(seen, s, low)


def lanes_at(ref, p):
    return ref[:, pl.ds(pl.multiple_of(p * 256, 256), 256)]


def walk(count, score, soften, gather):
    score(0, 0)
    score(1, 1)
    trips = lax.shift_right_logical(count + 3, 2)

    @pl.loop(0, trips)
    def _(i):
        t = 4 * i
        for half in (0, 2):
            cur, nxt = half, 2 - half
            for k in (0, 1):
                score(t + half + 2 + k, nxt + k)
            for k in (0, 1):
                gather(jnp.maximum(t + half - 2 + k, 0), nxt + k)
            for k in (0, 1):
                soften(t + half + k, cur + k)

    last = jnp.maximum(4 * trips - 2, 0)
    gather(last, 2)
    gather(last + 1, 3)


def fwd_kernel(steps, pos_ref, kpos_ref, own_ref, oth_ref, ot_ref, st_ref, vt, m_s, l_s, acc, s_buf, p_buf, a_buf):
    @pl.loop(0, KP, unroll=4)
    def _(p):
        vt[:, pl.ds(pl.multiple_of(p * 256, 256), 256)] = key_tile(own_ref, oth_ref, p, HD).T

    m_s[...] = jnp.full_like(m_s, NEG)
    l_s[...] = jnp.zeros_like(l_s)
    acc[...] = jnp.zeros_like(acc)

    def run(kind):
        def score(t, buf):
            n, p = unpack(steps, kind, t)
            s = nt(key_tile(own_ref, oth_ref, p, 0), row_tile(own_ref, n, 0)) * SC2
            s_buf[buf] = mask_scores(s, n, p, pos_ref, kpos_ref, 2 * NEG) if kind else s

        def soften(t, buf):
            n, _ = unpack(steps, kind, t)
            s = s_buf[buf]
            old = m_s[n]
            new = jnp.maximum(old, jnp.max(s, axis=0, keepdims=True))
            w = jnp.exp2(s - new)
            alpha = jnp.exp2(old - new)
            m_s[n] = new
            l_s[n] = l_s[n] * alpha + jnp.sum(w, axis=0, keepdims=True)
            a_buf[buf] = alpha
            p_buf[buf] = w.astype(bf16)

        def gather(t, buf):
            n, p = unpack(steps, kind, t)
            acc[n] = acc[n] * a_buf[buf] + nn(lanes_at(vt, p), p_buf[buf])

        for buf in (2, 3):
            p_buf[buf] = jnp.zeros((256, 256), bf16)
            a_buf[buf] = jnp.ones((1, 256), f32)
        walk(steps[kind, LIST - 1], score, soften, gather)

    run(0)
    run(1)

    @pl.loop(0, QT, unroll=4)
    def _(n):
        o = acc[n]
        ot_ref[n] = o
        st_ref[n, 0:1, :] = m_s[n]
        st_ref[n, 1:2, :] = l_s[n]
        st_ref[n, 2:3, :] = jnp.sum(row_tile(own_ref, n, 512).T.astype(f32) * o, axis=0, keepdims=True)


def bwd_kernel(steps, pos_ref, kpos_ref, st0_ref, st1_ref, st2_ref, st3_ref, own_ref, oth_ref, ot_ref,
               out_ref, oth_out_ref, kt, lse_s, delta_s, w_s, dq, dk, dv, s_buf, dp_buf, p_buf, ds_buf):
    @pl.loop(0, KP, unroll=4)
    def _(p):
        kt[:, pl.ds(pl.multiple_of(p * 256, 256), 256)] = key_tile(own_ref, oth_ref, p, 0).T

    refs = (st0_ref, st1_ref, st2_ref, st3_ref)

    @pl.loop(0, QT, unroll=4)
    def _(n):
        top = refs[0][n, 0:1, :]
        for ref in refs[1:]:
            top = jnp.maximum(top, ref[n, 0:1, :])
        share = [jnp.exp2(ref[n, 0:1, :] - top) for ref in refs]
        total = sum(w * ref[n, 1:2, :] for w, ref in zip(share, refs))
        lse_s[n] = top + jnp.log2(total)
        delta_s[n] = sum(w * ref[n, 2:3, :] for w, ref in zip(share, refs)) / total
        w_s[n] = share[0] / total
    lse_s[QT] = jnp.full((1, 256), -NEG, f32)
    delta_s[QT] = jnp.zeros((1, 256), f32)
    dq[...] = jnp.zeros_like(dq)
    dk[...] = jnp.zeros_like(dk)
    dv[...] = jnp.zeros_like(dv)

    def run(kind):
        def score(t, buf):
            n, p = unpack(steps, kind, t)
            s = nt(key_tile(own_ref, oth_ref, p, 0), row_tile(own_ref, n, 0)) * SC2
            s_buf[buf] = mask_scores(s, n, p, pos_ref, kpos_ref, NEG) if kind else s
            dp_buf[buf] = nt(key_tile(own_ref, oth_ref, p, HD), row_tile(own_ref, n, 512))

        def soften(t, buf):
            n, _ = unpack(steps, kind, t)
            w = jnp.exp2(s_buf[buf] - lse_s[n])
            p_buf[buf] = w.astype(bf16)
            ds_buf[buf] = (w * (dp_buf[buf] - delta_s[n])).astype(bf16)

        def gather(t, buf):
            n, p = unpack(steps, kind, t)
            ds = ds_buf[buf]
            dv[p] += nn(p_buf[buf], row_tile(own_ref, n, 512))
            dk[p] += nn(ds, row_tile(own_ref, n, 0))
            dq[n] += nn(lanes_at(kt, p), ds)

        for buf in (2, 3):
            p_buf[buf] = jnp.zeros((256, 256), bf16)
            ds_buf[buf] = jnp.zeros((256, 256), bf16)
        walk(steps[kind, LIST - 1], score, soften, gather)

    run(0)
    run(1)

    @pl.loop(0, QT, unroll=4)
    def _(n):
        ob = (ot_ref[n] * w_s[n]).astype(bf16).T
        qb = (dq[n] * SCALE).astype(bf16).T
        for h in range(4):
            out_ref[:, n, :, h * HD:(h + 1) * HD] = ob[h * 64:(h + 1) * 64].reshape(4, 16, HD)
            out_ref[:, n, :, 512 + h * HD:512 + (h + 1) * HD] = qb[h * 64:(h + 1) * 64].reshape(4, 16, HD)

    @pl.loop(0, KP, unroll=4)
    def _(p):
        for first, tile in ((0, (dk[p] * SCALE).astype(bf16)), (HD, dv[p].astype(bf16))):
            for h in (0, 1):
                at = 256 * h + first
                out_ref[:, p, :, 1024 + at:1024 + at + HD] = tile[64 * h:64 * h + 64].reshape(4, 16, HD)
                oth_out_ref[:, p, :, at:at + HD] = tile[128 + 64 * h:192 + 64 * h].reshape(4, 16, HD)


def fwd(steps, pos, kpos, own, oth):
    return pl.pallas_call(
        fwd_kernel,
        in_specs=[SMEM] + [VMEM] * 4,
        out_specs=[VMEM, VMEM],
        scratch_shapes=[
            pltpu.VMEM((HD, KP * 256), bf16),
            pltpu.VMEM((QT + 1, 1, 256), f32), pltpu.VMEM((QT + 1, 1, 256), f32), pltpu.VMEM((QT + 1, HD, 256), f32),
            pltpu.VMEM((4, 256, 256), f32), pltpu.VMEM((4, 256, 256), bf16), pltpu.VMEM((4, 1, 256), f32),
        ],
        out_shape=[jax.ShapeDtypeStruct((QT, HD, 256), f32), jax.ShapeDtypeStruct((QT, 4, 256), f32)],
        compiler_params=pltpu.CompilerParams(vmem_limit_bytes=40 << 20),
        name="fwd",
    )(steps, pos, kpos, own, oth)


def bwd(steps, pos, kpos, sts, own, oth, ot):
    return pl.pallas_call(
        bwd_kernel,
        in_specs=[SMEM] + [VMEM] * 9,
        out_specs=[VMEM] * 2,
        scratch_shapes=[
            pltpu.VMEM((HD, KP * 256), bf16),
            pltpu.VMEM((QT + 1, 1, 256), f32), pltpu.VMEM((QT + 1, 1, 256), f32), pltpu.VMEM((QT + 1, 1, 256), f32),
            pltpu.VMEM((QT + 1, HD, 256), f32), pltpu.VMEM((KP, 256, HD), f32), pltpu.VMEM((KP, 256, HD), f32),
            pltpu.VMEM((4, 256, 256), f32), pltpu.VMEM((4, 256, 256), f32),
            pltpu.VMEM((4, 256, 256), bf16), pltpu.VMEM((4, 256, 256), bf16),
        ],
        out_shape=[jax.ShapeDtypeStruct((4, QT, 16, WIDE), bf16), jax.ShapeDtypeStruct((4, KP, 16, 512), bf16)],
        compiler_params=pltpu.CompilerParams(vmem_limit_bytes=48 << 20),
        name="bwd",
    )(steps, pos, kpos, *sts, own, oth, ot)


def pack_kernel(q_ref, k_ref, v_ref, do_ref, out_ref):
    for j in range(4):
        for u in range(8):
            for g in range(2):
                at = j * 16 + u * 2 + g
                out_ref[at, :, 0:512] = q_ref[16 * u:16 * u + 16, 512 * g:512 * g + 512]
                out_ref[at, :, 512:1024] = do_ref[16 * u:16 * u + 16, 512 * g:512 * g + 512]
                for h in (0, 1):
                    rows = slice(32 * j + 16 * h, 32 * j + 16 * h + 16)
                    out_ref[at, :, 1024 + 256 * h:1152 + 256 * h] = k_ref[rows, HD * g:HD * g + HD]
                    out_ref[at, :, 1152 + 256 * h:1280 + 256 * h] = v_ref[rows, HD * g:HD * g + HD]


def pack(q, k, v, do):
    return pl.pallas_call(
        pack_kernel, in_specs=[VMEM] * 4, out_specs=VMEM,
        out_shape=jax.ShapeDtypeStruct((64, 16, WIDE), bf16),
        compiler_params=pltpu.CompilerParams(vmem_limit_bytes=24 << 20), name="pack",
    )(q, k, v, do)


def add_kernel(own_ref, other_ref, out_ref):
    out_ref[...] = (own_ref[...].astype(f32) + other_ref[...].astype(f32)).astype(bf16)


def add_other(out, other):
    last = pl.BlockSpec((4, KP, 16, 512), lambda i: (0, 0, 0, 2))
    return pl.pallas_call(
        add_kernel, grid=(1,), in_specs=[last, pl.BlockSpec((4, KP, 16, 512), lambda i: (0, 0, 0, 0))], out_specs=last,
        out_shape=jax.ShapeDtypeStruct(out.shape, bf16), input_output_aliases={0: 0},
        compiler_params=pltpu.CompilerParams(vmem_limit_bytes=24 << 20), name="add_cores",
    )(out, other)


def sum_kernel(in_ref, at_ref, qg_ref, kg_ref, vg_ref):
    for u in range(8):
        for g in range(2):
            rows, cols = slice(16 * u, 16 * u + 16), slice(512 * g, 512 * g + 512)
            for first, ref in ((0, at_ref), (512, qg_ref)):
                parts = [in_ref[j * 16 + u * 2 + g, :, first:first + 512].astype(f32) for j in range(4)]
                ref[rows, cols] = (parts[0] + parts[1] + parts[2] + parts[3]).astype(bf16)
    for j in range(4):
        for g in range(2):
            for h in (0, 1):
                rows, cols = slice(32 * j + 16 * h, 32 * j + 16 * h + 16), slice(HD * g, HD * g + HD)
                both = sum(in_ref[j * 16 + u * 2 + g, :, 1024 + 256 * h:1280 + 256 * h].astype(f32) for u in range(8))
                kg_ref[rows, cols] = both[:, :HD].astype(bf16)
                vg_ref[rows, cols] = both[:, HD:].astype(bf16)


def sum_pieces(pieces):
    big, small = jax.ShapeDtypeStruct((128, 1024), bf16), jax.ShapeDtypeStruct((128, 256), bf16)
    return pl.pallas_call(
        sum_kernel, in_specs=[VMEM], out_specs=[VMEM] * 4, out_shape=[big, big, small, small],
        compiler_params=pltpu.CompilerParams(vmem_limit_bytes=24 << 20), name="sum_pieces",
    )(pieces)


def make_plan(lengths, core, u, j):
    n = jnp.arange(QT + 1, dtype=i32)[:, None, None]
    x = jnp.arange(4, dtype=i32)[None, :, None]
    t = jnp.arange(16, dtype=i32)[None, None, :]
    pos = (512 * (2 * n + core) + 128 * x + 16 * u + t).reshape(QT + 1, 64)
    ends = jnp.cumsum(lengths)
    start = jnp.sum(jnp.where(ends[None, None, :] <= pos[:, :, None], lengths, 0), axis=-1)
    rows = jnp.stack([jnp.tile(pos, (1, 4)), jnp.tile(start, (1, 4))], axis=1).astype(i32)
    low = (start[:QT, 0] // 1024)[None, :]
    plain_low = ((start[:QT, -1] + 1023) // 1024)[None, :]
    d = jnp.arange(KP, dtype=i32)[:, None]
    m = jnp.arange(QT, dtype=i32)[None, :]
    live = (m - d >= 0) & (m - d >= low)
    plain = live & (d > 0) & (m - d >= plain_low)
    code = (m * 256 + m - d).reshape(1, QT * KP)
    at = jnp.arange(LIST, dtype=i32)[:, None]

    def compact(mask):
        mask = mask.reshape(1, QT * KP)
        rank = jnp.cumsum(mask.astype(i32), axis=1) - 1
        listed = QT * 256 + jnp.sum(jnp.where(mask & (rank == at), code - QT * 256, 0), axis=1)
        return jnp.where(at[:, 0] == LIST - 1, rank[0, -1] + 1, listed)

    steps = jnp.stack([compact(plain), compact(live & ~plain)]).astype(i32)
    r = jnp.arange(256, dtype=i32)
    parity = jnp.where(r < 128, core, 1 - core)
    kpos = 512 * parity + 128 * (r % 64 // 16) + 32 * j + 16 * (r // 64 % 2) + r % 16
    return steps, rows, jnp.broadcast_to(kpos[:, None], (256, 128)).astype(i32)


PLANE = ("head", "inner", "zl")


def on_device(query_rows, key_rows, value_rows, out_grad, lengths):
    j, u, core = (lax.axis_index(name) for name in ("head", "inner", "core"))
    swap = [(0, 1), (1, 0)]
    steps, pos, kpos = make_plan(lengths, core, u, j)
    pieces = pack(query_rows.reshape(128, 1024), key_rows.reshape(128, 256), value_rows.reshape(128, 256),
                  out_grad.reshape(128, 1024))
    own = lax.all_to_all(pieces, PLANE, 0, 0, tiled=True).reshape(4, QT, 16, WIDE)
    oth = lax.ppermute(own[..., 1024:], "core", swap)
    ot, st = fwd(steps, pos, kpos, own, oth)
    sts = [st] + [lax.ppermute(st, "head", [(i, (i + k) % 4) for i in range(4)]) for k in (1, 2, 3)]
    out, oth_out = bwd(steps, pos, kpos, sts, own, oth, ot)
    out = add_other(out, lax.ppermute(oth_out, "core", swap))
    out = lax.all_to_all(out.reshape(64, 16, WIDE), PLANE, 0, 0, tiled=True)
    attended, query_grad, key_grad, value_grad = sum_pieces(out)
    return (attended.reshape(1, 1, 128, 1024), query_grad.reshape(1, 1, 128, 1024),
            key_grad.reshape(1, 1, 128, 256), value_grad.reshape(1, 1, 128, 256))


def solution(mesh):
    finer = Mesh(mesh.devices.reshape(4, 8, 2, 2), ("head", "inner", "zl", "core"))
    placed = P(("inner", "zl", "core"), "head", None, None)
    return jax.shard_map(
        on_device,
        mesh=finer,
        in_specs=(placed, placed, placed, placed, P()),
        out_specs=(placed, placed, placed, placed),
        check_vma=False,
    )
```

```python
import jax
import jax.numpy as jnp
from jax import lax
from jax.experimental import pallas as pl
from jax.experimental.pallas import tpu as pltpu
from jax.sharding import Mesh
from jax.sharding import PartitionSpec as P

HD = 128
NEG = -1.0e30
SCALE = HD ** -0.5
SC2 = SCALE * 1.4426950408889634
QT = 16
KP = 16
LIST = 160
WIDE = 1536
bf16, f32, i32 = jnp.bfloat16, jnp.float32, jnp.int32
VMEM = pl.BlockSpec(memory_space=pltpu.VMEM)
SMEM = pl.BlockSpec(memory_space=pltpu.SMEM)


def nt(a, b):
    return lax.dot_general(a, b, (((1,), (1,)), ((), ())), preferred_element_type=f32)


def nn(a, b):
    return jnp.dot(a, b, preferred_element_type=f32)


def row_tile(ref, n, first):
    n = jnp.minimum(n, QT - 1)
    return jnp.concatenate([ref[:, n, :, first + h * HD:first + (h + 1) * HD].reshape(64, HD) for h in range(4)], axis=0)


def key_tile(own_ref, oth_ref, p, first):
    parts = [own_ref[:, p, :, 1024 + 256 * h + first:1024 + 256 * h + first + HD].reshape(64, HD) for h in (0, 1)]
    parts += [oth_ref[:, p, :, 256 * h + first:256 * h + first + HD].reshape(64, HD) for h in (0, 1)]
    return jnp.concatenate(parts, axis=0)


def unpack(steps, kind, t):
    word = steps[kind, t]
    return lax.shift_right_logical(word, 8), word & 255


def mask_scores(s, n, p, pos_ref, kpos_ref, low):
    kpos = kpos_ref[...]
    kpos = jnp.concatenate([kpos, kpos], axis=1)
    first = p * 1024
    seen = (kpos <= pos_ref[n, 0:1, :] - first) & (kpos >= pos_ref[n, 1:2, :] - first)
    return jnp.where(seen, s, low)


def lanes_at(ref, p):
    return ref[:, pl.ds(pl.multiple_of(p * 256, 256), 256)]


def walk(count, score, soften, gather):
    score(0, 0)
    score(1, 1)
    trips = lax.shift_right_logical(count + 3, 2)

    @pl.loop(0, trips)
    def _(i):
        t = 4 * i
        for half in (0, 2):
            cur, nxt = half, 2 - half
            for k in (0, 1):
                score(t + half + 2 + k, nxt + k)
                soften(t + half + k, cur + k)
                gather(jnp.maximum(t + half - 2 + k, 0), nxt + k)

    last = jnp.maximum(4 * trips - 2, 0)
    gather(last, 2)
    gather(last + 1, 3)


def fwd_kernel(steps, pos_ref, kpos_ref, own_ref, oth_ref, ot_ref, st_ref, vt, m_s, l_s, acc, s_buf, p_buf, a_buf):
    @pl.loop(0, KP, unroll=4)
    def _(p):
        vt[:, pl.ds(pl.multiple_of(p * 256, 256), 256)] = key_tile(own_ref, oth_ref, p, HD).T

    m_s[...] = jnp.full_like(m_s, NEG)
    l_s[...] = jnp.zeros_like(l_s)
    acc[...] = jnp.zeros_like(acc)

    def run(kind):
        def score(t, buf):
            n, p = unpack(steps, kind, t)
            s = nt(key_tile(own_ref, oth_ref, p, 0), row_tile(own_ref, n, 0)) * SC2
            s_buf[buf] = mask_scores(s, n, p, pos_ref, kpos_ref, 2 * NEG) if kind else s

        def soften(t, buf):
            n, _ = unpack(steps, kind, t)
            s = s_buf[buf]
            old = m_s[n]
            new = jnp.maximum(old, jnp.max(s, axis=0, keepdims=True))
            w = jnp.exp2(s - new)
            alpha = jnp.exp2(old - new)
            m_s[n] = new
            l_s[n] = l_s[n] * alpha + jnp.sum(w, axis=0, keepdims=True)
            a_buf[buf] = alpha
            p_buf[buf] = w.astype(bf16)

        def gather(t, buf):
            n, p = unpack(steps, kind, t)
            acc[n] = acc[n] * a_buf[buf] + nn(lanes_at(vt, p), p_buf[buf])

        for buf in (2, 3):
            p_buf[buf] = jnp.zeros((256, 256), bf16)
            a_buf[buf] = jnp.ones((1, 256), f32)
        walk(steps[kind, LIST - 1], score, soften, gather)

    run(0)
    run(1)

    @pl.loop(0, QT, unroll=4)
    def _(n):
        o = acc[n]
        ot_ref[n] = o
        st_ref[n, 0:1, :] = m_s[n]
        st_ref[n, 1:2, :] = l_s[n]
        st_ref[n, 2:3, :] = jnp.sum(row_tile(own_ref, n, 512).T.astype(f32) * o, axis=0, keepdims=True)


def bwd_kernel(steps, pos_ref, kpos_ref, st0_ref, st1_ref, st2_ref, st3_ref, own_ref, oth_ref, ot_ref,
               out_ref, oth_out_ref, kt, lse_s, delta_s, w_s, dq, dk, dv, s_buf, dp_buf, p_buf, ds_buf):
    @pl.loop(0, KP, unroll=4)
    def _(p):
        kt[:, pl.ds(pl.multiple_of(p * 256, 256), 256)] = key_tile(own_ref, oth_ref, p, 0).T

    refs = (st0_ref, st1_ref, st2_ref, st3_ref)

    @pl.loop(0, QT, unroll=4)
    def _(n):
        top = refs[0][n, 0:1, :]
        for ref in refs[1:]:
            top = jnp.maximum(top, ref[n, 0:1, :])
        share = [jnp.exp2(ref[n, 0:1, :] - top) for ref in refs]
        total = sum(w * ref[n, 1:2, :] for w, ref in zip(share, refs))
        lse_s[n] = top + jnp.log2(total)
        delta_s[n] = sum(w * ref[n, 2:3, :] for w, ref in zip(share, refs)) / total
        w_s[n] = share[0] / total
    lse_s[QT] = jnp.full((1, 256), -NEG, f32)
    delta_s[QT] = jnp.zeros((1, 256), f32)
    dq[...] = jnp.zeros_like(dq)
    dk[...] = jnp.zeros_like(dk)
    dv[...] = jnp.zeros_like(dv)

    def run(kind):
        def score(t, buf):
            n, p = unpack(steps, kind, t)
            s = nt(key_tile(own_ref, oth_ref, p, 0), row_tile(own_ref, n, 0)) * SC2
            s_buf[buf] = mask_scores(s, n, p, pos_ref, kpos_ref, NEG) if kind else s
            dp_buf[buf] = nt(key_tile(own_ref, oth_ref, p, HD), row_tile(own_ref, n, 512))

        def soften(t, buf):
            n, _ = unpack(steps, kind, t)
            w = jnp.exp2(s_buf[buf] - lse_s[n])
            p_buf[buf] = w.astype(bf16)
            ds_buf[buf] = (w * (dp_buf[buf] - delta_s[n])).astype(bf16)

        def gather(t, buf):
            n, p = unpack(steps, kind, t)
            ds = ds_buf[buf]
            dv[p] += nn(p_buf[buf], row_tile(own_ref, n, 512))
            dk[p] += nn(ds, row_tile(own_ref, n, 0))
            dq[n] += nn(lanes_at(kt, p), ds)

        for buf in (2, 3):
            p_buf[buf] = jnp.zeros((256, 256), bf16)
            ds_buf[buf] = jnp.zeros((256, 256), bf16)
        walk(steps[kind, LIST - 1], score, soften, gather)

    run(0)
    run(1)

    @pl.loop(0, QT, unroll=4)
    def _(n):
        ob = (ot_ref[n] * w_s[n]).astype(bf16).T
        qb = (dq[n] * SCALE).astype(bf16).T
        for h in range(4):
            out_ref[:, n, :, h * HD:(h + 1) * HD] = ob[h * 64:(h + 1) * 64].reshape(4, 16, HD)
            out_ref[:, n, :, 512 + h * HD:512 + (h + 1) * HD] = qb[h * 64:(h + 1) * 64].reshape(4, 16, HD)

    @pl.loop(0, KP, unroll=4)
    def _(p):
        for first, tile in ((0, (dk[p] * SCALE).astype(bf16)), (HD, dv[p].astype(bf16))):
            for h in (0, 1):
                at = 256 * h + first
                out_ref[:, p, :, 1024 + at:1024 + at + HD] = tile[64 * h:64 * h + 64].reshape(4, 16, HD)
                oth_out_ref[:, p, :, at:at + HD] = tile[128 + 64 * h:192 + 64 * h].reshape(4, 16, HD)


def fwd(steps, pos, kpos, own, oth):
    return pl.pallas_call(
        fwd_kernel,
        in_specs=[SMEM] + [VMEM] * 4,
        out_specs=[VMEM, VMEM],
        scratch_shapes=[
            pltpu.VMEM((HD, KP * 256), bf16),
            pltpu.VMEM((QT + 1, 1, 256), f32), pltpu.VMEM((QT + 1, 1, 256), f32), pltpu.VMEM((QT + 1, HD, 256), f32),
            pltpu.VMEM((4, 256, 256), f32), pltpu.VMEM((4, 256, 256), bf16), pltpu.VMEM((4, 1, 256), f32),
        ],
        out_shape=[jax.ShapeDtypeStruct((QT, HD, 256), f32), jax.ShapeDtypeStruct((QT, 4, 256), f32)],
        compiler_params=pltpu.CompilerParams(vmem_limit_bytes=16 << 20),
        name="fwd",
    )(steps, pos, kpos, own, oth)


def bwd(steps, pos, kpos, sts, own, oth, ot):
    return pl.pallas_call(
        bwd_kernel,
        in_specs=[SMEM] + [VMEM] * 9,
        out_specs=[VMEM] * 2,
        scratch_shapes=[
            pltpu.VMEM((HD, KP * 256), bf16),
            pltpu.VMEM((QT + 1, 1, 256), f32), pltpu.VMEM((QT + 1, 1, 256), f32), pltpu.VMEM((QT + 1, 1, 256), f32),
            pltpu.VMEM((QT + 1, HD, 256), f32), pltpu.VMEM((KP, 256, HD), f32), pltpu.VMEM((KP, 256, HD), f32),
            pltpu.VMEM((4, 256, 256), f32), pltpu.VMEM((4, 256, 256), f32),
            pltpu.VMEM((4, 256, 256), bf16), pltpu.VMEM((4, 256, 256), bf16),
        ],
        out_shape=[jax.ShapeDtypeStruct((4, QT, 16, WIDE), bf16), jax.ShapeDtypeStruct((4, KP, 16, 512), bf16)],
        compiler_params=pltpu.CompilerParams(vmem_limit_bytes=24 << 20),
        name="bwd",
    )(steps, pos, kpos, *sts, own, oth, ot)


def pack_kernel(q_ref, k_ref, v_ref, do_ref, out_ref):
    for j in range(4):
        for u in range(8):
            for g in range(2):
                at = j * 16 + u * 2 + g
                out_ref[at, :, 0:512] = q_ref[16 * u:16 * u + 16, 512 * g:512 * g + 512]
                out_ref[at, :, 512:1024] = do_ref[16 * u:16 * u + 16, 512 * g:512 * g + 512]
                for h in (0, 1):
                    rows = slice(32 * j + 16 * h, 32 * j + 16 * h + 16)
                    out_ref[at, :, 1024 + 256 * h:1152 + 256 * h] = k_ref[rows, HD * g:HD * g + HD]
                    out_ref[at, :, 1152 + 256 * h:1280 + 256 * h] = v_ref[rows, HD * g:HD * g + HD]


def pack(q, k, v, do):
    return pl.pallas_call(
        pack_kernel, in_specs=[VMEM] * 4, out_specs=VMEM,
        out_shape=jax.ShapeDtypeStruct((64, 16, WIDE), bf16),
        compiler_params=pltpu.CompilerParams(vmem_limit_bytes=12 << 20), name="pack",
    )(q, k, v, do)


def add_kernel(own_ref, other_ref, out_ref):
    out_ref[...] = (own_ref[...].astype(f32) + other_ref[...].astype(f32)).astype(bf16)


def add_other(out, other):
    last = pl.BlockSpec((4, KP, 16, 512), lambda i: (0, 0, 0, 2))
    return pl.pallas_call(
        add_kernel, grid=(1,), in_specs=[last, pl.BlockSpec((4, KP, 16, 512), lambda i: (0, 0, 0, 0))], out_specs=last,
        out_shape=jax.ShapeDtypeStruct(out.shape, bf16), input_output_aliases={0: 0},
        compiler_params=pltpu.CompilerParams(vmem_limit_bytes=12 << 20), name="add_cores",
    )(out, other)


def sum_kernel(in_ref, at_ref, qg_ref, kg_ref, vg_ref):
    for u in range(8):
        for g in range(2):
            rows, cols = slice(16 * u, 16 * u + 16), slice(512 * g, 512 * g + 512)
            for first, ref in ((0, at_ref), (512, qg_ref)):
                parts = [in_ref[j * 16 + u * 2 + g, :, first:first + 512].astype(f32) for j in range(4)]
                ref[rows, cols] = (parts[0] + parts[1] + parts[2] + parts[3]).astype(bf16)
    for j in range(4):
        for g in range(2):
            for h in (0, 1):
                rows, cols = slice(32 * j + 16 * h, 32 * j + 16 * h + 16), slice(HD * g, HD * g + HD)
                both = sum(in_ref[j * 16 + u * 2 + g, :, 1024 + 256 * h:1280 + 256 * h].astype(f32) for u in range(8))
                kg_ref[rows, cols] = both[:, :HD].astype(bf16)
                vg_ref[rows, cols] = both[:, HD:].astype(bf16)


def sum_pieces(pieces):
    big, small = jax.ShapeDtypeStruct((128, 1024), bf16), jax.ShapeDtypeStruct((128, 256), bf16)
    return pl.pallas_call(
        sum_kernel, in_specs=[VMEM], out_specs=[VMEM] * 4, out_shape=[big, big, small, small],
        compiler_params=pltpu.CompilerParams(vmem_limit_bytes=12 << 20), name="sum_pieces",
    )(pieces)


def make_plan(lengths, core, u, j):
    n = jnp.arange(QT + 1, dtype=i32)[:, None, None]
    x = jnp.arange(4, dtype=i32)[None, :, None]
    t = jnp.arange(16, dtype=i32)[None, None, :]
    pos = (512 * (2 * n + core) + 128 * x + 16 * u + t).reshape(QT + 1, 64)
    docs = jnp.arange(lengths.shape[0])
    ends = jnp.sum(jnp.where(docs[:, None] <= docs[None, :], lengths[:, None], 0), axis=0)
    start = jnp.sum(jnp.where(ends[None, None, :] <= pos[:, :, None], lengths, 0), axis=-1)
    rows = jnp.stack([jnp.tile(pos, (1, 4)), jnp.tile(start, (1, 4))], axis=1).astype(i32)
    low = (start[:QT, 0] // 1024)[None, :]
    plain_low = ((start[:QT, -1] + 1023) // 1024)[None, :]
    d = jnp.arange(KP, dtype=i32)[:, None]
    m = jnp.arange(QT, dtype=i32)[None, :]
    live = (m - d >= 0) & (m - d >= low)
    plain = live & (d > 0) & (m - d >= plain_low)
    code = (m * 256 + m - d).reshape(1, QT * KP)
    order = jnp.arange(QT * KP, dtype=i32)
    earlier = order[:, None] < order[None, :]
    at = jnp.arange(LIST, dtype=i32)[:, None]

    def compact(mask):
        mask = mask.reshape(1, QT * KP)
        rank = jnp.sum((earlier & mask.reshape(QT * KP, 1)).astype(i32), axis=0, keepdims=True)
        listed = QT * 256 + jnp.sum(jnp.where(mask & (rank == at), code - QT * 256, 0), axis=1)
        return jnp.where(at[:, 0] == LIST - 1, jnp.sum(mask.astype(i32)), listed)

    steps = jnp.stack([compact(plain), compact(live & ~plain)]).astype(i32)
    r = jnp.arange(256, dtype=i32)
    parity = jnp.where(r < 128, core, 1 - core)
    kpos = 512 * parity + 128 * (r % 64 // 16) + 32 * j + 16 * (r // 64 % 2) + r % 16
    return steps, rows, jnp.broadcast_to(kpos[:, None], (256, 128)).astype(i32)


PLANE = ("head", "inner", "zl")


def on_device(query_rows, key_rows, value_rows, out_grad, lengths):
    j, u, core = (lax.axis_index(name) for name in ("head", "inner", "core"))
    swap = [(0, 1), (1, 0)]
    steps, pos, kpos = make_plan(lengths, core, u, j)
    pieces = pack(query_rows.reshape(128, 1024), key_rows.reshape(128, 256), value_rows.reshape(128, 256),
                  out_grad.reshape(128, 1024))
    own = lax.all_to_all(pieces, PLANE, 0, 0, tiled=True).reshape(4, QT, 16, WIDE)
    oth = lax.ppermute(own[..., 1024:], "core", swap)
    ot, st = fwd(steps, pos, kpos, own, oth)
    sts = [st] + [lax.ppermute(st, "head", [(i, (i + k) % 4) for i in range(4)]) for k in (1, 2, 3)]
    out, oth_out = bwd(steps, pos, kpos, sts, own, oth, ot)
    out = add_other(out, lax.ppermute(oth_out, "core", swap))
    out = lax.all_to_all(out.reshape(64, 16, WIDE), PLANE, 0, 0, tiled=True)
    attended, query_grad, key_grad, value_grad = sum_pieces(out)
    return (attended.reshape(1, 1, 128, 1024), query_grad.reshape(1, 1, 128, 1024),
            key_grad.reshape(1, 1, 128, 256), value_grad.reshape(1, 1, 128, 256))


def solution(mesh):
    finer = Mesh(mesh.devices.reshape(4, 8, 2, 2), ("head", "inner", "zl", "core"))
    placed = P(("inner", "zl", "core"), "head", None, None)
    return jax.shard_map(
        on_device,
        mesh=finer,
        in_specs=(placed, placed, placed, placed, P()),
        out_specs=(placed, placed, placed, placed),
        check_vma=False,
    )
```

```python
import jax
import jax.numpy as jnp
from jax import lax
from jax.experimental import pallas as pl
from jax.experimental.pallas import tpu as pltpu
from jax.sharding import Mesh
from jax.sharding import PartitionSpec as P

HD = 128
NEG = -1.0e30
SCALE = HD ** -0.5
SC2 = SCALE * 1.4426950408889634
QT = 16
KP = 16
LIST = 160
WIDE = 1024
bf16, f32, i32 = jnp.bfloat16, jnp.float32, jnp.int32
VMEM = pl.BlockSpec(memory_space=pltpu.VMEM)
SMEM = pl.BlockSpec(memory_space=pltpu.SMEM)


def nt(a, b):
    return lax.dot_general(a, b, (((1,), (1,)), ((), ())), preferred_element_type=f32)


def nn(a, b):
    return jnp.dot(a, b, preferred_element_type=f32)


def row_tile(ref, n, first):
    n = jnp.minimum(n, QT - 1)
    return jnp.concatenate([ref[:, n, :, first + h * HD:first + (h + 1) * HD].reshape(64, HD) for h in range(4)], axis=0)


def key_tile(own_ref, oth_ref, p, first):
    parts = [own_ref[:, p, :, 512 + 256 * h + first:512 + 256 * h + first + HD].reshape(64, HD) for h in (0, 1)]
    parts += [oth_ref[:, p, :, 256 * h + first:256 * h + first + HD].reshape(64, HD) for h in (0, 1)]
    return jnp.concatenate(parts, axis=0)


def unpack(steps, kind, t):
    word = steps[kind, t]
    return lax.shift_right_logical(word, 8), word & 255


def mask_scores(s, n, p, pos_ref, kpos_ref, low):
    kpos = kpos_ref[...]
    kpos = jnp.concatenate([kpos, kpos], axis=1)
    first = p * 1024
    seen = (kpos <= pos_ref[n, 0:1, :] - first) & (kpos >= pos_ref[n, 1:2, :] - first)
    return jnp.where(seen, s, low)


def lanes_at(ref, p):
    return ref[:, pl.ds(pl.multiple_of(p * 256, 256), 256)]


def walk(count, score, soften, gather):
    score(0, 0)
    score(1, 1)
    trips = lax.shift_right_logical(count + 3, 2)

    @pl.loop(0, trips)
    def _(i):
        t = 4 * i
        for half in (0, 2):
            cur, nxt = half, 2 - half
            for k in (0, 1):
                score(t + half + 2 + k, nxt + k)
                soften(t + half + k, cur + k)
                gather(jnp.maximum(t + half - 2 + k, 0), nxt + k)

    last = jnp.maximum(4 * trips - 2, 0)
    gather(last, 2)
    gather(last + 1, 3)


def fwd_kernel(steps, pos_ref, kpos_ref, own_ref, oth_ref, ot_ref, st_ref, vt, m_s, l_s, acc, s_buf, p_buf, a_buf):
    @pl.loop(0, KP, unroll=4)
    def _(p):
        vt[:, pl.ds(pl.multiple_of(p * 256, 256), 256)] = key_tile(own_ref, oth_ref, p, HD).T

    m_s[...] = jnp.full_like(m_s, NEG)
    l_s[...] = jnp.zeros_like(l_s)
    acc[...] = jnp.zeros_like(acc)

    def run(kind):
        def score(t, buf):
            n, p = unpack(steps, kind, t)
            s = nt(key_tile(own_ref, oth_ref, p, 0), row_tile(own_ref, n, 0)) * SC2
            s_buf[buf] = mask_scores(s, n, p, pos_ref, kpos_ref, 2 * NEG) if kind else s

        def soften(t, buf):
            n, _ = unpack(steps, kind, t)
            s = s_buf[buf]
            old = m_s[n]
            new = jnp.maximum(old, jnp.max(s, axis=0, keepdims=True))
            w = jnp.exp2(s - new)
            alpha = jnp.exp2(old - new)
            m_s[n] = new
            l_s[n] = l_s[n] * alpha + jnp.sum(w, axis=0, keepdims=True)
            a_buf[buf] = alpha
            p_buf[buf] = w.astype(bf16)

        def gather(t, buf):
            n, p = unpack(steps, kind, t)
            acc[n] = acc[n] * a_buf[buf] + nn(lanes_at(vt, p), p_buf[buf])

        for buf in (2, 3):
            p_buf[buf] = jnp.zeros((256, 256), bf16)
            a_buf[buf] = jnp.ones((1, 256), f32)
        walk(steps[kind, LIST - 1], score, soften, gather)

    run(0)
    run(1)

    @pl.loop(0, QT, unroll=4)
    def _(n):
        o = acc[n]
        ot_ref[n] = o
        st_ref[n, 0:1, :] = m_s[n]
        st_ref[n, 1:2, :] = l_s[n]


def delta_kernel(st_ref, ot_ref, do_ref, out_ref):
    @pl.loop(0, QT, unroll=4)
    def _(n):
        out_ref[n, 0:2, :] = st_ref[n, 0:2, :]
        out_ref[n, 2:3, :] = jnp.sum(row_tile(do_ref, n, 0).T.astype(f32) * ot_ref[n], axis=0, keepdims=True)


def scale_kernel(st0_ref, st1_ref, st2_ref, st3_ref, ot_ref, stat_ref, out_ref):
    refs = (st0_ref, st1_ref, st2_ref, st3_ref)

    @pl.loop(0, QT, unroll=4)
    def _(n):
        top = refs[0][n, 0:1, :]
        for ref in refs[1:]:
            top = jnp.maximum(top, ref[n, 0:1, :])
        share = [jnp.exp2(ref[n, 0:1, :] - top) for ref in refs]
        total = sum(w * ref[n, 1:2, :] for w, ref in zip(share, refs))
        stat_ref[n, 0:1, :] = top + jnp.log2(total)
        stat_ref[n, 1:2, :] = sum(w * ref[n, 2:3, :] for w, ref in zip(share, refs)) / total
        ob = (ot_ref[n] * (share[0] / total)).astype(bf16).T
        for h in range(4):
            out_ref[:, n, :, h * HD:(h + 1) * HD] = ob[h * 64:(h + 1) * 64].reshape(4, 16, HD)
    stat_ref[QT, 0:1, :] = jnp.full((1, 256), -NEG, f32)
    stat_ref[QT, 1:2, :] = jnp.zeros((1, 256), f32)


def bwd_kernel(steps, pos_ref, kpos_ref, stat_ref, own_ref, oth_ref, do_ref, out_ref, oth_out_ref,
               kt, dq, dk, dv, s_buf, dp_buf, p_buf, ds_buf):
    @pl.loop(0, KP, unroll=4)
    def _(p):
        kt[:, pl.ds(pl.multiple_of(p * 256, 256), 256)] = key_tile(own_ref, oth_ref, p, 0).T

    dq[...] = jnp.zeros_like(dq)
    dk[...] = jnp.zeros_like(dk)
    dv[...] = jnp.zeros_like(dv)

    def run(kind):
        def score(t, buf):
            n, p = unpack(steps, kind, t)
            s = nt(key_tile(own_ref, oth_ref, p, 0), row_tile(own_ref, n, 0)) * SC2
            s_buf[buf] = mask_scores(s, n, p, pos_ref, kpos_ref, NEG) if kind else s
            dp_buf[buf] = nt(key_tile(own_ref, oth_ref, p, HD), row_tile(do_ref, n, 0))

        def soften(t, buf):
            n, _ = unpack(steps, kind, t)
            w = jnp.exp2(s_buf[buf] - stat_ref[n, 0:1, :])
            p_buf[buf] = w.astype(bf16)
            ds_buf[buf] = (w * (dp_buf[buf] - stat_ref[n, 1:2, :])).astype(bf16)

        def gather(t, buf):
            n, p = unpack(steps, kind, t)
            ds = ds_buf[buf]
            dv[p] += nn(p_buf[buf], row_tile(do_ref, n, 0))
            dk[p] += nn(ds, row_tile(own_ref, n, 0))
            dq[n] += nn(lanes_at(kt, p), ds)

        for buf in (2, 3):
            p_buf[buf] = jnp.zeros((256, 256), bf16)
            ds_buf[buf] = jnp.zeros((256, 256), bf16)
        walk(steps[kind, LIST - 1], score, soften, gather)

    run(0)
    run(1)

    @pl.loop(0, QT, unroll=4)
    def _(n):
        qb = (dq[n] * SCALE).astype(bf16).T
        for h in range(4):
            out_ref[:, n, :, h * HD:(h + 1) * HD] = qb[h * 64:(h + 1) * 64].reshape(4, 16, HD)

    @pl.loop(0, KP, unroll=4)
    def _(p):
        for first, tile in ((0, (dk[p] * SCALE).astype(bf16)), (HD, dv[p].astype(bf16))):
            for h in (0, 1):
                at = 256 * h + first
                out_ref[:, p, :, 512 + at:512 + at + HD] = tile[64 * h:64 * h + 64].reshape(4, 16, HD)
                oth_out_ref[:, p, :, at:at + HD] = tile[128 + 64 * h:192 + 64 * h].reshape(4, 16, HD)


def fwd(steps, pos, kpos, own, oth):
    return pl.pallas_call(
        fwd_kernel,
        in_specs=[SMEM] + [VMEM] * 4,
        out_specs=[VMEM, VMEM],
        scratch_shapes=[
            pltpu.VMEM((HD, KP * 256), bf16),
            pltpu.VMEM((QT + 1, 1, 256), f32), pltpu.VMEM((QT + 1, 1, 256), f32), pltpu.VMEM((QT + 1, HD, 256), f32),
            pltpu.VMEM((4, 256, 256), f32), pltpu.VMEM((4, 256, 256), bf16), pltpu.VMEM((4, 1, 256), f32),
        ],
        out_shape=[jax.ShapeDtypeStruct((QT, HD, 256), f32), jax.ShapeDtypeStruct((QT, 4, 256), f32)],
        compiler_params=pltpu.CompilerParams(vmem_limit_bytes=16 << 20),
        cost_estimate=pl.CostEstimate(flops=15 * 10 ** 9, bytes_accessed=8 << 20, transcendentals=0),
        name="fwd",
    )(steps, pos, kpos, own, oth)


def delta(st, ot, do):
    return pl.pallas_call(
        delta_kernel, in_specs=[VMEM] * 3, out_specs=VMEM, out_shape=jax.ShapeDtypeStruct((QT, 4, 256), f32),
        compiler_params=pltpu.CompilerParams(vmem_limit_bytes=12 << 20), name="delta",
    )(st, ot, do)


def scale(sts, ot):
    return pl.pallas_call(
        scale_kernel, in_specs=[VMEM] * 5, out_specs=[VMEM] * 2,
        out_shape=[jax.ShapeDtypeStruct((QT + 1, 2, 256), f32), jax.ShapeDtypeStruct((4, QT, 16, 512), bf16)],
        compiler_params=pltpu.CompilerParams(vmem_limit_bytes=12 << 20), name="scale",
    )(*sts, ot)


def bwd(steps, pos, kpos, stat, own, oth, do):
    return pl.pallas_call(
        bwd_kernel,
        in_specs=[SMEM] + [VMEM] * 6,
        out_specs=[VMEM] * 2,
        scratch_shapes=[
            pltpu.VMEM((HD, KP * 256), bf16),
            pltpu.VMEM((QT + 1, HD, 256), f32), pltpu.VMEM((KP, 256, HD), f32), pltpu.VMEM((KP, 256, HD), f32),
            pltpu.VMEM((4, 256, 256), f32), pltpu.VMEM((4, 256, 256), f32),
            pltpu.VMEM((4, 256, 256), bf16), pltpu.VMEM((4, 256, 256), bf16),
        ],
        out_shape=[jax.ShapeDtypeStruct((4, QT, 16, WIDE), bf16), jax.ShapeDtypeStruct((4, KP, 16, 512), bf16)],
        compiler_params=pltpu.CompilerParams(vmem_limit_bytes=24 << 20),
        cost_estimate=pl.CostEstimate(flops=25 * 10 ** 9, bytes_accessed=8 << 20, transcendentals=0),
        name="bwd",
    )(steps, pos, kpos, stat, own, oth, do)


def pack_kernel(q_hbm, k_hbm, v_hbm, out_hbm, q_ref, k_ref, v_ref, out_ref, in_sem, out_sem):
    loads = [pltpu.make_async_copy(src, dst, in_sem.at[i])
             for i, (src, dst) in enumerate(((q_hbm, q_ref), (k_hbm, k_ref), (v_hbm, v_ref)))]
    for load in loads:
        load.start()
    for load in loads:
        load.wait()
    stores = []
    for j in range(4):
        for u in range(8):
            for g in range(2):
                at = u * 2 + g
                out_ref[j, at, :, 0:512] = q_ref[16 * u:16 * u + 16, 512 * g:512 * g + 512]
                for h in (0, 1):
                    rows = slice(32 * j + 16 * h, 32 * j + 16 * h + 16)
                    out_ref[j, at, :, 512 + 256 * h:640 + 256 * h] = k_ref[rows, HD * g:HD * g + HD]
                    out_ref[j, at, :, 640 + 256 * h:768 + 256 * h] = v_ref[rows, HD * g:HD * g + HD]
        stores.append(pltpu.make_async_copy(out_ref.at[j], out_hbm.at[j], out_sem.at[j]))
        stores[-1].start()
    for store in stores:
        store.wait()


def pack(q, k, v):
    any_spec = pl.BlockSpec(memory_space=pltpu.HBM)
    return pl.pallas_call(
        pack_kernel, in_specs=[any_spec] * 3, out_specs=any_spec,
        out_shape=jax.ShapeDtypeStruct((4, 16, 16, WIDE), bf16),
        scratch_shapes=[pltpu.VMEM((128, 1024), bf16), pltpu.VMEM((128, 256), bf16), pltpu.VMEM((128, 256), bf16),
                        pltpu.VMEM((4, 16, 16, WIDE), bf16), pltpu.SemaphoreType.DMA((3,)), pltpu.SemaphoreType.DMA((4,))],
        compiler_params=pltpu.CompilerParams(vmem_limit_bytes=60 << 20), name="pack",
    )(q, k, v)


def spread_kernel(do_ref, out_ref):
    for j in range(4):
        for u in range(8):
            for g in range(2):
                out_ref[j * 16 + u * 2 + g] = do_ref[16 * u:16 * u + 16, 512 * g:512 * g + 512]


def spread(do):
    return pl.pallas_call(
        spread_kernel, in_specs=[VMEM], out_specs=VMEM, out_shape=jax.ShapeDtypeStruct((64, 16, 512), bf16),
        compiler_params=pltpu.CompilerParams(vmem_limit_bytes=12 << 20), name="spread",
    )(do)


def pass_kernel(*refs):
    del refs


def pass_after(x, earlier):
    any_spec = pl.BlockSpec(memory_space=pl.ANY)
    return pl.pallas_call(
        pass_kernel, in_specs=[any_spec] * 2, out_specs=any_spec, out_shape=jax.ShapeDtypeStruct(x.shape, x.dtype),
        input_output_aliases={0: 0}, name="pass_after",
    )(x, earlier)


def add_kernel(own_ref, other_ref, out_ref):
    out_ref[...] = (own_ref[...].astype(f32) + other_ref[...].astype(f32)).astype(bf16)


def add_other(out, other):
    last = pl.BlockSpec((4, KP, 16, 512), lambda i: (0, 0, 0, 1))
    return pl.pallas_call(
        add_kernel, grid=(1,), in_specs=[last, pl.BlockSpec((4, KP, 16, 512), lambda i: (0, 0, 0, 0))], out_specs=last,
        out_shape=jax.ShapeDtypeStruct(out.shape, bf16), input_output_aliases={0: 0},
        compiler_params=pltpu.CompilerParams(vmem_limit_bytes=12 << 20), name="add_cores",
    )(out, other)


def sum_rows(in_ref, out_ref):
    for u in range(8):
        for g in range(2):
            parts = [in_ref[j * 16 + u * 2 + g, :, 0:512].astype(f32) for j in range(4)]
            out_ref[16 * u:16 * u + 16, 512 * g:512 * g + 512] = (parts[0] + parts[1] + parts[2] + parts[3]).astype(bf16)


def sum_attended(pieces):
    return pl.pallas_call(
        sum_rows, in_specs=[VMEM], out_specs=VMEM, out_shape=jax.ShapeDtypeStruct((128, 1024), bf16),
        compiler_params=pltpu.CompilerParams(vmem_limit_bytes=12 << 20), name="sum_attended",
    )(pieces)


def sum_kernel(in_ref, qg_ref, kg_ref, vg_ref):
    sum_rows(in_ref, qg_ref)
    for j in range(4):
        for g in range(2):
            for h in (0, 1):
                rows, cols = slice(32 * j + 16 * h, 32 * j + 16 * h + 16), slice(HD * g, HD * g + HD)
                both = sum(in_ref[j * 16 + u * 2 + g, :, 512 + 256 * h:768 + 256 * h].astype(f32) for u in range(8))
                kg_ref[rows, cols] = both[:, :HD].astype(bf16)
                vg_ref[rows, cols] = both[:, HD:].astype(bf16)


def sum_grads(pieces):
    big, small = jax.ShapeDtypeStruct((128, 1024), bf16), jax.ShapeDtypeStruct((128, 256), bf16)
    return pl.pallas_call(
        sum_kernel, in_specs=[VMEM], out_specs=[VMEM] * 3, out_shape=[big, small, small],
        compiler_params=pltpu.CompilerParams(vmem_limit_bytes=12 << 20), name="sum_grads",
    )(pieces)


def make_plan(lengths, core, u, j):
    n = jnp.arange(QT + 1, dtype=i32)[:, None, None]
    x = jnp.arange(4, dtype=i32)[None, :, None]
    t = jnp.arange(16, dtype=i32)[None, None, :]
    pos = (512 * (2 * n + core) + 128 * x + 16 * u + t).reshape(QT + 1, 64)
    docs = jnp.arange(lengths.shape[0])
    ends = jnp.sum(jnp.where(docs[:, None] <= docs[None, :], lengths[:, None], 0), axis=0)
    start = jnp.sum(jnp.where(ends[None, None, :] <= pos[:, :, None], lengths, 0), axis=-1)
    rows = jnp.stack([jnp.tile(pos, (1, 4)), jnp.tile(start, (1, 4))], axis=1).astype(i32)
    low = (start[:QT, 0] // 1024)[None, :]
    plain_low = ((start[:QT, -1] + 1023) // 1024)[None, :]
    d = jnp.arange(KP, dtype=i32)[:, None]
    m = jnp.arange(QT, dtype=i32)[None, :]
    live = (m - d >= 0) & (m - d >= low)
    plain = live & (d > 0) & (m - d >= plain_low)
    code = (m * 256 + m - d).reshape(1, QT * KP)
    order = jnp.arange(QT * KP, dtype=i32)
    earlier = order[:, None] < order[None, :]
    at = jnp.arange(LIST, dtype=i32)[:, None]

    def compact(mask):
        mask = mask.reshape(1, QT * KP)
        rank = jnp.sum((earlier & mask.reshape(QT * KP, 1)).astype(i32), axis=0, keepdims=True)
        listed = QT * 256 + jnp.sum(jnp.where(mask & (rank == at), code - QT * 256, 0), axis=1)
        return jnp.where(at[:, 0] == LIST - 1, jnp.sum(mask.astype(i32)), listed)

    steps = jnp.stack([compact(plain), compact(live & ~plain)]).astype(i32)
    r = jnp.arange(256, dtype=i32)
    parity = jnp.where(r < 128, core, 1 - core)
    kpos = 512 * parity + 128 * (r % 64 // 16) + 32 * j + 16 * (r // 64 % 2) + r % 16
    return steps, rows, jnp.broadcast_to(kpos[:, None], (256, 128)).astype(i32)


PLANE = ("head", "inner", "zl")


def on_device(query_rows, key_rows, value_rows, out_grad, lengths):
    j, u, core = (lax.axis_index(name) for name in ("head", "inner", "core"))
    swap = [(0, 1), (1, 0)]
    steps, pos, kpos = make_plan(lengths, core, u, j)
    pieces = pack(query_rows.reshape(128, 1024), key_rows.reshape(128, 256), value_rows.reshape(128, 256))
    own = lax.all_to_all(pieces.reshape(64, 16, WIDE), PLANE, 0, 0, tiled=True)
    own = own.reshape(4, QT, 16, WIDE)
    do = lax.all_to_all(spread(out_grad.reshape(128, 1024)), PLANE, 0, 0, tiled=True).reshape(4, QT, 16, 512)
    oth = lax.ppermute(own[..., 512:], "core", swap)
    ot, st = fwd(steps, pos, kpos, own, oth)
    st = delta(st, ot, do)
    sts = [st] + [lax.ppermute(st, "head", [(i, (i + k) % 4) for i in range(4)]) for k in (1, 2, 3)]
    stat, scaled = scale(sts, ot)
    scaled = lax.all_to_all(scaled.reshape(64, 16, 512), PLANE, 0, 0, tiled=True)
    out, oth_out = bwd(steps, pos, kpos, stat, own, oth, do)
    out = add_other(out, lax.ppermute(pass_after(oth_out, scaled), "core", swap))
    out = lax.all_to_all(out.reshape(64, 16, WIDE), PLANE, 0, 0, tiled=True)
    attended = sum_attended(scaled)
    query_grad, key_grad, value_grad = sum_grads(out)
    return (attended.reshape(1, 1, 128, 1024), query_grad.reshape(1, 1, 128, 1024),
            key_grad.reshape(1, 1, 128, 256), value_grad.reshape(1, 1, 128, 256))


def solution(mesh):
    finer = Mesh(mesh.devices.reshape(4, 8, 2, 2), ("head", "inner", "zl", "core"))
    placed = P(("inner", "zl", "core"), "head", None, None)
    return jax.shard_map(
        on_device,
        mesh=finer,
        in_specs=(placed, placed, placed, placed, P()),
        out_specs=(placed, placed, placed, placed),
        check_vma=False,
    )
```

```python
import jax
import jax.numpy as jnp
from jax import lax
from jax.experimental import pallas as pl
from jax.experimental.pallas import tpu as pltpu
from jax.sharding import Mesh
from jax.sharding import PartitionSpec as P

HD = 128
NEG = -1.0e30
SCALE = HD ** -0.5
SC2 = SCALE * 1.4426950408889634
QT = 16
KP = 16
LIST = 160
WIDE = 1152
bf16, f32, i32 = jnp.bfloat16, jnp.float32, jnp.int32
VMEM = pl.BlockSpec(memory_space=pltpu.VMEM)
SMEM = pl.BlockSpec(memory_space=pltpu.SMEM)


def nt(a, b):
    return lax.dot_general(a, b, (((1,), (1,)), ((), ())), preferred_element_type=f32)


def nn(a, b):
    return jnp.dot(a, b, preferred_element_type=f32)


def row_tile(ref, n, first):
    n = jnp.minimum(n, QT - 1)
    return jnp.concatenate([ref[:, n, :, first + h * HD:first + (h + 1) * HD].reshape(64, HD) for h in range(4)], axis=0)


def head_tile(refs, n):
    n = jnp.minimum(n, QT - 1)
    return jnp.concatenate([ref[:, n].reshape(64, HD) for ref in refs], axis=0)


def key_tile(own_ref, oth_ref, p, first):
    parts = [own_ref[:, p, :, 512 + 256 * h + first:512 + 256 * h + first + HD].reshape(64, HD) for h in (0, 1)]
    parts += [oth_ref[:, p, :, 256 * h + first:256 * h + first + HD].reshape(64, HD) for h in (0, 1)]
    return jnp.concatenate(parts, axis=0)


def unpack(steps, kind, t):
    word = steps[kind, t]
    return lax.shift_right_logical(word, 8), word & 255


def mask_scores(s, n, p, pos_ref, kpos_ref, low):
    kpos = kpos_ref[...]
    kpos = jnp.concatenate([kpos, kpos], axis=1)
    first = p * 1024
    seen = (kpos <= pos_ref[n, 0:1, :] - first) & (kpos >= pos_ref[n, 1:2, :] - first)
    return jnp.where(seen, s, low)


def lanes_at(ref, p):
    return ref[:, pl.ds(pl.multiple_of(p * 256, 256), 256)]


def walk(count, score, soften, gather):
    score(0, 0)
    score(1, 1)
    trips = lax.shift_right_logical(count + 3, 2)

    @pl.loop(0, trips)
    def _(i):
        t = 4 * i
        for half in (0, 2):
            cur, nxt = half, 2 - half
            for k in (0, 1):
                score(t + half + 2 + k, nxt + k)
                soften(t + half + k, cur + k)
                gather(jnp.maximum(t + half - 2 + k, 0), nxt + k)

    last = jnp.maximum(4 * trips - 2, 0)
    gather(last, 2)
    gather(last + 1, 3)


def fwd_kernel(steps, pos_ref, kpos_ref, own_ref, oth_ref, ot_ref, st_ref, vt, m_s, l_s, acc, s_buf, p_buf, a_buf):
    @pl.loop(0, KP, unroll=4)
    def _(p):
        vt[:, pl.ds(pl.multiple_of(p * 256, 256), 256)] = key_tile(own_ref, oth_ref, p, HD).T

    m_s[...] = jnp.full_like(m_s, NEG)
    l_s[...] = jnp.zeros_like(l_s)
    acc[...] = jnp.zeros_like(acc)

    def run(kind):
        def score(t, buf):
            n, p = unpack(steps, kind, t)
            s = nt(key_tile(own_ref, oth_ref, p, 0), row_tile(own_ref, n, 0)) * SC2
            s_buf[buf] = mask_scores(s, n, p, pos_ref, kpos_ref, 2 * NEG) if kind else s

        def soften(t, buf):
            n, _ = unpack(steps, kind, t)
            s = s_buf[buf]
            old = m_s[n]
            new = jnp.maximum(old, jnp.max(s, axis=0, keepdims=True))
            w = jnp.exp2(s - new)
            alpha = jnp.exp2(old - new)
            m_s[n] = new
            l_s[n] = l_s[n] * alpha + jnp.sum(w, axis=0, keepdims=True)
            a_buf[buf] = alpha
            p_buf[buf] = w.astype(bf16)

        def gather(t, buf):
            n, p = unpack(steps, kind, t)
            acc[n] = acc[n] * a_buf[buf] + nn(lanes_at(vt, p), p_buf[buf])

        for buf in (2, 3):
            p_buf[buf] = jnp.zeros((256, 256), bf16)
            a_buf[buf] = jnp.ones((1, 256), f32)
        walk(steps[kind, LIST - 1], score, soften, gather)

    run(0)
    run(1)

    @pl.loop(0, QT, unroll=4)
    def _(n):
        o = acc[n]
        ot_ref[n] = o
        st_ref[n, 0:1, :] = m_s[n]
        st_ref[n, 1:2, :] = l_s[n]


def delta_kernel(st_ref, ot_ref, do0_ref, do1_ref, do2_ref, do3_ref, out_ref):
    refs = (do0_ref, do1_ref, do2_ref, do3_ref)

    @pl.loop(0, QT, unroll=4)
    def _(n):
        total = st_ref[n, 1:2, :]
        some = total > 0.0
        dots = jnp.sum(head_tile(refs, n).T.astype(f32) * ot_ref[n], axis=0, keepdims=True)
        out_ref[n, 0:1, :] = jnp.where(some, st_ref[n, 0:1, :] + jnp.log2(total), NEG)
        out_ref[n, 1:2, :] = jnp.where(some, dots / jnp.where(some, total, 1.0), 0.0)


def scale_kernel(st0_ref, st1_ref, st2_ref, st3_ref, st_ref, ot_ref, stat_ref, *out_refs):
    refs = (st0_ref, st1_ref, st2_ref, st3_ref)

    @pl.loop(0, QT, unroll=4)
    def _(n):
        parts = [refs[0][n]] + [pltpu.roll(refs[k][n], 64 * k, 1) for k in (1, 2, 3)]
        top = jnp.maximum(jnp.maximum(parts[0][0:1], parts[1][0:1]), jnp.maximum(parts[2][0:1], parts[3][0:1]))
        share = [jnp.exp2(part[0:1] - top) for part in parts]
        total = share[0] + share[1] + share[2] + share[3]
        lse = top + jnp.log2(total)
        stat_ref[n, 0:1, :] = lse
        stat_ref[n, 1:2, :] = sum(w * part[1:2] for w, part in zip(share, parts)) / total
        ob = (ot_ref[n] * jnp.exp2(st_ref[n, 0:1, :] - lse)).astype(bf16).T
        for h in range(4):
            out_refs[h][:, n] = ob[h * 64:(h + 1) * 64].reshape(4, 16, HD)
    stat_ref[QT, 0:1, :] = jnp.full((1, 256), -NEG, f32)
    stat_ref[QT, 1:2, :] = jnp.zeros((1, 256), f32)


def bwd_kernel(steps, pos_ref, kpos_ref, stat_ref, own_ref, oth_ref, do0_ref, do1_ref, do2_ref, do3_ref, out_ref,
               oth_out_ref, kt, dq, dk, dv, s_buf, dp_buf, p_buf, ds_buf):
    do_refs = (do0_ref, do1_ref, do2_ref, do3_ref)

    @pl.loop(0, KP, unroll=4)
    def _(p):
        kt[:, pl.ds(pl.multiple_of(p * 256, 256), 256)] = key_tile(own_ref, oth_ref, p, 0).T

    dq[...] = jnp.zeros_like(dq)
    dk[...] = jnp.zeros_like(dk)
    dv[...] = jnp.zeros_like(dv)

    def run(kind):
        def score(t, buf):
            n, p = unpack(steps, kind, t)
            s = nt(key_tile(own_ref, oth_ref, p, 0), row_tile(own_ref, n, 0)) * SC2
            s_buf[buf] = mask_scores(s, n, p, pos_ref, kpos_ref, NEG) if kind else s
            dp_buf[buf] = nt(key_tile(own_ref, oth_ref, p, HD), head_tile(do_refs, n))

        def soften(t, buf):
            n, _ = unpack(steps, kind, t)
            w = jnp.exp2(s_buf[buf] - stat_ref[n, 0:1, :])
            p_buf[buf] = w.astype(bf16)
            ds_buf[buf] = (w * (dp_buf[buf] - stat_ref[n, 1:2, :])).astype(bf16)

        def gather(t, buf):
            n, p = unpack(steps, kind, t)
            ds = ds_buf[buf]
            dv[p] += nn(p_buf[buf], head_tile(do_refs, n))
            dk[p] += nn(ds, row_tile(own_ref, n, 0))
            dq[n] += nn(lanes_at(kt, p), ds)

        for buf in (2, 3):
            p_buf[buf] = jnp.zeros((256, 256), bf16)
            ds_buf[buf] = jnp.zeros((256, 256), bf16)
        walk(steps[kind, LIST - 1], score, soften, gather)

    run(0)
    run(1)

    @pl.loop(0, QT, unroll=4)
    def _(n):
        qb = (dq[n] * SCALE).astype(bf16).T
        for h in range(4):
            out_ref[:, n, :, 640 + h * HD:768 + h * HD] = qb[h * 64:(h + 1) * 64].reshape(4, 16, HD)

    @pl.loop(0, KP, unroll=4)
    def _(p):
        for first, tile in ((0, (dk[p] * SCALE).astype(bf16)), (HD, dv[p].astype(bf16))):
            for h in (0, 1):
                at = 256 * h + first
                out_ref[:, p, :, at:at + HD] = tile[64 * h:64 * h + 64].reshape(4, 16, HD)
                oth_out_ref[:, p, :, at:at + HD] = tile[128 + 64 * h:192 + 64 * h].reshape(4, 16, HD)


def fwd(steps, pos, kpos, own, oth):
    return pl.pallas_call(
        fwd_kernel,
        in_specs=[SMEM] + [VMEM] * 4,
        out_specs=[VMEM, VMEM],
        scratch_shapes=[
            pltpu.VMEM((HD, KP * 256), bf16),
            pltpu.VMEM((QT + 1, 1, 256), f32), pltpu.VMEM((QT + 1, 1, 256), f32), pltpu.VMEM((QT + 1, HD, 256), f32),
            pltpu.VMEM((4, 256, 256), f32), pltpu.VMEM((4, 256, 256), bf16), pltpu.VMEM((4, 1, 256), f32),
        ],
        out_shape=[jax.ShapeDtypeStruct((QT, HD, 256), f32), jax.ShapeDtypeStruct((QT, 4, 256), f32)],
        compiler_params=pltpu.CompilerParams(vmem_limit_bytes=16 << 20),
        cost_estimate=pl.CostEstimate(flops=15 * 10 ** 9, bytes_accessed=8 << 20, transcendentals=0),
        name="fwd",
    )(steps, pos, kpos, own, oth)


def delta(st, ot, dos):
    return pl.pallas_call(
        delta_kernel, in_specs=[VMEM] * 6, out_specs=VMEM, out_shape=jax.ShapeDtypeStruct((QT, 2, 256), f32),
        compiler_params=pltpu.CompilerParams(vmem_limit_bytes=12 << 20), name="delta",
    )(st, ot, *dos)


def scale(sts, st, ot):
    return pl.pallas_call(
        scale_kernel, in_specs=[VMEM] * 6, out_specs=[VMEM] * 5,
        out_shape=[jax.ShapeDtypeStruct((QT + 1, 2, 256), f32)] + [jax.ShapeDtypeStruct((4, QT, 16, HD), bf16)] * 4,
        compiler_params=pltpu.CompilerParams(vmem_limit_bytes=12 << 20), name="scale",
    )(*sts, st, ot)


def bwd(steps, pos, kpos, stat, own, oth, dos):
    return pl.pallas_call(
        bwd_kernel,
        in_specs=[SMEM] + [VMEM] * 9,
        out_specs=[VMEM] * 2,
        scratch_shapes=[
            pltpu.VMEM((HD, KP * 256), bf16),
            pltpu.VMEM((QT + 1, HD, 256), f32), pltpu.VMEM((KP, 256, HD), f32), pltpu.VMEM((KP, 256, HD), f32),
            pltpu.VMEM((4, 256, 256), f32), pltpu.VMEM((4, 256, 256), f32),
            pltpu.VMEM((4, 256, 256), bf16), pltpu.VMEM((4, 256, 256), bf16),
        ],
        out_shape=[jax.ShapeDtypeStruct((4, QT, 16, WIDE), bf16), jax.ShapeDtypeStruct((4, KP, 16, 512), bf16)],
        compiler_params=pltpu.CompilerParams(vmem_limit_bytes=24 << 20),
        cost_estimate=pl.CostEstimate(flops=25 * 10 ** 9, bytes_accessed=8 << 20, transcendentals=0),
        name="bwd",
    )(steps, pos, kpos, stat, own, oth, *dos)


def pack_kernel(q_hbm, k_hbm, v_hbm, do_hbm, out_hbm, q_ref, k_ref, v_ref, do_ref, out_ref, in_sem, out_sem):
    loads = [pltpu.make_async_copy(src, dst, in_sem.at[i])
             for i, (src, dst) in enumerate(((q_hbm, q_ref), (k_hbm, k_ref), (v_hbm, v_ref), (do_hbm, do_ref)))]
    for load in loads:
        load.start()
    for load in loads:
        load.wait()
    stores = []
    for j in range(4):
        for u in range(8):
            for g in range(2):
                at = u * 2 + g
                tokens = slice(16 * u, 16 * u + 16)
                for r in range(4):
                    head = 512 * g + HD * ((j - r) % 4)
                    out_ref[j, at, :, r * HD:r * HD + HD] = q_ref[tokens, head:head + HD]
                head = 512 * g + HD * j
                out_ref[j, at, :, 1024:1152] = do_ref[tokens, head:head + HD]
                for h in (0, 1):
                    rows = slice(32 * j + 16 * h, 32 * j + 16 * h + 16)
                    out_ref[j, at, :, 512 + 256 * h:640 + 256 * h] = k_ref[rows, HD * g:HD * g + HD]
                    out_ref[j, at, :, 640 + 256 * h:768 + 256 * h] = v_ref[rows, HD * g:HD * g + HD]
        stores.append(pltpu.make_async_copy(out_ref.at[j], out_hbm.at[j], out_sem.at[j]))
        stores[-1].start()
    for store in stores:
        store.wait()


def pack(q, k, v, do):
    any_spec = pl.BlockSpec(memory_space=pltpu.HBM)
    return pl.pallas_call(
        pack_kernel, in_specs=[any_spec] * 4, out_specs=any_spec,
        out_shape=jax.ShapeDtypeStruct((4, 16, 16, WIDE), bf16),
        scratch_shapes=[pltpu.VMEM((128, 1024), bf16), pltpu.VMEM((128, 256), bf16), pltpu.VMEM((128, 256), bf16),
                        pltpu.VMEM((128, 1024), bf16), pltpu.VMEM((4, 16, 16, WIDE), bf16), pltpu.SemaphoreType.DMA((4,)), pltpu.SemaphoreType.DMA((4,))],
        compiler_params=pltpu.CompilerParams(vmem_limit_bytes=60 << 20), name="pack",
    )(q, k, v, do)


def pass_kernel(*refs):
    del refs


def pass_after(x, earlier):
    any_spec = pl.BlockSpec(memory_space=pl.ANY)
    return pl.pallas_call(
        pass_kernel, in_specs=[any_spec] * (1 + len(earlier)), out_specs=any_spec,
        out_shape=jax.ShapeDtypeStruct(x.shape, x.dtype), input_output_aliases={0: 0}, name="pass_after",
    )(x, *earlier)


def add_kernel(own_ref, other_ref, o0_ref, o1_ref, o2_ref, o3_ref, out_ref):
    out_ref[..., :512] = (own_ref[..., :512].astype(f32) + other_ref[...].astype(f32)).astype(bf16)
    total = o0_ref[...].astype(f32) + o1_ref[...].astype(f32) + o2_ref[...].astype(f32) + o3_ref[...].astype(f32)
    out_ref[..., 512:] = total.astype(bf16)


def add_parts(out, other, heads):
    block = lambda columns: pl.BlockSpec((1, KP, 16, columns), lambda i: (i, 0, 0, 0))
    return pl.pallas_call(
        add_kernel, grid=(4,), in_specs=[block(640), block(512)] + [block(HD)] * 4, out_specs=block(640),
        out_shape=jax.ShapeDtypeStruct(out.shape, bf16), input_output_aliases={0: 0},
        compiler_params=pltpu.CompilerParams(vmem_limit_bytes=12 << 20), name="add_parts",
    )(out, other, *heads)


def sum_kernel(in_ref, at_ref, qg_ref, kg_ref, vg_ref):
    for u in range(8):
        for g in range(2):
            rows = slice(16 * u, 16 * u + 16)
            for h in range(4):
                cols = slice(512 * g + HD * h, 512 * g + HD * h + HD)
                at_ref[rows, cols] = in_ref[h * 16 + u * 2 + g, :, 512:640]
                first = [640 + HD * ((j - h) % 4) for j in range(4)]
                parts = [in_ref[j * 16 + u * 2 + g, :, first[j]:first[j] + HD].astype(f32) for j in range(4)]
                qg_ref[rows, cols] = (parts[0] + parts[1] + parts[2] + parts[3]).astype(bf16)
    for j in range(4):
        for g in range(2):
            for h in (0, 1):
                rows, cols = slice(32 * j + 16 * h, 32 * j + 16 * h + 16), slice(HD * g, HD * g + HD)
                both = sum(in_ref[j * 16 + u * 2 + g, :, 256 * h:256 * h + 256].astype(f32) for u in range(8))
                kg_ref[rows, cols] = both[:, :HD].astype(bf16)
                vg_ref[rows, cols] = both[:, HD:].astype(bf16)


def sum_pieces(pieces):
    big, small = jax.ShapeDtypeStruct((128, 1024), bf16), jax.ShapeDtypeStruct((128, 256), bf16)
    return pl.pallas_call(
        sum_kernel, in_specs=[VMEM], out_specs=[VMEM] * 4, out_shape=[big, big, small, small],
        compiler_params=pltpu.CompilerParams(vmem_limit_bytes=12 << 20), name="sum_pieces",
    )(pieces)


def make_plan(lengths, core, u, j):
    n = jnp.arange(QT + 1, dtype=i32)[:, None, None]
    x = jnp.arange(4, dtype=i32)[None, :, None]
    t = jnp.arange(16, dtype=i32)[None, None, :]
    pos = (512 * (2 * n + core) + 128 * x + 16 * u + t).reshape(QT + 1, 64)
    docs = jnp.arange(lengths.shape[0])
    ends = jnp.sum(jnp.where(docs[:, None] <= docs[None, :], lengths[:, None], 0), axis=0)
    start = jnp.sum(jnp.where(ends[None, None, :] <= pos[:, :, None], lengths, 0), axis=-1)
    rows = jnp.stack([jnp.tile(pos, (1, 4)), jnp.tile(start, (1, 4))], axis=1).astype(i32)
    low = (start[:QT, 0] // 1024)[None, :]
    plain_low = ((start[:QT, -1] + 1023) // 1024)[None, :]
    d = jnp.arange(KP, dtype=i32)[:, None]
    m = jnp.arange(QT, dtype=i32)[None, :]
    live = (m - d >= 0) & (m - d >= low)
    plain = live & (d > 0) & (m - d >= plain_low)
    code = (m * 256 + m - d).reshape(1, QT * KP)
    order = jnp.arange(QT * KP, dtype=i32)
    earlier = order[:, None] < order[None, :]
    at = jnp.arange(LIST, dtype=i32)[:, None]

    def compact(mask):
        mask = mask.reshape(1, QT * KP)
        rank = jnp.sum((earlier & mask.reshape(QT * KP, 1)).astype(i32), axis=0, keepdims=True)
        listed = QT * 256 + jnp.sum(jnp.where(mask & (rank == at), code - QT * 256, 0), axis=1)
        return jnp.where(at[:, 0] == LIST - 1, jnp.sum(mask.astype(i32)), listed)

    steps = jnp.stack([compact(plain), compact(live & ~plain)]).astype(i32)
    r = jnp.arange(256, dtype=i32)
    parity = jnp.where(r < 128, core, 1 - core)
    kpos = 512 * parity + 128 * (r % 64 // 16) + 32 * j + 16 * (r // 64 % 2) + r % 16
    return steps, rows, jnp.broadcast_to(kpos[:, None], (256, 128)).astype(i32)


PLANE = ("head", "inner", "zl")


def on_device(query_rows, key_rows, value_rows, out_grad, lengths):
    j, u, core = (lax.axis_index(name) for name in ("head", "inner", "core"))
    swap = [(0, 1), (1, 0)]
    steps, pos, kpos = make_plan(lengths, core, u, j)
    pieces = pack(query_rows.reshape(128, 1024), key_rows.reshape(128, 256), value_rows.reshape(128, 256),
                  out_grad.reshape(128, 1024))
    own = lax.all_to_all(pieces.reshape(64, 16, WIDE), PLANE, 0, 0, tiled=True).reshape(4, QT, 16, WIDE)
    oth = lax.ppermute(own[..., 512:1024], "core", swap)

    def along(x, k):
        return lax.ppermute(x, "head", [(i, (i + k) % 4) for i in range(4)])

    do = own[..., 1024:]
    dos = [do] + [along(do, k) for k in (1, 2, 3)]
    ot, st = fwd(steps, pos, kpos, own, oth)
    part = delta(st, ot, dos)
    stat, *heads = scale([part] + [along(part, k) for k in (1, 2, 3)], st, ot)
    heads = heads[:1] + [along(heads[k], -k) for k in (1, 2, 3)]
    out, oth_out = bwd(steps, pos, kpos, stat, own, oth, dos)
    oth_out = pass_after(oth_out, heads[1:])
    out = add_parts(out, lax.ppermute(oth_out, "core", swap), heads)
    out = lax.all_to_all(out.reshape(64, 16, WIDE), PLANE, 0, 0, tiled=True)
    attended, query_grad, key_grad, value_grad = sum_pieces(out)
    return (attended.reshape(1, 1, 128, 1024), query_grad.reshape(1, 1, 128, 1024),
            key_grad.reshape(1, 1, 128, 256), value_grad.reshape(1, 1, 128, 256))


def solution(mesh):
    finer = Mesh(mesh.devices.reshape(4, 8, 2, 2), ("head", "inner", "zl", "core"))
    placed = P(("inner", "zl", "core"), "head", None, None)
    return jax.shard_map(
        on_device,
        mesh=finer,
        in_specs=(placed, placed, placed, placed, P()),
        out_specs=(placed, placed, placed, placed),
        check_vma=False,
    )
```

```python
import jax
import jax.numpy as jnp
from jax import lax
from jax.experimental import pallas as pl
from jax.experimental.pallas import tpu as pltpu
from jax.sharding import Mesh
from jax.sharding import PartitionSpec as P

HD = 128
NEG = -1.0e30
SCALE = HD ** -0.5
SC2 = SCALE * 1.4426950408889634
QT = 16
KP = 16
LIST = 160
WIDE = 1152
bf16, f32, i32 = jnp.bfloat16, jnp.float32, jnp.int32
VMEM = pl.BlockSpec(memory_space=pltpu.VMEM)
SMEM = pl.BlockSpec(memory_space=pltpu.SMEM)


def nt(a, b):
    return lax.dot_general(a, b, (((1,), (1,)), ((), ())), preferred_element_type=f32)


def nn(a, b):
    return jnp.dot(a, b, preferred_element_type=f32)


def row_tile(ref, n, first):
    n = jnp.minimum(n, QT - 1)
    return jnp.concatenate([ref[:, n, :, first + h * HD:first + (h + 1) * HD].reshape(64, HD) for h in range(4)], axis=0)


def head_tile(refs, n):
    n = jnp.minimum(n, QT - 1)
    return jnp.concatenate([ref[:, n].reshape(64, HD) for ref in refs], axis=0)


def key_tile(own_ref, oth_ref, p, first):
    parts = [own_ref[:, p, :, 512 + 256 * h + first:512 + 256 * h + first + HD].reshape(64, HD) for h in (0, 1)]
    parts += [oth_ref[:, p, :, 256 * h + first:256 * h + first + HD].reshape(64, HD) for h in (0, 1)]
    return jnp.concatenate(parts, axis=0)


def unpack(steps, kind, t):
    word = steps[kind, t]
    return lax.shift_right_logical(word, 8), word & 255


def mask_scores(s, n, p, pos_ref, kpos_ref, low):
    kpos = kpos_ref[...]
    kpos = jnp.concatenate([kpos, kpos], axis=1)
    first = p * 1024
    seen = (kpos <= pos_ref[n, 0:1, :] - first) & (kpos >= pos_ref[n, 1:2, :] - first)
    return jnp.where(seen, s, low)


def lanes_at(ref, p):
    return ref[:, pl.ds(pl.multiple_of(p * 256, 256), 256)]


def walk(count, score, soften, gather):
    score(0, 0)
    score(1, 1)
    trips = lax.shift_right_logical(count + 3, 2)

    @pl.loop(0, trips)
    def _(i):
        t = 4 * i
        for half in (0, 2):
            cur, nxt = half, 2 - half
            for k in (0, 1):
                score(t + half + 2 + k, nxt + k)
                soften(t + half + k, cur + k)
                gather(jnp.maximum(t + half - 2 + k, 0), nxt + k)

    last = jnp.maximum(4 * trips - 2, 0)
    gather(last, 2)
    gather(last + 1, 3)


def fwd_kernel(steps, pos_ref, kpos_ref, own_ref, oth_ref, ot_ref, st_ref, vt, m_s, l_s, acc, s_buf, p_buf, a_buf):
    @pl.loop(0, KP, unroll=4)
    def _(p):
        vt[:, pl.ds(pl.multiple_of(p * 256, 256), 256)] = key_tile(own_ref, oth_ref, p, HD).T

    m_s[...] = jnp.full_like(m_s, NEG)
    l_s[...] = jnp.zeros_like(l_s)
    acc[...] = jnp.zeros_like(acc)

    def run(kind):
        def score(t, buf):
            n, p = unpack(steps, kind, t)
            s = nt(key_tile(own_ref, oth_ref, p, 0), row_tile(own_ref, n, 0)) * SC2
            s_buf[buf] = mask_scores(s, n, p, pos_ref, kpos_ref, 2 * NEG) if kind else s

        def soften(t, buf):
            n, _ = unpack(steps, kind, t)
            s = s_buf[buf]
            old = m_s[n]
            new = jnp.maximum(old, jnp.max(s, axis=0, keepdims=True))
            w = jnp.exp2(s - new)
            alpha = jnp.exp2(old - new)
            m_s[n] = new
            l_s[n] = l_s[n] * alpha + jnp.sum(w, axis=0, keepdims=True)
            a_buf[buf] = alpha
            p_buf[buf] = w.astype(bf16)

        def gather(t, buf):
            n, p = unpack(steps, kind, t)
            acc[n] = acc[n] * a_buf[buf] + nn(lanes_at(vt, p), p_buf[buf])

        for buf in (2, 3):
            p_buf[buf] = jnp.zeros((256, 256), bf16)
            a_buf[buf] = jnp.ones((1, 256), f32)
        walk(steps[kind, LIST - 1], score, soften, gather)

    run(0)
    run(1)

    @pl.loop(0, QT, unroll=4)
    def _(n):
        o = acc[n]
        ot_ref[n] = o
        st_ref[n, 0:1, :] = m_s[n]
        st_ref[n, 1:2, :] = l_s[n]


def delta_kernel(st_ref, ot_ref, do0_ref, do1_ref, do2_ref, do3_ref, out_ref):
    refs = (do0_ref, do1_ref, do2_ref, do3_ref)

    @pl.loop(0, QT, unroll=4)
    def _(n):
        total = st_ref[n, 1:2, :]
        some = total > 0.0
        dots = jnp.sum(head_tile(refs, n).T.astype(f32) * ot_ref[n], axis=0, keepdims=True)
        out_ref[n, 0:1, :] = jnp.where(some, st_ref[n, 0:1, :] + jnp.log2(total), NEG)
        out_ref[n, 1:2, :] = jnp.where(some, dots / jnp.where(some, total, 1.0), 0.0)


def scale_kernel(st0_ref, st1_ref, st2_ref, st3_ref, st_ref, ot_ref, stat_ref, *out_refs):
    refs = (st0_ref, st1_ref, st2_ref, st3_ref)

    @pl.loop(0, QT, unroll=4)
    def _(n):
        parts = [refs[0][n]] + [pltpu.roll(refs[k][n], 64 * k, 1) for k in (1, 2, 3)]
        top = jnp.maximum(jnp.maximum(parts[0][0:1], parts[1][0:1]), jnp.maximum(parts[2][0:1], parts[3][0:1]))
        share = [jnp.exp2(part[0:1] - top) for part in parts]
        total = share[0] + share[1] + share[2] + share[3]
        lse = top + jnp.log2(total)
        stat_ref[n, 0:1, :] = lse
        stat_ref[n, 1:2, :] = sum(w * part[1:2] for w, part in zip(share, parts)) / total
        ob = (ot_ref[n] * jnp.exp2(st_ref[n, 0:1, :] - lse)).astype(bf16).T
        for h in range(4):
            out_refs[h][:, n] = ob[h * 64:(h + 1) * 64].reshape(4, 16, HD)
    stat_ref[QT, 0:1, :] = jnp.full((1, 256), -NEG, f32)
    stat_ref[QT, 1:2, :] = jnp.zeros((1, 256), f32)


def bwd_kernel(steps, pos_ref, kpos_ref, stat_ref, own_ref, oth_ref, do0_ref, do1_ref, do2_ref, do3_ref, out_ref,
               oth_out_ref, kt, dq, dk, dv, s_buf, dp_buf, p_buf, ds_buf):
    do_refs = (do0_ref, do1_ref, do2_ref, do3_ref)

    @pl.loop(0, KP, unroll=4)
    def _(p):
        kt[:, pl.ds(pl.multiple_of(p * 256, 256), 256)] = key_tile(own_ref, oth_ref, p, 0).T

    dq[...] = jnp.zeros_like(dq)
    dk[...] = jnp.zeros_like(dk)
    dv[...] = jnp.zeros_like(dv)

    def run(kind):
        def score(t, buf):
            n, p = unpack(steps, kind, t)
            s = nt(key_tile(own_ref, oth_ref, p, 0), row_tile(own_ref, n, 0)) * SC2
            s_buf[buf] = mask_scores(s, n, p, pos_ref, kpos_ref, NEG) if kind else s
            dp_buf[buf] = nt(key_tile(own_ref, oth_ref, p, HD), head_tile(do_refs, n))

        def soften(t, buf):
            n, _ = unpack(steps, kind, t)
            w = jnp.exp2(s_buf[buf] - stat_ref[n, 0:1, :])
            p_buf[buf] = w.astype(bf16)
            ds_buf[buf] = (w * (dp_buf[buf] - stat_ref[n, 1:2, :])).astype(bf16)

        def gather(t, buf):
            n, p = unpack(steps, kind, t)
            ds = ds_buf[buf]
            dv[p] += nn(p_buf[buf], head_tile(do_refs, n))
            dk[p] += nn(ds, row_tile(own_ref, n, 0))
            dq[n] += nn(lanes_at(kt, p), ds)

        for buf in (2, 3):
            p_buf[buf] = jnp.zeros((256, 256), bf16)
            ds_buf[buf] = jnp.zeros((256, 256), bf16)
        walk(steps[kind, LIST - 1], score, soften, gather)

    run(0)
    run(1)

    @pl.loop(0, QT, unroll=4)
    def _(n):
        qb = (dq[n] * SCALE).astype(bf16).T
        for h in range(4):
            out_ref[:, n, :, 640 + h * HD:768 + h * HD] = qb[h * 64:(h + 1) * 64].reshape(4, 16, HD)

    @pl.loop(0, KP, unroll=4)
    def _(p):
        for first, tile in ((0, (dk[p] * SCALE).astype(bf16)), (HD, dv[p].astype(bf16))):
            for h in (0, 1):
                at = 256 * h + first
                out_ref[:, p, :, at:at + HD] = tile[64 * h:64 * h + 64].reshape(4, 16, HD)
                oth_out_ref[:, p, :, at:at + HD] = tile[128 + 64 * h:192 + 64 * h].reshape(4, 16, HD)


def fwd(steps, pos, kpos, own, oth):
    return pl.pallas_call(
        fwd_kernel,
        in_specs=[SMEM] + [VMEM] * 4,
        out_specs=[VMEM, VMEM],
        scratch_shapes=[
            pltpu.VMEM((HD, KP * 256), bf16),
            pltpu.VMEM((QT + 1, 1, 256), f32), pltpu.VMEM((QT + 1, 1, 256), f32), pltpu.VMEM((QT + 1, HD, 256), f32),
            pltpu.VMEM((4, 256, 256), f32), pltpu.VMEM((4, 256, 256), bf16), pltpu.VMEM((4, 1, 256), f32),
        ],
        out_shape=[jax.ShapeDtypeStruct((QT, HD, 256), f32), jax.ShapeDtypeStruct((QT, 4, 256), f32)],
        compiler_params=pltpu.CompilerParams(vmem_limit_bytes=16 << 20),
        cost_estimate=pl.CostEstimate(flops=15 * 10 ** 9, bytes_accessed=8 << 20, transcendentals=0),
        name="fwd",
    )(steps, pos, kpos, own, oth)


def delta(st, ot, dos):
    return pl.pallas_call(
        delta_kernel, in_specs=[VMEM] * 6, out_specs=VMEM, out_shape=jax.ShapeDtypeStruct((QT, 2, 256), f32),
        compiler_params=pltpu.CompilerParams(vmem_limit_bytes=12 << 20), name="delta",
    )(st, ot, *dos)


def scale(sts, st, ot):
    return pl.pallas_call(
        scale_kernel, in_specs=[VMEM] * 6, out_specs=[VMEM] * 5,
        out_shape=[jax.ShapeDtypeStruct((QT + 1, 2, 256), f32)] + [jax.ShapeDtypeStruct((4, QT, 16, HD), bf16)] * 4,
        compiler_params=pltpu.CompilerParams(vmem_limit_bytes=12 << 20), name="scale",
    )(*sts, st, ot)


def bwd(steps, pos, kpos, stat, own, oth, dos):
    return pl.pallas_call(
        bwd_kernel,
        in_specs=[SMEM] + [VMEM] * 9,
        out_specs=[VMEM] * 2,
        scratch_shapes=[
            pltpu.VMEM((HD, KP * 256), bf16),
            pltpu.VMEM((QT + 1, HD, 256), f32), pltpu.VMEM((KP, 256, HD), f32), pltpu.VMEM((KP, 256, HD), f32),
            pltpu.VMEM((4, 256, 256), f32), pltpu.VMEM((4, 256, 256), f32),
            pltpu.VMEM((4, 256, 256), bf16), pltpu.VMEM((4, 256, 256), bf16),
        ],
        out_shape=[jax.ShapeDtypeStruct((4, QT, 16, WIDE), bf16), jax.ShapeDtypeStruct((4, KP, 16, 512), bf16)],
        compiler_params=pltpu.CompilerParams(vmem_limit_bytes=24 << 20),
        cost_estimate=pl.CostEstimate(flops=25 * 10 ** 9, bytes_accessed=8 << 20, transcendentals=0),
        name="bwd",
    )(steps, pos, kpos, stat, own, oth, *dos)


def pack_kernel(q_hbm, k_hbm, v_hbm, do_hbm, out_hbm, q_ref, k_ref, v_ref, do_ref, out_ref, in_sem, out_sem):
    loads = [pltpu.make_async_copy(src, dst, in_sem.at[i])
             for i, (src, dst) in enumerate(((q_hbm, q_ref), (k_hbm, k_ref), (v_hbm, v_ref), (do_hbm, do_ref)))]
    for load in loads:
        load.start()
    for load in loads:
        load.wait()
    stores = []
    for j in range(4):
        for u in range(8):
            for g in range(2):
                at = u * 2 + g
                tokens = slice(16 * u, 16 * u + 16)
                for r in range(4):
                    head = 512 * g + HD * ((j - r) % 4)
                    out_ref[j, at, :, r * HD:r * HD + HD] = q_ref[tokens, head:head + HD]
                head = 512 * g + HD * j
                out_ref[j, at, :, 1024:1152] = do_ref[tokens, head:head + HD]
                for h in (0, 1):
                    rows = slice(32 * j + 16 * h, 32 * j + 16 * h + 16)
                    out_ref[j, at, :, 512 + 256 * h:640 + 256 * h] = k_ref[rows, HD * g:HD * g + HD]
                    out_ref[j, at, :, 640 + 256 * h:768 + 256 * h] = v_ref[rows, HD * g:HD * g + HD]
        stores.append(pltpu.make_async_copy(out_ref.at[j], out_hbm.at[j], out_sem.at[j]))
        stores[-1].start()
    for store in stores:
        store.wait()


def pack(q, k, v, do):
    any_spec = pl.BlockSpec(memory_space=pltpu.HBM)
    return pl.pallas_call(
        pack_kernel, in_specs=[any_spec] * 4, out_specs=any_spec,
        out_shape=jax.ShapeDtypeStruct((4, 16, 16, WIDE), bf16),
        scratch_shapes=[pltpu.VMEM((128, 1024), bf16), pltpu.VMEM((128, 256), bf16), pltpu.VMEM((128, 256), bf16),
                        pltpu.VMEM((128, 1024), bf16), pltpu.VMEM((4, 16, 16, WIDE), bf16), pltpu.SemaphoreType.DMA((4,)), pltpu.SemaphoreType.DMA((4,))],
        compiler_params=pltpu.CompilerParams(vmem_limit_bytes=60 << 20), name="pack",
    )(q, k, v, do)


def gather_kernel(oth_ref, o0_ref, o1_ref, o2_ref, o3_ref, out_ref, sum_ref):
    out_ref[...] = oth_ref[...]
    total = o0_ref[...].astype(f32) + o1_ref[...].astype(f32) + o2_ref[...].astype(f32) + o3_ref[...].astype(f32)
    sum_ref[...] = total.astype(bf16)


def gather_parts(oth, heads):
    return pl.pallas_call(
        gather_kernel, in_specs=[VMEM] * 5, out_specs=[VMEM] * 2,
        out_shape=[jax.ShapeDtypeStruct(oth.shape, bf16), jax.ShapeDtypeStruct(heads[0].shape, bf16)],
        compiler_params=pltpu.CompilerParams(vmem_limit_bytes=12 << 20), name="gather_parts",
    )(oth, *heads)


def add_kernel(own_ref, other_ref, head_ref, out_ref):
    out_ref[..., :512] = (own_ref[..., :512].astype(f32) + other_ref[...].astype(f32)).astype(bf16)
    out_ref[..., 512:] = head_ref[...]


def add_parts(out, other, head):
    block = lambda columns: pl.BlockSpec((1, KP, 16, columns), lambda i: (i, 0, 0, 0))
    return pl.pallas_call(
        add_kernel, grid=(4,), in_specs=[block(640), block(512), block(HD)], out_specs=block(640),
        out_shape=jax.ShapeDtypeStruct(out.shape, bf16), input_output_aliases={0: 0},
        compiler_params=pltpu.CompilerParams(vmem_limit_bytes=12 << 20), name="add_parts",
    )(out, other, head)


def sum_kernel(in_ref, at_ref, qg_ref, kg_ref, vg_ref):
    for u in range(8):
        for g in range(2):
            rows = slice(16 * u, 16 * u + 16)
            for h in range(4):
                cols = slice(512 * g + HD * h, 512 * g + HD * h + HD)
                at_ref[rows, cols] = in_ref[h * 16 + u * 2 + g, :, 512:640]
                first = [640 + HD * ((j - h) % 4) for j in range(4)]
                parts = [in_ref[j * 16 + u * 2 + g, :, first[j]:first[j] + HD].astype(f32) for j in range(4)]
                qg_ref[rows, cols] = (parts[0] + parts[1] + parts[2] + parts[3]).astype(bf16)
    for j in range(4):
        for g in range(2):
            for h in (0, 1):
                rows, cols = slice(32 * j + 16 * h, 32 * j + 16 * h + 16), slice(HD * g, HD * g + HD)
                both = sum(in_ref[j * 16 + u * 2 + g, :, 256 * h:256 * h + 256].astype(f32) for u in range(8))
                kg_ref[rows, cols] = both[:, :HD].astype(bf16)
                vg_ref[rows, cols] = both[:, HD:].astype(bf16)


def sum_pieces(pieces):
    big, small = jax.ShapeDtypeStruct((128, 1024), bf16), jax.ShapeDtypeStruct((128, 256), bf16)
    return pl.pallas_call(
        sum_kernel, in_specs=[VMEM], out_specs=[VMEM] * 4, out_shape=[big, big, small, small],
        compiler_params=pltpu.CompilerParams(vmem_limit_bytes=12 << 20), name="sum_pieces",
    )(pieces)


def make_plan(lengths, core, u, j):
    n = jnp.arange(QT + 1, dtype=i32)[:, None, None]
    x = jnp.arange(4, dtype=i32)[None, :, None]
    t = jnp.arange(16, dtype=i32)[None, None, :]
    pos = (512 * (2 * n + core) + 128 * x + 16 * u + t).reshape(QT + 1, 64)
    docs = jnp.arange(lengths.shape[0])
    ends = jnp.sum(jnp.where(docs[:, None] <= docs[None, :], lengths[:, None], 0), axis=0)
    start = jnp.sum(jnp.where(ends[None, None, :] <= pos[:, :, None], lengths, 0), axis=-1)
    rows = jnp.stack([jnp.tile(pos, (1, 4)), jnp.tile(start, (1, 4))], axis=1).astype(i32)
    low = (start[:QT, 0] // 1024)[None, :]
    plain_low = ((start[:QT, -1] + 1023) // 1024)[None, :]
    d = jnp.arange(KP, dtype=i32)[:, None]
    m = jnp.arange(QT, dtype=i32)[None, :]
    live = (m - d >= 0) & (m - d >= low)
    plain = live & (d > 0) & (m - d >= plain_low)
    code = (m * 256 + m - d).reshape(1, QT * KP)
    order = jnp.arange(QT * KP, dtype=i32)
    earlier = order[:, None] < order[None, :]
    at = jnp.arange(LIST, dtype=i32)[:, None]

    def compact(mask):
        mask = mask.reshape(1, QT * KP)
        rank = jnp.sum((earlier & mask.reshape(QT * KP, 1)).astype(i32), axis=0, keepdims=True)
        listed = QT * 256 + jnp.sum(jnp.where(mask & (rank == at), code - QT * 256, 0), axis=1)
        return jnp.where(at[:, 0] == LIST - 1, jnp.sum(mask.astype(i32)), listed)

    steps = jnp.stack([compact(plain), compact(live & ~plain)]).astype(i32)
    r = jnp.arange(256, dtype=i32)
    parity = jnp.where(r < 128, core, 1 - core)
    kpos = 512 * parity + 128 * (r % 64 // 16) + 32 * j + 16 * (r // 64 % 2) + r % 16
    return steps, rows, jnp.broadcast_to(kpos[:, None], (256, 128)).astype(i32)


PLANE = ("head", "inner", "zl")


def on_device(query_rows, key_rows, value_rows, out_grad, lengths):
    j, u, core = (lax.axis_index(name) for name in ("head", "inner", "core"))
    swap = [(0, 1), (1, 0)]
    steps, pos, kpos = make_plan(lengths, core, u, j)
    pieces = pack(query_rows.reshape(128, 1024), key_rows.reshape(128, 256), value_rows.reshape(128, 256),
                  out_grad.reshape(128, 1024))
    own = lax.all_to_all(pieces.reshape(64, 16, WIDE), PLANE, 0, 0, tiled=True).reshape(4, QT, 16, WIDE)
    oth = lax.ppermute(own[..., 512:1024], "core", swap)

    def along(x, k):
        return lax.ppermute(x, "head", [(i, (i + k) % 4) for i in range(4)])

    do = own[..., 1024:]
    dos = [do] + [along(do, k) for k in (1, 2, 3)]
    ot, st = fwd(steps, pos, kpos, own, oth)
    part = delta(st, ot, dos)
    stat, *heads = scale([part] + [along(part, k) for k in (1, 2, 3)], st, ot)
    heads = heads[:1] + [along(heads[k], -k) for k in (1, 2, 3)]
    out, oth_out = bwd(steps, pos, kpos, stat, own, oth, dos)
    oth_out, head = gather_parts(oth_out, heads)
    out = add_parts(out, lax.ppermute(oth_out, "core", swap), head)
    out = lax.all_to_all(out.reshape(64, 16, WIDE), PLANE, 0, 0, tiled=True)
    attended, query_grad, key_grad, value_grad = sum_pieces(out)
    return (attended.reshape(1, 1, 128, 1024), query_grad.reshape(1, 1, 128, 1024),
            key_grad.reshape(1, 1, 128, 256), value_grad.reshape(1, 1, 128, 256))


def solution(mesh):
    finer = Mesh(mesh.devices.reshape(4, 8, 2, 2), ("head", "inner", "zl", "core"))
    placed = P(("inner", "zl", "core"), "head", None, None)
    return jax.shard_map(
        on_device,
        mesh=finer,
        in_specs=(placed, placed, placed, placed, P()),
        out_specs=(placed, placed, placed, placed),
        check_vma=False,
    )
```

```python
import jax
import jax.numpy as jnp
from jax import lax
from jax.experimental import pallas as pl
from jax.experimental.pallas import tpu as pltpu
from jax.sharding import Mesh
from jax.sharding import PartitionSpec as P

HD = 128
NEG = -1.0e30
SCALE = HD ** -0.5
SC2 = SCALE * 1.4426950408889634
QT = 16
KP = 16
LIST = 160
WIDE = 1152
bf16, f32, i32 = jnp.bfloat16, jnp.float32, jnp.int32
VMEM = pl.BlockSpec(memory_space=pltpu.VMEM)
SMEM = pl.BlockSpec(memory_space=pltpu.SMEM)


def nt(a, b):
    return lax.dot_general(a, b, (((1,), (1,)), ((), ())), preferred_element_type=f32)


def nn(a, b):
    return jnp.dot(a, b, preferred_element_type=f32)


def row_tile(ref, n, first):
    n = jnp.minimum(n, QT - 1)
    return jnp.concatenate([ref[:, n, :, first + h * HD:first + (h + 1) * HD].reshape(64, HD) for h in range(4)], axis=0)


def head_tile(refs, n):
    n = jnp.minimum(n, QT - 1)
    return jnp.concatenate([ref[:, n].reshape(64, HD) for ref in refs], axis=0)


def key_tile(own_ref, oth_ref, p, first):
    parts = [own_ref[:, p, :, 512 + 256 * h + first:512 + 256 * h + first + HD].reshape(64, HD) for h in (0, 1)]
    parts += [oth_ref[:, p, :, 256 * h + first:256 * h + first + HD].reshape(64, HD) for h in (0, 1)]
    return jnp.concatenate(parts, axis=0)


def unpack(steps, kind, t):
    word = steps[kind, t]
    return lax.shift_right_logical(word, 8), word & 255


def mask_scores(s, n, p, pos_ref, kpos_ref, low):
    kpos = kpos_ref[...]
    kpos = jnp.concatenate([kpos, kpos], axis=1)
    first = p * 1024
    seen = (kpos <= pos_ref[n, 0:1, :] - first) & (kpos >= pos_ref[n, 1:2, :] - first)
    return jnp.where(seen, s, low)


def lanes_at(ref, p):
    return ref[:, pl.ds(pl.multiple_of(p * 256, 256), 256)]


def walk(count, score, soften, gather):
    score(0, 0)
    score(1, 1)
    trips = lax.shift_right_logical(count + 3, 2)

    @pl.loop(0, trips)
    def _(i):
        t = 4 * i
        for half in (0, 2):
            cur, nxt = half, 2 - half
            for k in (0, 1):
                score(t + half + 2 + k, nxt + k)
                soften(t + half + k, cur + k)
                gather(jnp.maximum(t + half - 2 + k, 0), nxt + k)

    last = jnp.maximum(4 * trips - 2, 0)
    gather(last, 2)
    gather(last + 1, 3)


def walk_two(count, soften, gather):
    soften(0, 0)
    soften(1, 1)

    @pl.loop(0, lax.shift_right_logical(count + 3, 2))
    def _(i):
        t = 4 * i
        for half in (0, 2):
            cur, nxt = half, 2 - half
            for k in (0, 1):
                gather(t + half + k, cur + k)
                soften(t + half + 2 + k, nxt + k)


def fwd_kernel(steps, pos_ref, kpos_ref, own_ref, oth_ref, ot_ref, st_ref, vt, m_s, l_s, acc, s_buf, p_buf, a_buf):
    @pl.loop(0, KP, unroll=4)
    def _(p):
        vt[:, pl.ds(pl.multiple_of(p * 256, 256), 256)] = key_tile(own_ref, oth_ref, p, HD).T

    m_s[...] = jnp.full_like(m_s, NEG)
    l_s[...] = jnp.zeros_like(l_s)
    acc[...] = jnp.zeros_like(acc)

    def run(kind):
        def score(t, buf):
            n, p = unpack(steps, kind, t)
            s = nt(key_tile(own_ref, oth_ref, p, 0), row_tile(own_ref, n, 0)) * SC2
            s_buf[buf] = mask_scores(s, n, p, pos_ref, kpos_ref, 2 * NEG) if kind else s

        def soften(t, buf):
            n, _ = unpack(steps, kind, t)
            s = s_buf[buf]
            old = m_s[n]
            new = jnp.maximum(old, jnp.max(s, axis=0, keepdims=True))
            w = jnp.exp2(s - new)
            alpha = jnp.exp2(old - new)
            m_s[n] = new
            l_s[n] = l_s[n] * alpha + jnp.sum(w, axis=0, keepdims=True)
            a_buf[buf] = alpha
            p_buf[buf] = w.astype(bf16)

        def gather(t, buf):
            n, p = unpack(steps, kind, t)
            acc[n] = acc[n] * a_buf[buf] + nn(lanes_at(vt, p), p_buf[buf])

        for buf in (2, 3):
            p_buf[buf] = jnp.zeros((256, 256), bf16)
            a_buf[buf] = jnp.ones((1, 256), f32)
        walk(steps[kind, LIST - 1], score, soften, gather)

    run(0)
    run(1)

    @pl.loop(0, QT, unroll=4)
    def _(n):
        o = acc[n]
        ot_ref[n] = o
        st_ref[n, 0:1, :] = m_s[n]
        st_ref[n, 1:2, :] = l_s[n]


def delta_kernel(st_ref, ot_ref, do0_ref, do1_ref, do2_ref, do3_ref, out_ref):
    refs = (do0_ref, do1_ref, do2_ref, do3_ref)

    @pl.loop(0, QT, unroll=4)
    def _(n):
        total = st_ref[n, 1:2, :]
        some = total > 0.0
        dots = jnp.sum(head_tile(refs, n).T.astype(f32) * ot_ref[n], axis=0, keepdims=True)
        out_ref[n, 0:1, :] = jnp.where(some, st_ref[n, 0:1, :] + jnp.log2(total), NEG)
        out_ref[n, 1:2, :] = jnp.where(some, dots / jnp.where(some, total, 1.0), 0.0)


def scale_kernel(st0_ref, st1_ref, st2_ref, st3_ref, st_ref, ot_ref, stat_ref, *out_refs):
    refs = (st0_ref, st1_ref, st2_ref, st3_ref)

    @pl.loop(0, QT, unroll=4)
    def _(n):
        parts = [refs[0][n]] + [pltpu.roll(refs[k][n], 64 * k, 1) for k in (1, 2, 3)]
        top = jnp.maximum(jnp.maximum(parts[0][0:1], parts[1][0:1]), jnp.maximum(parts[2][0:1], parts[3][0:1]))
        share = [jnp.exp2(part[0:1] - top) for part in parts]
        total = share[0] + share[1] + share[2] + share[3]
        lse = top + jnp.log2(total)
        stat_ref[n, 0:1, :] = lse
        stat_ref[n, 1:2, :] = sum(w * part[1:2] for w, part in zip(share, parts)) / total
        ob = (ot_ref[n] * jnp.exp2(st_ref[n, 0:1, :] - lse)).astype(bf16).T
        for h in range(4):
            out_refs[h][:, n] = ob[h * 64:(h + 1) * 64].reshape(4, 16, HD)
    stat_ref[QT, 0:1, :] = jnp.full((1, 256), -NEG, f32)
    stat_ref[QT, 1:2, :] = jnp.zeros((1, 256), f32)


def bwd_kernel(steps, pos_ref, kpos_ref, stat_ref, own_ref, oth_ref, do0_ref, do1_ref, do2_ref, do3_ref, kt, out_ref,
               oth_out_ref, dq, dk, dv, p_buf, ds_buf):
    do_refs = (do0_ref, do1_ref, do2_ref, do3_ref)

    dq[...] = jnp.zeros_like(dq)
    dk[...] = jnp.zeros_like(dk)
    dv[...] = jnp.zeros_like(dv)

    def run(kind):
        def soften(t, buf):
            n, p = unpack(steps, kind, t)
            s = nt(key_tile(own_ref, oth_ref, p, 0), row_tile(own_ref, n, 0)) * SC2
            if kind:
                s = mask_scores(s, n, p, pos_ref, kpos_ref, NEG)
            w = jnp.exp2(s - stat_ref[n, 0:1, :])
            dp = nt(key_tile(own_ref, oth_ref, p, HD), head_tile(do_refs, n))
            p_buf[buf] = w.astype(bf16)
            ds_buf[buf] = (w * (dp - stat_ref[n, 1:2, :])).astype(bf16)

        def gather(t, buf):
            n, p = unpack(steps, kind, t)
            ds = ds_buf[buf]
            dv[p] += nn(p_buf[buf], head_tile(do_refs, n))
            dk[p] += nn(ds, row_tile(own_ref, n, 0))
            dq[n] += nn(lanes_at(kt, p), ds)

        walk_two(steps[kind, LIST - 1], soften, gather)

    run(0)
    run(1)

    @pl.loop(0, QT, unroll=4)
    def _(n):
        qb = (dq[n] * SCALE).astype(bf16).T
        for h in range(4):
            out_ref[:, n, :, 640 + h * HD:768 + h * HD] = qb[h * 64:(h + 1) * 64].reshape(4, 16, HD)

    @pl.loop(0, KP, unroll=4)
    def _(p):
        for first, tile in ((0, (dk[p] * SCALE).astype(bf16)), (HD, dv[p].astype(bf16))):
            for h in (0, 1):
                at = 256 * h + first
                out_ref[:, p, :, at:at + HD] = tile[64 * h:64 * h + 64].reshape(4, 16, HD)
                oth_out_ref[:, p, :, at:at + HD] = tile[128 + 64 * h:192 + 64 * h].reshape(4, 16, HD)


def fwd(steps, pos, kpos, own, oth):
    return pl.pallas_call(
        fwd_kernel,
        in_specs=[SMEM] + [VMEM] * 4,
        out_specs=[VMEM, VMEM],
        scratch_shapes=[
            pltpu.VMEM((HD, KP * 256), bf16),
            pltpu.VMEM((QT + 1, 1, 256), f32), pltpu.VMEM((QT + 1, 1, 256), f32), pltpu.VMEM((QT + 1, HD, 256), f32),
            pltpu.VMEM((4, 256, 256), f32), pltpu.VMEM((4, 256, 256), bf16), pltpu.VMEM((4, 1, 256), f32),
        ],
        out_shape=[jax.ShapeDtypeStruct((QT, HD, 256), f32), jax.ShapeDtypeStruct((QT, 4, 256), f32)],
        compiler_params=pltpu.CompilerParams(vmem_limit_bytes=16 << 20),
        cost_estimate=pl.CostEstimate(flops=15 * 10 ** 9, bytes_accessed=8 << 20, transcendentals=0),
        name="fwd",
    )(steps, pos, kpos, own, oth)


def delta(st, ot, dos):
    return pl.pallas_call(
        delta_kernel, in_specs=[VMEM] * 6, out_specs=VMEM, out_shape=jax.ShapeDtypeStruct((QT, 2, 256), f32),
        compiler_params=pltpu.CompilerParams(vmem_limit_bytes=12 << 20), name="delta",
    )(st, ot, *dos)


def scale(sts, st, ot):
    return pl.pallas_call(
        scale_kernel, in_specs=[VMEM] * 6, out_specs=[VMEM] * 5,
        out_shape=[jax.ShapeDtypeStruct((QT + 1, 2, 256), f32)] + [jax.ShapeDtypeStruct((4, QT, 16, HD), bf16)] * 4,
        compiler_params=pltpu.CompilerParams(vmem_limit_bytes=12 << 20), name="scale",
    )(*sts, st, ot)


def turn_kernel(own_ref, oth_ref, kt):
    @pl.loop(0, KP, unroll=4)
    def _(p):
        kt[:, pl.ds(pl.multiple_of(p * 256, 256), 256)] = key_tile(own_ref, oth_ref, p, 0).T


def turn_keys(own, oth):
    return pl.pallas_call(
        turn_kernel, in_specs=[VMEM] * 2, out_specs=VMEM, out_shape=jax.ShapeDtypeStruct((HD, KP * 256), bf16),
        cost_estimate=pl.CostEstimate(flops=10 ** 9, bytes_accessed=2 << 20, transcendentals=0),
        compiler_params=pltpu.CompilerParams(vmem_limit_bytes=12 << 20), name="turn_keys",
    )(own, oth)


def bwd(steps, pos, kpos, stat, own, oth, dos, kt):
    return pl.pallas_call(
        bwd_kernel,
        in_specs=[SMEM] + [VMEM] * 10,
        out_specs=[VMEM] * 2,
        scratch_shapes=[
            pltpu.VMEM((QT + 1, HD, 256), f32), pltpu.VMEM((KP, 256, HD), f32), pltpu.VMEM((KP, 256, HD), f32),
            pltpu.VMEM((4, 256, 256), bf16), pltpu.VMEM((4, 256, 256), bf16),
        ],
        out_shape=[jax.ShapeDtypeStruct((4, QT, 16, WIDE), bf16), jax.ShapeDtypeStruct((4, KP, 16, 512), bf16)],
        compiler_params=pltpu.CompilerParams(vmem_limit_bytes=24 << 20),
        cost_estimate=pl.CostEstimate(flops=25 * 10 ** 9, bytes_accessed=8 << 20, transcendentals=0),
        name="bwd",
    )(steps, pos, kpos, stat, own, oth, *dos, kt)


def pack_kernel(q_hbm, k_hbm, v_hbm, do_hbm, out_hbm, q_ref, k_ref, v_ref, do_ref, out_ref, in_sem, out_sem):
    loads = [pltpu.make_async_copy(src, dst, in_sem.at[i])
             for i, (src, dst) in enumerate(((q_hbm, q_ref), (k_hbm, k_ref), (v_hbm, v_ref), (do_hbm, do_ref)))]
    for load in loads:
        load.start()
    for load in loads:
        load.wait()
    stores = []
    for j in range(4):
        for u in range(8):
            for g in range(2):
                at = u * 2 + g
                tokens = slice(16 * u, 16 * u + 16)
                for r in range(4):
                    head = 512 * g + HD * ((j - r) % 4)
                    out_ref[j, at, :, r * HD:r * HD + HD] = q_ref[tokens, head:head + HD]
                head = 512 * g + HD * j
                out_ref[j, at, :, 1024:1152] = do_ref[tokens, head:head + HD]
                for h in (0, 1):
                    rows = slice(32 * j + 16 * h, 32 * j + 16 * h + 16)
                    out_ref[j, at, :, 512 + 256 * h:640 + 256 * h] = k_ref[rows, HD * g:HD * g + HD]
                    out_ref[j, at, :, 640 + 256 * h:768 + 256 * h] = v_ref[rows, HD * g:HD * g + HD]
        stores.append(pltpu.make_async_copy(out_ref.at[j], out_hbm.at[j], out_sem.at[j]))
        stores[-1].start()
    for store in stores:
        store.wait()


def pack(q, k, v, do):
    any_spec = pl.BlockSpec(memory_space=pltpu.HBM)
    return pl.pallas_call(
        pack_kernel, in_specs=[any_spec] * 4, out_specs=any_spec,
        out_shape=jax.ShapeDtypeStruct((4, 16, 16, WIDE), bf16),
        scratch_shapes=[pltpu.VMEM((128, 1024), bf16), pltpu.VMEM((128, 256), bf16), pltpu.VMEM((128, 256), bf16),
                        pltpu.VMEM((128, 1024), bf16), pltpu.VMEM((4, 16, 16, WIDE), bf16), pltpu.SemaphoreType.DMA((4,)), pltpu.SemaphoreType.DMA((4,))],
        compiler_params=pltpu.CompilerParams(vmem_limit_bytes=60 << 20), name="pack",
    )(q, k, v, do)


def gather_kernel(oth_ref, o0_ref, o1_ref, o2_ref, o3_ref, out_ref, sum_ref):
    out_ref[...] = oth_ref[...]
    total = o0_ref[...].astype(f32) + o1_ref[...].astype(f32) + o2_ref[...].astype(f32) + o3_ref[...].astype(f32)
    sum_ref[...] = total.astype(bf16)


def gather_parts(oth, heads):
    return pl.pallas_call(
        gather_kernel, in_specs=[VMEM] * 5, out_specs=[VMEM] * 2,
        out_shape=[jax.ShapeDtypeStruct(oth.shape, bf16), jax.ShapeDtypeStruct(heads[0].shape, bf16)],
        compiler_params=pltpu.CompilerParams(vmem_limit_bytes=12 << 20), name="gather_parts",
    )(oth, *heads)


def add_kernel(own_ref, other_ref, head_ref, out_ref):
    out_ref[..., :512] = (own_ref[..., :512].astype(f32) + other_ref[...].astype(f32)).astype(bf16)
    out_ref[..., 512:] = head_ref[...]


def add_parts(out, other, head):
    block = lambda columns: pl.BlockSpec((1, KP, 16, columns), lambda i: (i, 0, 0, 0))
    return pl.pallas_call(
        add_kernel, grid=(4,), in_specs=[block(640), block(512), block(HD)], out_specs=block(640),
        out_shape=jax.ShapeDtypeStruct(out.shape, bf16), input_output_aliases={0: 0},
        compiler_params=pltpu.CompilerParams(vmem_limit_bytes=12 << 20), name="add_parts",
    )(out, other, head)


def sum_kernel(in_ref, at_ref, qg_ref, kg_ref, vg_ref):
    for u in range(8):
        for g in range(2):
            rows = slice(16 * u, 16 * u + 16)
            for h in range(4):
                cols = slice(512 * g + HD * h, 512 * g + HD * h + HD)
                at_ref[rows, cols] = in_ref[h * 16 + u * 2 + g, :, 512:640]
                first = [640 + HD * ((j - h) % 4) for j in range(4)]
                parts = [in_ref[j * 16 + u * 2 + g, :, first[j]:first[j] + HD].astype(f32) for j in range(4)]
                qg_ref[rows, cols] = (parts[0] + parts[1] + parts[2] + parts[3]).astype(bf16)
    for j in range(4):
        for g in range(2):
            for h in (0, 1):
                rows, cols = slice(32 * j + 16 * h, 32 * j + 16 * h + 16), slice(HD * g, HD * g + HD)
                both = sum(in_ref[j * 16 + u * 2 + g, :, 256 * h:256 * h + 256].astype(f32) for u in range(8))
                kg_ref[rows, cols] = both[:, :HD].astype(bf16)
                vg_ref[rows, cols] = both[:, HD:].astype(bf16)


def sum_pieces(pieces):
    big, small = jax.ShapeDtypeStruct((128, 1024), bf16), jax.ShapeDtypeStruct((128, 256), bf16)
    return pl.pallas_call(
        sum_kernel, in_specs=[VMEM], out_specs=[VMEM] * 4, out_shape=[big, big, small, small],
        compiler_params=pltpu.CompilerParams(vmem_limit_bytes=12 << 20), name="sum_pieces",
    )(pieces)


def make_plan(lengths, core, u, j):
    n = jnp.arange(QT + 1, dtype=i32)[:, None, None]
    x = jnp.arange(4, dtype=i32)[None, :, None]
    t = jnp.arange(16, dtype=i32)[None, None, :]
    pos = (512 * (2 * n + core) + 128 * x + 16 * u + t).reshape(QT + 1, 64)
    docs = jnp.arange(lengths.shape[0])
    ends = jnp.sum(jnp.where(docs[:, None] <= docs[None, :], lengths[:, None], 0), axis=0)
    start = jnp.sum(jnp.where(ends[None, None, :] <= pos[:, :, None], lengths, 0), axis=-1)
    rows = jnp.stack([jnp.tile(pos, (1, 4)), jnp.tile(start, (1, 4))], axis=1).astype(i32)
    low = (start[:QT, 0] // 1024)[None, :]
    plain_low = ((start[:QT, -1] + 1023) // 1024)[None, :]
    d = jnp.arange(KP, dtype=i32)[:, None]
    m = jnp.arange(QT, dtype=i32)[None, :]
    live = (m - d >= 0) & (m - d >= low)
    plain = live & (d > 0) & (m - d >= plain_low)
    code = (m * 256 + m - d).reshape(1, QT * KP)
    order = jnp.arange(QT * KP, dtype=i32)
    earlier = order[:, None] < order[None, :]
    at = jnp.arange(LIST, dtype=i32)[:, None]

    def compact(mask):
        mask = mask.reshape(1, QT * KP)
        rank = jnp.sum((earlier & mask.reshape(QT * KP, 1)).astype(i32), axis=0, keepdims=True)
        listed = QT * 256 + jnp.sum(jnp.where(mask & (rank == at), code - QT * 256, 0), axis=1)
        return jnp.where(at[:, 0] == LIST - 1, jnp.sum(mask.astype(i32)), listed)

    steps = jnp.stack([compact(plain), compact(live & ~plain)]).astype(i32)
    r = jnp.arange(256, dtype=i32)
    parity = jnp.where(r < 128, core, 1 - core)
    kpos = 512 * parity + 128 * (r % 64 // 16) + 32 * j + 16 * (r // 64 % 2) + r % 16
    return steps, rows, jnp.broadcast_to(kpos[:, None], (256, 128)).astype(i32)


PLANE = ("head", "inner", "zl")


def on_device(query_rows, key_rows, value_rows, out_grad, lengths):
    j, u, core = (lax.axis_index(name) for name in ("head", "inner", "core"))
    swap = [(0, 1), (1, 0)]
    steps, pos, kpos = make_plan(lengths, core, u, j)
    pieces = pack(query_rows.reshape(128, 1024), key_rows.reshape(128, 256), value_rows.reshape(128, 256),
                  out_grad.reshape(128, 1024))
    own = lax.all_to_all(pieces.reshape(64, 16, WIDE), PLANE, 0, 0, tiled=True).reshape(4, QT, 16, WIDE)
    own, steps, pos, kpos = lax.optimization_barrier((own, steps, pos, kpos))
    oth = lax.ppermute(own[..., 512:1024], "core", swap)

    def along(x, k):
        return lax.ppermute(x, "head", [(i, (i + k) % 4) for i in range(4)])

    do = own[..., 1024:]
    dos = [do] + [along(do, k) for k in (1, 2, 3)]
    ot, st = fwd(steps, pos, kpos, own, oth)
    part = delta(st, ot, dos)
    stat, *heads = scale([part] + [along(part, k) for k in (1, 2, 3)], st, ot)
    heads = heads[:1] + [along(heads[k], -k) for k in (1, 2, 3)]
    out, oth_out = bwd(steps, pos, kpos, stat, own, oth, dos, turn_keys(own, oth))
    oth_out, head = gather_parts(oth_out, heads)
    out = add_parts(out, lax.ppermute(oth_out, "core", swap), head)
    out = lax.all_to_all(out.reshape(64, 16, WIDE), PLANE, 0, 0, tiled=True)
    attended, query_grad, key_grad, value_grad = sum_pieces(out)
    return (attended.reshape(1, 1, 128, 1024), query_grad.reshape(1, 1, 128, 1024),
            key_grad.reshape(1, 1, 128, 256), value_grad.reshape(1, 1, 128, 256))


def solution(mesh):
    finer = Mesh(mesh.devices.reshape(4, 8, 2, 2), ("head", "inner", "zl", "core"))
    placed = P(("inner", "zl", "core"), "head", None, None)
    return jax.shard_map(
        on_device,
        mesh=finer,
        in_specs=(placed, placed, placed, placed, P()),
        out_specs=(placed, placed, placed, placed),
        check_vma=False,
    )
```

```python
import jax
import jax.numpy as jnp
from jax import lax
from jax.experimental import pallas as pl
from jax.experimental.pallas import tpu as pltpu
from jax.sharding import Mesh
from jax.sharding import PartitionSpec as P

HD = 128
NEG = -1.0e30
SCALE = HD ** -0.5
SC2 = SCALE * 1.4426950408889634
QT = 16
KP = 16
LIST = 160
TRIP = 8
WIDE = 1152
bf16, f32, i32 = jnp.bfloat16, jnp.float32, jnp.int32
VMEM = pl.BlockSpec(memory_space=pltpu.VMEM)
SMEM = pl.BlockSpec(memory_space=pltpu.SMEM)


def nt(a, b):
    return lax.dot_general(a, b, (((1,), (1,)), ((), ())), preferred_element_type=f32)


def nn(a, b):
    return jnp.dot(a, b, preferred_element_type=f32)


def row_tile(ref, n, first):
    n = jnp.minimum(n, QT - 1)
    return jnp.concatenate([ref[:, n, :, first + h * HD:first + (h + 1) * HD].reshape(64, HD) for h in range(4)], axis=0)


def head_tile(refs, n):
    n = jnp.minimum(n, QT - 1)
    return jnp.concatenate([ref[:, n].reshape(64, HD) for ref in refs], axis=0)


def key_tile(own_ref, oth_ref, p, first):
    parts = [own_ref[:, p, :, 512 + 256 * h + first:512 + 256 * h + first + HD].reshape(64, HD) for h in (0, 1)]
    parts += [oth_ref[:, p, :, 256 * h + first:256 * h + first + HD].reshape(64, HD) for h in (0, 1)]
    return jnp.concatenate(parts, axis=0)


def unpack(steps, kind, t):
    word = steps[kind, t]
    return lax.shift_right_logical(word, 8), word & 255


def mask_scores(s, n, p, pos_ref, kpos_ref, low):
    kpos = kpos_ref[...]
    kpos = jnp.concatenate([kpos, kpos], axis=1)
    first = p * 1024
    seen = (kpos <= pos_ref[n, 0:1, :] - first) & (kpos >= pos_ref[n, 1:2, :] - first)
    return jnp.where(seen, s, low)


def lanes_at(ref, p):
    return ref[:, pl.ds(pl.multiple_of(p * 256, 256), 256)]


def walk(count, score, soften, gather):
    score(0, 0)
    score(1, 1)
    trips = lax.shift_right_logical(count + 3, 2)

    @pl.loop(0, trips)
    def _(i):
        t = 4 * i
        for half in (0, 2):
            cur, nxt = half, 2 - half
            for k in (0, 1):
                score(t + half + 2 + k, nxt + k)
                soften(t + half + k, cur + k)
                gather(jnp.maximum(t + half - 2 + k, 0), nxt + k)

    last = jnp.maximum(4 * trips - 2, 0)
    gather(last, 2)
    gather(last + 1, 3)


def walk_two(count, soften, gather):
    for k in range(4):
        soften(k, k)

    @pl.loop(0, lax.shift_right_logical(count + 7, 3))
    def _(i):
        t = 8 * i
        for half in (0, 4):
            cur, nxt = half, 4 - half
            for k in range(4):
                gather(t + half + k, cur + k)
                soften(t + half + 4 + k, nxt + k)


def fwd_kernel(steps, pos_ref, kpos_ref, own_ref, oth_ref, ot_ref, st_ref, vt, m_s, l_s, acc, s_buf, p_buf, a_buf):
    @pl.loop(0, KP, unroll=4)
    def _(p):
        vt[:, pl.ds(pl.multiple_of(p * 256, 256), 256)] = key_tile(own_ref, oth_ref, p, HD).T

    m_s[...] = jnp.full_like(m_s, NEG)
    l_s[...] = jnp.zeros_like(l_s)
    acc[...] = jnp.zeros_like(acc)

    def run(kind):
        def score(t, buf):
            n, p = unpack(steps, kind, t)
            s = nt(key_tile(own_ref, oth_ref, p, 0), row_tile(own_ref, n, 0)) * SC2
            s_buf[buf] = mask_scores(s, n, p, pos_ref, kpos_ref, 2 * NEG) if kind else s

        def soften(t, buf):
            n, _ = unpack(steps, kind, t)
            s = s_buf[buf]
            old = m_s[n]
            new = jnp.maximum(old, jnp.max(s, axis=0, keepdims=True))
            w = jnp.exp2(s - new)
            alpha = jnp.exp2(old - new)
            m_s[n] = new
            l_s[n] = l_s[n] * alpha + jnp.sum(w, axis=0, keepdims=True)
            a_buf[buf] = alpha
            p_buf[buf] = w.astype(bf16)

        def gather(t, buf):
            n, p = unpack(steps, kind, t)
            acc[n] = acc[n] * a_buf[buf] + nn(lanes_at(vt, p), p_buf[buf])

        for buf in (2, 3):
            p_buf[buf] = jnp.zeros((256, 256), bf16)
            a_buf[buf] = jnp.ones((1, 256), f32)
        walk(steps[kind, LIST - 1], score, soften, gather)

    run(0)
    run(1)

    @pl.loop(0, QT, unroll=4)
    def _(n):
        o = acc[n]
        ot_ref[n] = o
        st_ref[n, 0:1, :] = m_s[n]
        st_ref[n, 1:2, :] = l_s[n]


def delta_kernel(st_ref, ot_ref, do0_ref, do1_ref, do2_ref, do3_ref, out_ref):
    refs = (do0_ref, do1_ref, do2_ref, do3_ref)

    @pl.loop(0, QT, unroll=4)
    def _(n):
        total = st_ref[n, 1:2, :]
        some = total > 0.0
        dots = jnp.sum(head_tile(refs, n).T.astype(f32) * ot_ref[n], axis=0, keepdims=True)
        out_ref[n, 0:1, :] = jnp.where(some, st_ref[n, 0:1, :] + jnp.log2(total), NEG)
        out_ref[n, 1:2, :] = jnp.where(some, dots / jnp.where(some, total, 1.0), 0.0)


def scale_kernel(st0_ref, st1_ref, st2_ref, st3_ref, st_ref, ot_ref, stat_ref, *out_refs):
    refs = (st0_ref, st1_ref, st2_ref, st3_ref)

    @pl.loop(0, QT, unroll=4)
    def _(n):
        parts = [refs[0][n]] + [pltpu.roll(refs[k][n], 64 * k, 1) for k in (1, 2, 3)]
        top = jnp.maximum(jnp.maximum(parts[0][0:1], parts[1][0:1]), jnp.maximum(parts[2][0:1], parts[3][0:1]))
        share = [jnp.exp2(part[0:1] - top) for part in parts]
        total = share[0] + share[1] + share[2] + share[3]
        lse = top + jnp.log2(total)
        stat_ref[n, 0:1, :] = lse
        stat_ref[n, 1:2, :] = sum(w * part[1:2] for w, part in zip(share, parts)) / total
        ob = (ot_ref[n] * jnp.exp2(st_ref[n, 0:1, :] - lse)).astype(bf16).T
        for h in range(4):
            out_refs[h][:, n] = ob[h * 64:(h + 1) * 64].reshape(4, 16, HD)
    stat_ref[QT, 0:1, :] = jnp.full((1, 256), -NEG, f32)
    stat_ref[QT, 1:2, :] = jnp.zeros((1, 256), f32)


def bwd_kernel(steps, pos_ref, kpos_ref, stat_ref, own_ref, oth_ref, do0_ref, do1_ref, do2_ref, do3_ref, kt, out_ref,
               oth_out_ref, dq, dk, dv, p_buf, ds_buf):
    do_refs = (do0_ref, do1_ref, do2_ref, do3_ref)

    dq[...] = jnp.zeros_like(dq)
    dk[...] = jnp.zeros_like(dk)
    dv[...] = jnp.zeros_like(dv)

    def run(kind):
        def soften(t, buf):
            n, p = unpack(steps, kind, t)
            s = nt(key_tile(own_ref, oth_ref, p, 0), row_tile(own_ref, n, 0)) * SC2
            if kind:
                s = mask_scores(s, n, p, pos_ref, kpos_ref, NEG)
            w = jnp.exp2(s - stat_ref[n, 0:1, :])
            dp = nt(key_tile(own_ref, oth_ref, p, HD), head_tile(do_refs, n))
            p_buf[buf] = w.astype(bf16)
            ds_buf[buf] = (w * (dp - stat_ref[n, 1:2, :])).astype(bf16)

        def gather(t, buf):
            n, p = unpack(steps, kind, t)
            ds = ds_buf[buf]
            dv[p] += nn(p_buf[buf], head_tile(do_refs, n))
            dk[p] += nn(ds, row_tile(own_ref, n, 0))
            dq[n] += nn(lanes_at(kt, p), ds)

        walk_two(steps[kind, LIST - 1], soften, gather)

    run(0)
    run(1)

    @pl.loop(0, QT, unroll=4)
    def _(n):
        qb = (dq[n] * SCALE).astype(bf16).T
        for h in range(4):
            out_ref[:, n, :, 640 + h * HD:768 + h * HD] = qb[h * 64:(h + 1) * 64].reshape(4, 16, HD)

    @pl.loop(0, KP, unroll=4)
    def _(p):
        for first, tile in ((0, (dk[p] * SCALE).astype(bf16)), (HD, dv[p].astype(bf16))):
            for h in (0, 1):
                at = 256 * h + first
                out_ref[:, p, :, at:at + HD] = tile[64 * h:64 * h + 64].reshape(4, 16, HD)
                oth_out_ref[:, p, :, at:at + HD] = tile[128 + 64 * h:192 + 64 * h].reshape(4, 16, HD)


def fwd(steps, pos, kpos, own, oth):
    return pl.pallas_call(
        fwd_kernel,
        in_specs=[SMEM] + [VMEM] * 4,
        out_specs=[VMEM, VMEM],
        scratch_shapes=[
            pltpu.VMEM((HD, KP * 256), bf16),
            pltpu.VMEM((QT + 1, 1, 256), f32), pltpu.VMEM((QT + 1, 1, 256), f32), pltpu.VMEM((QT + 1, HD, 256), f32),
            pltpu.VMEM((4, 256, 256), f32), pltpu.VMEM((4, 256, 256), bf16), pltpu.VMEM((4, 1, 256), f32),
        ],
        out_shape=[jax.ShapeDtypeStruct((QT, HD, 256), f32), jax.ShapeDtypeStruct((QT, 4, 256), f32)],
        compiler_params=pltpu.CompilerParams(vmem_limit_bytes=16 << 20),
        cost_estimate=pl.CostEstimate(flops=15 * 10 ** 9, bytes_accessed=8 << 20, transcendentals=0),
        name="fwd",
    )(steps, pos, kpos, own, oth)


def delta(st, ot, dos):
    return pl.pallas_call(
        delta_kernel, in_specs=[VMEM] * 6, out_specs=VMEM, out_shape=jax.ShapeDtypeStruct((QT, 2, 256), f32),
        compiler_params=pltpu.CompilerParams(vmem_limit_bytes=12 << 20), name="delta",
    )(st, ot, *dos)


def scale(sts, st, ot):
    return pl.pallas_call(
        scale_kernel, in_specs=[VMEM] * 6, out_specs=[VMEM] * 5,
        out_shape=[jax.ShapeDtypeStruct((QT + 1, 2, 256), f32)] + [jax.ShapeDtypeStruct((4, QT, 16, HD), bf16)] * 4,
        compiler_params=pltpu.CompilerParams(vmem_limit_bytes=12 << 20), name="scale",
    )(*sts, st, ot)


def turn_kernel(own_ref, oth_ref, kt):
    @pl.loop(0, KP, unroll=4)
    def _(p):
        kt[:, pl.ds(pl.multiple_of(p * 256, 256), 256)] = key_tile(own_ref, oth_ref, p, 0).T


def turn_keys(own, oth):
    return pl.pallas_call(
        turn_kernel, in_specs=[VMEM] * 2, out_specs=VMEM, out_shape=jax.ShapeDtypeStruct((HD, KP * 256), bf16),
        cost_estimate=pl.CostEstimate(flops=10 ** 9, bytes_accessed=2 << 20, transcendentals=0),
        compiler_params=pltpu.CompilerParams(vmem_limit_bytes=12 << 20), name="turn_keys",
    )(own, oth)


def bwd(steps, pos, kpos, stat, own, oth, dos, kt):
    return pl.pallas_call(
        bwd_kernel,
        in_specs=[SMEM] + [VMEM] * 10,
        out_specs=[VMEM] * 2,
        scratch_shapes=[
            pltpu.VMEM((QT + 1, HD, 256), f32), pltpu.VMEM((KP, 256, HD), f32), pltpu.VMEM((KP, 256, HD), f32),
            pltpu.VMEM((8, 256, 256), bf16), pltpu.VMEM((8, 256, 256), bf16),
        ],
        out_shape=[jax.ShapeDtypeStruct((4, QT, 16, WIDE), bf16), jax.ShapeDtypeStruct((4, KP, 16, 512), bf16)],
        compiler_params=pltpu.CompilerParams(vmem_limit_bytes=24 << 20),
        cost_estimate=pl.CostEstimate(flops=25 * 10 ** 9, bytes_accessed=8 << 20, transcendentals=0),
        name="bwd",
    )(steps, pos, kpos, stat, own, oth, *dos, kt)


def pack_kernel(q_hbm, k_hbm, v_hbm, do_hbm, out_hbm, q_ref, k_ref, v_ref, do_ref, out_ref, in_sem, out_sem):
    loads = [pltpu.make_async_copy(src, dst, in_sem.at[i])
             for i, (src, dst) in enumerate(((q_hbm, q_ref), (k_hbm, k_ref), (v_hbm, v_ref), (do_hbm, do_ref)))]
    for load in loads:
        load.start()
    for load in loads:
        load.wait()
    stores = []
    for j in range(4):
        for u in range(8):
            for g in range(2):
                at = u * 2 + g
                tokens = slice(16 * u, 16 * u + 16)
                for r in range(4):
                    head = 512 * g + HD * ((j - r) % 4)
                    out_ref[j, at, :, r * HD:r * HD + HD] = q_ref[tokens, head:head + HD]
                head = 512 * g + HD * j
                out_ref[j, at, :, 1024:1152] = do_ref[tokens, head:head + HD]
                for h in (0, 1):
                    rows = slice(32 * j + 16 * h, 32 * j + 16 * h + 16)
                    out_ref[j, at, :, 512 + 256 * h:640 + 256 * h] = k_ref[rows, HD * g:HD * g + HD]
                    out_ref[j, at, :, 640 + 256 * h:768 + 256 * h] = v_ref[rows, HD * g:HD * g + HD]
        stores.append(pltpu.make_async_copy(out_ref.at[j], out_hbm.at[j], out_sem.at[j]))
        stores[-1].start()
    for store in stores:
        store.wait()


def pack(q, k, v, do):
    any_spec = pl.BlockSpec(memory_space=pltpu.HBM)
    return pl.pallas_call(
        pack_kernel, in_specs=[any_spec] * 4, out_specs=any_spec,
        out_shape=jax.ShapeDtypeStruct((4, 16, 16, WIDE), bf16),
        scratch_shapes=[pltpu.VMEM((128, 1024), bf16), pltpu.VMEM((128, 256), bf16), pltpu.VMEM((128, 256), bf16),
                        pltpu.VMEM((128, 1024), bf16), pltpu.VMEM((4, 16, 16, WIDE), bf16), pltpu.SemaphoreType.DMA((4,)), pltpu.SemaphoreType.DMA((4,))],
        compiler_params=pltpu.CompilerParams(vmem_limit_bytes=60 << 20), name="pack",
    )(q, k, v, do)


def gather_kernel(oth_ref, o0_ref, o1_ref, o2_ref, o3_ref, out_ref, sum_ref):
    out_ref[...] = oth_ref[...]
    total = o0_ref[...].astype(f32) + o1_ref[...].astype(f32) + o2_ref[...].astype(f32) + o3_ref[...].astype(f32)
    sum_ref[...] = total.astype(bf16)


def gather_parts(oth, heads):
    return pl.pallas_call(
        gather_kernel, in_specs=[VMEM] * 5, out_specs=[VMEM] * 2,
        out_shape=[jax.ShapeDtypeStruct(oth.shape, bf16), jax.ShapeDtypeStruct(heads[0].shape, bf16)],
        compiler_params=pltpu.CompilerParams(vmem_limit_bytes=12 << 20), name="gather_parts",
    )(oth, *heads)


def add_kernel(own_ref, other_ref, head_ref, out_ref):
    out_ref[..., :512] = (own_ref[..., :512].astype(f32) + other_ref[...].astype(f32)).astype(bf16)
    out_ref[..., 512:] = head_ref[...]


def add_parts(out, other, head):
    block = lambda columns: pl.BlockSpec((1, KP, 16, columns), lambda i: (i, 0, 0, 0))
    return pl.pallas_call(
        add_kernel, grid=(4,), in_specs=[block(640), block(512), block(HD)], out_specs=block(640),
        out_shape=jax.ShapeDtypeStruct(out.shape, bf16), input_output_aliases={0: 0},
        compiler_params=pltpu.CompilerParams(vmem_limit_bytes=12 << 20), name="add_parts",
    )(out, other, head)


def sum_kernel(in_ref, at_ref, qg_ref, kg_ref, vg_ref):
    for u in range(8):
        for g in range(2):
            rows = slice(16 * u, 16 * u + 16)
            for h in range(4):
                cols = slice(512 * g + HD * h, 512 * g + HD * h + HD)
                at_ref[rows, cols] = in_ref[h * 16 + u * 2 + g, :, 512:640]
                first = [640 + HD * ((j - h) % 4) for j in range(4)]
                parts = [in_ref[j * 16 + u * 2 + g, :, first[j]:first[j] + HD].astype(f32) for j in range(4)]
                qg_ref[rows, cols] = (parts[0] + parts[1] + parts[2] + parts[3]).astype(bf16)
    for j in range(4):
        for g in range(2):
            for h in (0, 1):
                rows, cols = slice(32 * j + 16 * h, 32 * j + 16 * h + 16), slice(HD * g, HD * g + HD)
                both = sum(in_ref[j * 16 + u * 2 + g, :, 256 * h:256 * h + 256].astype(f32) for u in range(8))
                kg_ref[rows, cols] = both[:, :HD].astype(bf16)
                vg_ref[rows, cols] = both[:, HD:].astype(bf16)


def sum_pieces(pieces):
    big, small = jax.ShapeDtypeStruct((128, 1024), bf16), jax.ShapeDtypeStruct((128, 256), bf16)
    return pl.pallas_call(
        sum_kernel, in_specs=[VMEM], out_specs=[VMEM] * 4, out_shape=[big, big, small, small],
        compiler_params=pltpu.CompilerParams(vmem_limit_bytes=12 << 20), name="sum_pieces",
    )(pieces)


def make_plan(lengths, core, u, j):
    n = jnp.arange(QT + 1, dtype=i32)[:, None, None]
    x = jnp.arange(4, dtype=i32)[None, :, None]
    t = jnp.arange(16, dtype=i32)[None, None, :]
    pos = (512 * (2 * n + core) + 128 * x + 16 * u + t).reshape(QT + 1, 64)
    docs = jnp.arange(lengths.shape[0])
    ends = jnp.sum(jnp.where(docs[:, None] <= docs[None, :], lengths[:, None], 0), axis=0)
    start = jnp.sum(jnp.where(ends[None, None, :] <= pos[:, :, None], lengths, 0), axis=-1)
    rows = jnp.stack([jnp.tile(pos, (1, 4)), jnp.tile(start, (1, 4))], axis=1).astype(i32)
    low = (start[:QT, 0] // 1024)[None, :]
    plain_low = ((start[:QT, -1] + 1023) // 1024)[None, :]
    d = jnp.arange(KP, dtype=i32)[:, None]
    m = jnp.arange(QT, dtype=i32)[None, :]
    live = (m - d >= 0) & (m - d >= low)
    plain = live & (d > 0) & (m - d >= plain_low)
    code = (m * 256 + m - d).reshape(1, QT * KP)
    order = jnp.arange(QT * KP, dtype=i32)
    earlier = order[:, None] < order[None, :]
    at = jnp.arange(LIST, dtype=i32)[:, None]

    def ranks(mask):
        return jnp.sum((earlier & mask.reshape(QT * KP, 1)).astype(i32), axis=0, keepdims=True)

    def compact(mask, rank):
        mask = mask.reshape(1, QT * KP)
        listed = QT * 256 + jnp.sum(jnp.where(mask & (rank == at), code - QT * 256, 0), axis=1)
        return jnp.where(at[:, 0] == LIST - 1, jnp.sum(mask.astype(i32)), listed)

    rank = ranks(plain)
    plain = plain & (rank.reshape(KP, QT) < jnp.sum(plain.astype(i32)) // TRIP * TRIP)
    edge = live & ~plain
    steps = jnp.stack([compact(plain, rank), compact(edge, ranks(edge))]).astype(i32)
    r = jnp.arange(256, dtype=i32)
    parity = jnp.where(r < 128, core, 1 - core)
    kpos = 512 * parity + 128 * (r % 64 // 16) + 32 * j + 16 * (r // 64 % 2) + r % 16
    return steps, rows, jnp.broadcast_to(kpos[:, None], (256, 128)).astype(i32)


PLANE = ("head", "inner", "zl")


def on_device(query_rows, key_rows, value_rows, out_grad, lengths):
    j, u, core = (lax.axis_index(name) for name in ("head", "inner", "core"))
    swap = [(0, 1), (1, 0)]
    steps, pos, kpos = make_plan(lengths, core, u, j)
    pieces = pack(query_rows.reshape(128, 1024), key_rows.reshape(128, 256), value_rows.reshape(128, 256),
                  out_grad.reshape(128, 1024))
    own = lax.all_to_all(pieces.reshape(64, 16, WIDE), PLANE, 0, 0, tiled=True).reshape(4, QT, 16, WIDE)
    own, steps, pos, kpos = lax.optimization_barrier((own, steps, pos, kpos))
    oth = lax.ppermute(own[..., 512:1024], "core", swap)

    def along(x, k):
        return lax.ppermute(x, "head", [(i, (i + k) % 4) for i in range(4)])

    do = own[..., 1024:]
    dos = [do] + [along(do, k) for k in (1, 2, 3)]
    ot, st = fwd(steps, pos, kpos, own, oth)
    part = delta(st, ot, dos)
    stat, *heads = scale([part] + [along(part, k) for k in (1, 2, 3)], st, ot)
    heads = heads[:1] + [along(heads[k], -k) for k in (1, 2, 3)]
    out, oth_out = bwd(steps, pos, kpos, stat, own, oth, dos, turn_keys(own, oth))
    oth_out, head = gather_parts(oth_out, heads)
    out = add_parts(out, lax.ppermute(oth_out, "core", swap), head)
    out = lax.all_to_all(out.reshape(64, 16, WIDE), PLANE, 0, 0, tiled=True)
    attended, query_grad, key_grad, value_grad = sum_pieces(out)
    return (attended.reshape(1, 1, 128, 1024), query_grad.reshape(1, 1, 128, 1024),
            key_grad.reshape(1, 1, 128, 256), value_grad.reshape(1, 1, 128, 256))


def solution(mesh):
    finer = Mesh(mesh.devices.reshape(4, 8, 2, 2), ("head", "inner", "zl", "core"))
    placed = P(("inner", "zl", "core"), "head", None, None)
    return jax.shard_map(
        on_device,
        mesh=finer,
        in_specs=(placed, placed, placed, placed, P()),
        out_specs=(placed, placed, placed, placed),
        check_vma=False,
    )
```

```python
import jax
import jax.numpy as jnp
from jax import lax
from jax.experimental import pallas as pl
from jax.experimental.pallas import tpu as pltpu
from jax.sharding import Mesh
from jax.sharding import PartitionSpec as P

HD = 128
NEG = -1.0e30
SCALE = HD ** -0.5
SC2 = SCALE * 1.4426950408889634
QT = 16
KP = 16
LIST = 160
TRIP = 8
WIDE = 1152
bf16, f32, i32 = jnp.bfloat16, jnp.float32, jnp.int32
VMEM = pl.BlockSpec(memory_space=pltpu.VMEM)
SMEM = pl.BlockSpec(memory_space=pltpu.SMEM)


def nt(a, b):
    return lax.dot_general(a, b, (((1,), (1,)), ((), ())), preferred_element_type=f32)


def nn(a, b):
    return jnp.dot(a, b, preferred_element_type=f32)


def row_tile(ref, n, first):
    n = jnp.minimum(n, QT - 1)
    return jnp.concatenate([ref[:, n, :, first + h * HD:first + (h + 1) * HD].reshape(64, HD) for h in range(4)], axis=0)


def head_tile(refs, n):
    n = jnp.minimum(n, QT - 1)
    return jnp.concatenate([ref[:, n].reshape(64, HD) for ref in refs], axis=0)


def key_tile(own_ref, oth_ref, p, first):
    parts = [own_ref[:, p, :, 512 + 256 * h + first:512 + 256 * h + first + HD].reshape(64, HD) for h in (0, 1)]
    parts += [oth_ref[:, p, :, 256 * h + first:256 * h + first + HD].reshape(64, HD) for h in (0, 1)]
    return jnp.concatenate(parts, axis=0)


def unpack(steps, kind, t):
    word = steps[kind, t]
    return lax.shift_right_logical(word, 8), word & 255


def mask_scores(s, n, p, pos_ref, kpos_ref, low):
    kpos = kpos_ref[...]
    kpos = jnp.concatenate([kpos, kpos], axis=1)
    first = p * 1024
    seen = (kpos <= pos_ref[n, 0:1, :] - first) & (kpos >= pos_ref[n, 1:2, :] - first)
    return jnp.where(seen, s, low)


def lanes_at(ref, p):
    return ref[:, pl.ds(pl.multiple_of(p * 256, 256), 256)]


def walk(count, score, soften, gather):
    score(0, 0)
    score(1, 1)
    trips = lax.shift_right_logical(count + 3, 2)

    @pl.loop(0, trips)
    def _(i):
        t = 4 * i
        for half in (0, 2):
            cur, nxt = half, 2 - half
            for k in (0, 1):
                score(t + half + 2 + k, nxt + k)
                soften(t + half + k, cur + k)
                gather(jnp.maximum(t + half - 2 + k, 0), nxt + k)

    last = jnp.maximum(4 * trips - 2, 0)
    gather(last, 2)
    gather(last + 1, 3)


def walk_two(count, soften, gather):
    for k in range(4):
        soften(k, k)

    @pl.loop(0, lax.shift_right_logical(count + 7, 3))
    def _(i):
        t = 8 * i
        for half in (0, 4):
            cur, nxt = half, 4 - half
            for k in range(4):
                gather(t + half + k, cur + k)
                soften(t + half + 4 + k, nxt + k)


def fwd_kernel(steps, pos_ref, kpos_ref, own_ref, oth_ref, acc, st_ref, vt, m_s, l_s, s_buf, p_buf, a_buf):
    @pl.loop(0, KP, unroll=4)
    def _(p):
        vt[:, pl.ds(pl.multiple_of(p * 256, 256), 256)] = key_tile(own_ref, oth_ref, p, HD).T

    m_s[...] = jnp.full_like(m_s, NEG)
    l_s[...] = jnp.zeros_like(l_s)
    acc[...] = jnp.zeros_like(acc)

    def run(kind):
        def score(t, buf):
            n, p = unpack(steps, kind, t)
            s = nt(key_tile(own_ref, oth_ref, p, 0), row_tile(own_ref, n, 0)) * SC2
            s_buf[buf] = mask_scores(s, n, p, pos_ref, kpos_ref, 2 * NEG) if kind else s

        def soften(t, buf):
            n, _ = unpack(steps, kind, t)
            s = s_buf[buf]
            old = m_s[n]
            new = jnp.maximum(old, jnp.max(s, axis=0, keepdims=True))
            w = jnp.exp2(s - new)
            alpha = jnp.exp2(old - new)
            m_s[n] = new
            l_s[n] = l_s[n] * alpha + jnp.sum(w, axis=0, keepdims=True)
            a_buf[buf] = alpha
            p_buf[buf] = w.astype(bf16)

        def gather(t, buf):
            n, p = unpack(steps, kind, t)
            acc[n] = acc[n] * a_buf[buf] + nn(lanes_at(vt, p), p_buf[buf])

        for buf in (2, 3):
            p_buf[buf] = jnp.zeros((256, 256), bf16)
            a_buf[buf] = jnp.ones((1, 256), f32)
        walk(steps[kind, LIST - 1], score, soften, gather)

    run(0)
    run(1)

    @pl.loop(0, QT, unroll=4)
    def _(n):
        st_ref[n, 0:1, :] = m_s[n]
        st_ref[n, 1:2, :] = l_s[n]


def delta_kernel(st_ref, ot_ref, do0_ref, do1_ref, do2_ref, do3_ref, out_ref):
    refs = (do0_ref, do1_ref, do2_ref, do3_ref)

    @pl.loop(0, QT, unroll=4)
    def _(n):
        total = st_ref[n, 1:2, :]
        some = total > 0.0
        dots = jnp.sum(head_tile(refs, n).T.astype(f32) * ot_ref[n], axis=0, keepdims=True)
        out_ref[n, 0:1, :] = jnp.where(some, st_ref[n, 0:1, :] + jnp.log2(total), NEG)
        out_ref[n, 1:2, :] = jnp.where(some, dots / jnp.where(some, total, 1.0), 0.0)


def scale_kernel(st0_ref, st1_ref, st2_ref, st3_ref, st_ref, ot_ref, stat_ref, *out_refs):
    refs = (st0_ref, st1_ref, st2_ref, st3_ref)

    @pl.loop(0, QT, unroll=4)
    def _(n):
        parts = [refs[0][n]] + [pltpu.roll(refs[k][n], 64 * k, 1) for k in (1, 2, 3)]
        top = jnp.maximum(jnp.maximum(parts[0][0:1], parts[1][0:1]), jnp.maximum(parts[2][0:1], parts[3][0:1]))
        share = [jnp.exp2(part[0:1] - top) for part in parts]
        total = share[0] + share[1] + share[2] + share[3]
        lse = top + jnp.log2(total)
        stat_ref[n, 0:1, :] = lse
        stat_ref[n, 1:2, :] = sum(w * part[1:2] for w, part in zip(share, parts)) / total
        ob = (ot_ref[n] * jnp.exp2(st_ref[n, 0:1, :] - lse)).astype(bf16).T
        for h in range(4):
            out_refs[h][:, n] = ob[h * 64:(h + 1) * 64].reshape(4, 16, HD)
    stat_ref[QT, 0:1, :] = jnp.full((1, 256), -NEG, f32)
    stat_ref[QT, 1:2, :] = jnp.zeros((1, 256), f32)


def bwd_kernel(steps, pos_ref, kpos_ref, stat_ref, own_ref, oth_ref, do0_ref, do1_ref, do2_ref, do3_ref, kt, out_ref,
               oth_out_ref, dq, dk, dv, p_buf, ds_buf):
    do_refs = (do0_ref, do1_ref, do2_ref, do3_ref)

    dq[...] = jnp.zeros_like(dq)
    dk[...] = jnp.zeros_like(dk)
    dv[...] = jnp.zeros_like(dv)

    def run(kind):
        def soften(t, buf):
            n, p = unpack(steps, kind, t)
            s = nt(key_tile(own_ref, oth_ref, p, 0), row_tile(own_ref, n, 0)) * SC2
            if kind:
                s = mask_scores(s, n, p, pos_ref, kpos_ref, NEG)
            w = jnp.exp2(s - stat_ref[n, 0:1, :])
            dp = nt(key_tile(own_ref, oth_ref, p, HD), head_tile(do_refs, n))
            p_buf[buf] = w.astype(bf16)
            ds_buf[buf] = (w * (dp - stat_ref[n, 1:2, :])).astype(bf16)

        def gather(t, buf):
            n, p = unpack(steps, kind, t)
            ds = ds_buf[buf]
            dv[p] += nn(p_buf[buf], head_tile(do_refs, n))
            dk[p] += nn(ds, row_tile(own_ref, n, 0))
            dq[n] += nn(lanes_at(kt, p), ds)

        walk_two(steps[kind, LIST - 1], soften, gather)

    run(0)
    run(1)

    @pl.loop(0, QT, unroll=4)
    def _(n):
        qb = (dq[n] * SCALE).astype(bf16).T
        for h in range(4):
            out_ref[:, n, :, 640 + h * HD:768 + h * HD] = qb[h * 64:(h + 1) * 64].reshape(4, 16, HD)

    @pl.loop(0, KP, unroll=4)
    def _(p):
        for first, tile in ((0, (dk[p] * SCALE).astype(bf16)), (HD, dv[p].astype(bf16))):
            for h in (0, 1):
                at = 256 * h + first
                out_ref[:, p, :, at:at + HD] = tile[64 * h:64 * h + 64].reshape(4, 16, HD)
                oth_out_ref[:, p, :, at:at + HD] = tile[128 + 64 * h:192 + 64 * h].reshape(4, 16, HD)


def fwd(steps, pos, kpos, own, oth):
    return pl.pallas_call(
        fwd_kernel,
        in_specs=[SMEM] + [VMEM] * 4,
        out_specs=[VMEM, VMEM],
        scratch_shapes=[
            pltpu.VMEM((HD, KP * 256), bf16),
            pltpu.VMEM((QT + 1, 1, 256), f32), pltpu.VMEM((QT + 1, 1, 256), f32),
            pltpu.VMEM((4, 256, 256), f32), pltpu.VMEM((4, 256, 256), bf16), pltpu.VMEM((4, 1, 256), f32),
        ],
        out_shape=[jax.ShapeDtypeStruct((QT + 1, HD, 256), f32), jax.ShapeDtypeStruct((QT, 4, 256), f32)],
        compiler_params=pltpu.CompilerParams(vmem_limit_bytes=16 << 20),
        cost_estimate=pl.CostEstimate(flops=15 * 10 ** 9, bytes_accessed=8 << 20, transcendentals=0),
        name="fwd",
    )(steps, pos, kpos, own, oth)


def delta(st, ot, dos):
    return pl.pallas_call(
        delta_kernel, in_specs=[VMEM] * 6, out_specs=VMEM, out_shape=jax.ShapeDtypeStruct((QT, 2, 256), f32),
        compiler_params=pltpu.CompilerParams(vmem_limit_bytes=12 << 20), name="delta",
    )(st, ot, *dos)


def scale(sts, st, ot):
    return pl.pallas_call(
        scale_kernel, in_specs=[VMEM] * 6, out_specs=[VMEM] * 5,
        out_shape=[jax.ShapeDtypeStruct((QT + 1, 2, 256), f32)] + [jax.ShapeDtypeStruct((4, QT, 16, HD), bf16)] * 4,
        compiler_params=pltpu.CompilerParams(vmem_limit_bytes=12 << 20), name="scale",
    )(*sts, st, ot)


def turn_kernel(own_ref, oth_ref, kt):
    @pl.loop(0, KP, unroll=4)
    def _(p):
        kt[:, pl.ds(pl.multiple_of(p * 256, 256), 256)] = key_tile(own_ref, oth_ref, p, 0).T


def turn_keys(own, oth):
    return pl.pallas_call(
        turn_kernel, in_specs=[VMEM] * 2, out_specs=VMEM, out_shape=jax.ShapeDtypeStruct((HD, KP * 256), bf16),
        cost_estimate=pl.CostEstimate(flops=10 ** 9, bytes_accessed=2 << 20, transcendentals=0),
        compiler_params=pltpu.CompilerParams(vmem_limit_bytes=12 << 20), name="turn_keys",
    )(own, oth)


def bwd(steps, pos, kpos, stat, own, oth, dos, kt):
    return pl.pallas_call(
        bwd_kernel,
        in_specs=[SMEM] + [VMEM] * 10,
        out_specs=[VMEM] * 2,
        scratch_shapes=[
            pltpu.VMEM((QT + 1, HD, 256), f32), pltpu.VMEM((KP, 256, HD), f32), pltpu.VMEM((KP, 256, HD), f32),
            pltpu.VMEM((8, 256, 256), bf16), pltpu.VMEM((8, 256, 256), bf16),
        ],
        out_shape=[jax.ShapeDtypeStruct((4, QT, 16, WIDE), bf16), jax.ShapeDtypeStruct((4, KP, 16, 512), bf16)],
        compiler_params=pltpu.CompilerParams(vmem_limit_bytes=24 << 20),
        cost_estimate=pl.CostEstimate(flops=25 * 10 ** 9, bytes_accessed=8 << 20, transcendentals=0),
        name="bwd",
    )(steps, pos, kpos, stat, own, oth, *dos, kt)


def pack_kernel(q_hbm, k_hbm, v_hbm, do_hbm, out_hbm, q_ref, k_ref, v_ref, do_ref, out_ref, in_sem, out_sem):
    loads = [pltpu.make_async_copy(src, dst, in_sem.at[i])
             for i, (src, dst) in enumerate(((q_hbm, q_ref), (k_hbm, k_ref), (v_hbm, v_ref), (do_hbm, do_ref)))]
    for load in loads:
        load.start()
    for load in loads:
        load.wait()
    stores = []
    for j in range(4):
        for u in range(8):
            for g in range(2):
                at = u * 2 + g
                tokens = slice(16 * u, 16 * u + 16)
                for r in range(4):
                    head = 512 * g + HD * ((j - r) % 4)
                    out_ref[j, at, :, r * HD:r * HD + HD] = q_ref[tokens, head:head + HD]
                head = 512 * g + HD * j
                out_ref[j, at, :, 1024:1152] = do_ref[tokens, head:head + HD]
                for h in (0, 1):
                    rows = slice(32 * j + 16 * h, 32 * j + 16 * h + 16)
                    out_ref[j, at, :, 512 + 256 * h:640 + 256 * h] = k_ref[rows, HD * g:HD * g + HD]
                    out_ref[j, at, :, 640 + 256 * h:768 + 256 * h] = v_ref[rows, HD * g:HD * g + HD]
        stores.append(pltpu.make_async_copy(out_ref.at[j], out_hbm.at[j], out_sem.at[j]))
        stores[-1].start()
    for store in stores:
        store.wait()


def pack(q, k, v, do):
    any_spec = pl.BlockSpec(memory_space=pltpu.HBM)
    return pl.pallas_call(
        pack_kernel, in_specs=[any_spec] * 4, out_specs=any_spec,
        out_shape=jax.ShapeDtypeStruct((4, 16, 16, WIDE), bf16),
        scratch_shapes=[pltpu.VMEM((128, 1024), bf16), pltpu.VMEM((128, 256), bf16), pltpu.VMEM((128, 256), bf16),
                        pltpu.VMEM((128, 1024), bf16), pltpu.VMEM((4, 16, 16, WIDE), bf16), pltpu.SemaphoreType.DMA((4,)), pltpu.SemaphoreType.DMA((4,))],
        compiler_params=pltpu.CompilerParams(vmem_limit_bytes=60 << 20), name="pack",
    )(q, k, v, do)


def gather_kernel(oth_ref, o0_ref, o1_ref, o2_ref, o3_ref, out_ref, sum_ref):
    out_ref[...] = oth_ref[...]
    total = o0_ref[...].astype(f32) + o1_ref[...].astype(f32) + o2_ref[...].astype(f32) + o3_ref[...].astype(f32)
    sum_ref[...] = total.astype(bf16)


def gather_parts(oth, heads):
    return pl.pallas_call(
        gather_kernel, in_specs=[VMEM] * 5, out_specs=[VMEM] * 2,
        out_shape=[jax.ShapeDtypeStruct(oth.shape, bf16), jax.ShapeDtypeStruct(heads[0].shape, bf16)],
        compiler_params=pltpu.CompilerParams(vmem_limit_bytes=12 << 20), name="gather_parts",
    )(oth, *heads)


def add_kernel(own_ref, other_ref, head_ref, out_ref):
    out_ref[..., :512] = (own_ref[..., :512].astype(f32) + other_ref[...].astype(f32)).astype(bf16)
    out_ref[..., 512:] = head_ref[...]


def add_parts(out, other, head):
    block = lambda columns: pl.BlockSpec((1, KP, 16, columns), lambda i: (i, 0, 0, 0))
    return pl.pallas_call(
        add_kernel, grid=(4,), in_specs=[block(640), block(512), block(HD)], out_specs=block(640),
        out_shape=jax.ShapeDtypeStruct(out.shape, bf16), input_output_aliases={0: 0},
        compiler_params=pltpu.CompilerParams(vmem_limit_bytes=12 << 20), name="add_parts",
    )(out, other, head)


def sum_kernel(in_ref, at_ref, qg_ref, kg_ref, vg_ref):
    for u in range(8):
        for g in range(2):
            rows = slice(16 * u, 16 * u + 16)
            for h in range(4):
                cols = slice(512 * g + HD * h, 512 * g + HD * h + HD)
                at_ref[rows, cols] = in_ref[h * 16 + u * 2 + g, :, 512:640]
                first = [640 + HD * ((j - h) % 4) for j in range(4)]
                parts = [in_ref[j * 16 + u * 2 + g, :, first[j]:first[j] + HD].astype(f32) for j in range(4)]
                qg_ref[rows, cols] = (parts[0] + parts[1] + parts[2] + parts[3]).astype(bf16)
    for j in range(4):
        for g in range(2):
            for h in (0, 1):
                rows, cols = slice(32 * j + 16 * h, 32 * j + 16 * h + 16), slice(HD * g, HD * g + HD)
                both = sum(in_ref[j * 16 + u * 2 + g, :, 256 * h:256 * h + 256].astype(f32) for u in range(8))
                kg_ref[rows, cols] = both[:, :HD].astype(bf16)
                vg_ref[rows, cols] = both[:, HD:].astype(bf16)


def sum_pieces(pieces):
    big, small = jax.ShapeDtypeStruct((128, 1024), bf16), jax.ShapeDtypeStruct((128, 256), bf16)
    return pl.pallas_call(
        sum_kernel, in_specs=[VMEM], out_specs=[VMEM] * 4, out_shape=[big, big, small, small],
        compiler_params=pltpu.CompilerParams(vmem_limit_bytes=12 << 20), name="sum_pieces",
    )(pieces)


def make_plan(lengths, core, u, j):
    n = jnp.arange(QT + 1, dtype=i32)[:, None, None]
    x = jnp.arange(4, dtype=i32)[None, :, None]
    t = jnp.arange(16, dtype=i32)[None, None, :]
    pos = (512 * (2 * n + core) + 128 * x + 16 * u + t).reshape(QT + 1, 64)
    docs = jnp.arange(lengths.shape[0])
    ends = jnp.sum(jnp.where(docs[:, None] <= docs[None, :], lengths[:, None], 0), axis=0)
    start = jnp.sum(jnp.where(ends[None, None, :] <= pos[:, :, None], lengths, 0), axis=-1)
    rows = jnp.stack([jnp.tile(pos, (1, 4)), jnp.tile(start, (1, 4))], axis=1).astype(i32)
    low = (start[:QT, 0] // 1024)[None, :]
    plain_low = ((start[:QT, -1] + 1023) // 1024)[None, :]
    d = jnp.arange(KP, dtype=i32)[:, None]
    m = jnp.arange(QT, dtype=i32)[None, :]
    live = (m - d >= 0) & (m - d >= low)
    plain = live & (d > 0) & (m - d >= plain_low)
    code = (m * 256 + m - d).reshape(1, QT * KP)
    order = jnp.arange(QT * KP, dtype=i32)
    earlier = order[:, None] < order[None, :]
    at = jnp.arange(LIST, dtype=i32)[:, None]

    def ranks(mask):
        return jnp.sum((earlier & mask.reshape(QT * KP, 1)).astype(i32), axis=0, keepdims=True)

    def compact(mask, rank):
        mask = mask.reshape(1, QT * KP)
        listed = QT * 256 + jnp.sum(jnp.where(mask & (rank == at), code - QT * 256, 0), axis=1)
        return jnp.where(at[:, 0] == LIST - 1, jnp.sum(mask.astype(i32)), listed)

    rank = ranks(plain)
    plain = plain & (rank.reshape(KP, QT) < jnp.sum(plain.astype(i32)) // TRIP * TRIP)
    edge = live & ~plain
    steps = jnp.stack([compact(plain, rank), compact(edge, ranks(edge))]).astype(i32)
    r = jnp.arange(256, dtype=i32)
    parity = jnp.where(r < 128, core, 1 - core)
    kpos = 512 * parity + 128 * (r % 64 // 16) + 32 * j + 16 * (r // 64 % 2) + r % 16
    return steps, rows, jnp.broadcast_to(kpos[:, None], (256, 128)).astype(i32)


PLANE = ("head", "inner", "zl")


def on_device(query_rows, key_rows, value_rows, out_grad, lengths):
    j, u, core = (lax.axis_index(name) for name in ("head", "inner", "core"))
    swap = [(0, 1), (1, 0)]
    steps, pos, kpos = make_plan(lengths, core, u, j)
    pieces = pack(query_rows.reshape(128, 1024), key_rows.reshape(128, 256), value_rows.reshape(128, 256),
                  out_grad.reshape(128, 1024))
    own = lax.all_to_all(pieces.reshape(64, 16, WIDE), PLANE, 0, 0, tiled=True).reshape(4, QT, 16, WIDE)
    own, steps, pos, kpos = lax.optimization_barrier((own, steps, pos, kpos))
    oth = lax.ppermute(own[..., 512:1024], "core", swap)

    def along(x, k):
        return lax.ppermute(x, "head", [(i, (i + k) % 4) for i in range(4)])

    def spread(arrays, sign):
        moved = {k: along(arrays[k], sign * k) for k in (3, 1, 2)}
        return [arrays[0]] + [moved[k] for k in (1, 2, 3)]

    do = own[..., 1024:]
    dos = spread([do] * 4, 1)
    ot, st = fwd(steps, pos, kpos, own, oth)
    part = delta(st, ot, dos)
    stat, *heads = scale(spread([part] * 4, 1), st, ot)
    heads = spread(heads, -1)
    out, oth_out = bwd(steps, pos, kpos, stat, own, oth, dos, turn_keys(own, oth))
    oth_out, head = gather_parts(oth_out, heads)
    out = add_parts(out, lax.ppermute(oth_out, "core", swap), head)
    out = lax.all_to_all(out.reshape(64, 16, WIDE), PLANE, 0, 0, tiled=True)
    attended, query_grad, key_grad, value_grad = sum_pieces(out)
    return (attended.reshape(1, 1, 128, 1024), query_grad.reshape(1, 1, 128, 1024),
            key_grad.reshape(1, 1, 128, 256), value_grad.reshape(1, 1, 128, 256))


def solution(mesh):
    finer = Mesh(mesh.devices.reshape(4, 8, 2, 2), ("head", "inner", "zl", "core"))
    placed = P(("inner", "zl", "core"), "head", None, None)
    return jax.shard_map(
        on_device,
        mesh=finer,
        in_specs=(placed, placed, placed, placed, P()),
        out_specs=(placed, placed, placed, placed),
        check_vma=False,
    )
```

```python
import jax
import jax.numpy as jnp
from jax import lax
from jax.experimental import pallas as pl
from jax.experimental.pallas import tpu as pltpu
from jax.sharding import Mesh
from jax.sharding import PartitionSpec as P

HD = 128
NEG = -1.0e30
SCALE = HD ** -0.5
SC2 = SCALE * 1.4426950408889634
QT = 16
KP = 16
LIST = 160
TRIP = 8
WIDE = 1152
bf16, f32, i32 = jnp.bfloat16, jnp.float32, jnp.int32
VMEM = pl.BlockSpec(memory_space=pltpu.VMEM)
SMEM = pl.BlockSpec(memory_space=pltpu.SMEM)


def nt(a, b):
    return lax.dot_general(a, b, (((1,), (1,)), ((), ())), preferred_element_type=f32)


def nn(a, b):
    return jnp.dot(a, b, preferred_element_type=f32)


def row_tile(ref, n, first):
    n = jnp.minimum(n, QT - 1)
    return jnp.concatenate([ref[:, n, :, first + h * HD:first + (h + 1) * HD].reshape(64, HD) for h in range(4)], axis=0)


def head_tile(refs, n):
    n = jnp.minimum(n, QT - 1)
    return jnp.concatenate([ref[:, n].reshape(64, HD) for ref in refs], axis=0)


def key_tile(own_ref, oth_ref, p, first):
    parts = [own_ref[:, p, :, 512 + 256 * h + first:512 + 256 * h + first + HD].reshape(64, HD) for h in (0, 1)]
    parts += [oth_ref[:, p, :, 256 * h + first:256 * h + first + HD].reshape(64, HD) for h in (0, 1)]
    return jnp.concatenate(parts, axis=0)


def unpack(steps, kind, t):
    word = steps[kind, t]
    return lax.shift_right_logical(word, 8), word & 255


def mask_scores(s, n, p, pos_ref, kpos_ref, low):
    kpos = kpos_ref[...]
    kpos = jnp.concatenate([kpos, kpos], axis=1)
    first = p * 1024
    seen = (kpos <= pos_ref[n, 0:1, :] - first) & (kpos >= pos_ref[n, 1:2, :] - first)
    return jnp.where(seen, s, low)


def lanes_at(ref, p):
    return ref[:, pl.ds(pl.multiple_of(p * 256, 256), 256)]


def walk(count, score, soften, gather):
    score(0, 0)
    score(1, 1)
    trips = lax.shift_right_logical(count + 3, 2)

    @pl.loop(0, trips)
    def _(i):
        t = 4 * i
        for half in (0, 2):
            cur, nxt = half, 2 - half
            for k in (0, 1):
                score(t + half + 2 + k, nxt + k)
                soften(t + half + k, cur + k)
                gather(jnp.maximum(t + half - 2 + k, 0), nxt + k)

    last = jnp.maximum(4 * trips - 2, 0)
    gather(last, 2)
    gather(last + 1, 3)


def walk_two(count, soften, gather):
    for k in range(4):
        soften(k, k)

    @pl.loop(0, lax.shift_right_logical(count + 7, 3))
    def _(i):
        t = 8 * i
        for half in (0, 4):
            cur, nxt = half, 4 - half
            for k in range(4):
                gather(t + half + k, cur + k)
                soften(t + half + 4 + k, nxt + k)


def fwd_kernel(steps, pos_ref, kpos_ref, own_ref, oth_ref, acc, st_ref, vt, m_s, l_s, s_buf, p_buf, a_buf):
    @pl.loop(0, KP, unroll=8)
    def _(p):
        vt[:, pl.ds(pl.multiple_of(p * 256, 256), 256)] = key_tile(own_ref, oth_ref, p, HD).T

    m_s[...] = jnp.full_like(m_s, NEG)
    l_s[...] = jnp.zeros_like(l_s)
    acc[...] = jnp.zeros_like(acc)

    def run(kind):
        def score(t, buf):
            n, p = unpack(steps, kind, t)
            s = nt(key_tile(own_ref, oth_ref, p, 0), row_tile(own_ref, n, 0)) * SC2
            s_buf[buf] = mask_scores(s, n, p, pos_ref, kpos_ref, 2 * NEG) if kind else s

        def soften(t, buf):
            n, _ = unpack(steps, kind, t)
            s = s_buf[buf]
            old = m_s[n]
            new = jnp.maximum(old, jnp.max(s, axis=0, keepdims=True))
            w = jnp.exp2(s - new)
            alpha = jnp.exp2(old - new)
            m_s[n] = new
            l_s[n] = l_s[n] * alpha + jnp.sum(w, axis=0, keepdims=True)
            a_buf[buf] = alpha
            p_buf[buf] = w.astype(bf16)

        def gather(t, buf):
            n, p = unpack(steps, kind, t)
            acc[n] = acc[n] * a_buf[buf] + nn(lanes_at(vt, p), p_buf[buf])

        for buf in (2, 3):
            p_buf[buf] = jnp.zeros((256, 256), bf16)
            a_buf[buf] = jnp.ones((1, 256), f32)
        walk(steps[kind, LIST - 1], score, soften, gather)

    run(0)
    run(1)

    @pl.loop(0, QT, unroll=8)
    def _(n):
        st_ref[n, 0:1, :] = m_s[n]
        st_ref[n, 1:2, :] = l_s[n]


def delta_kernel(st_ref, ot_ref, do0_ref, do1_ref, do2_ref, do3_ref, out_ref):
    refs = (do0_ref, do1_ref, do2_ref, do3_ref)

    @pl.loop(0, QT, unroll=8)
    def _(n):
        total = st_ref[n, 1:2, :]
        some = total > 0.0
        dots = jnp.sum(head_tile(refs, n).T.astype(f32) * ot_ref[n], axis=0, keepdims=True)
        out_ref[n, 0:1, :] = jnp.where(some, st_ref[n, 0:1, :] + jnp.log2(total), NEG)
        out_ref[n, 1:2, :] = jnp.where(some, dots / jnp.where(some, total, 1.0), 0.0)


def scale_kernel(st0_ref, st1_ref, st2_ref, st3_ref, st_ref, ot_ref, stat_ref, *out_refs):
    refs = (st0_ref, st1_ref, st2_ref, st3_ref)

    @pl.loop(0, QT, unroll=8)
    def _(n):
        parts = [refs[0][n]] + [pltpu.roll(refs[k][n], 64 * k, 1) for k in (1, 2, 3)]
        top = jnp.maximum(jnp.maximum(parts[0][0:1], parts[1][0:1]), jnp.maximum(parts[2][0:1], parts[3][0:1]))
        share = [jnp.exp2(part[0:1] - top) for part in parts]
        total = share[0] + share[1] + share[2] + share[3]
        lse = top + jnp.log2(total)
        stat_ref[n, 0:1, :] = lse
        stat_ref[n, 1:2, :] = sum(w * part[1:2] for w, part in zip(share, parts)) / total
        ob = (ot_ref[n] * jnp.exp2(st_ref[n, 0:1, :] - lse)).astype(bf16).T
        for h in range(4):
            out_refs[h][:, n] = ob[h * 64:(h + 1) * 64].reshape(4, 16, HD)
    stat_ref[QT, 0:1, :] = jnp.full((1, 256), -NEG, f32)
    stat_ref[QT, 1:2, :] = jnp.zeros((1, 256), f32)


def bwd_kernel(steps, pos_ref, kpos_ref, stat_ref, own_ref, oth_ref, do0_ref, do1_ref, do2_ref, do3_ref, kt, out_ref,
               oth_out_ref, dq, dk, dv, p_buf, ds_buf):
    do_refs = (do0_ref, do1_ref, do2_ref, do3_ref)

    dq[...] = jnp.zeros_like(dq)
    dk[...] = jnp.zeros_like(dk)
    dv[...] = jnp.zeros_like(dv)

    def run(kind):
        def soften(t, buf):
            n, p = unpack(steps, kind, t)
            s = nt(key_tile(own_ref, oth_ref, p, 0), row_tile(own_ref, n, 0)) * SC2
            if kind:
                s = mask_scores(s, n, p, pos_ref, kpos_ref, NEG)
            w = jnp.exp2(s - stat_ref[n, 0:1, :])
            dp = nt(key_tile(own_ref, oth_ref, p, HD), head_tile(do_refs, n))
            p_buf[buf] = w.astype(bf16)
            ds_buf[buf] = (w * (dp - stat_ref[n, 1:2, :])).astype(bf16)

        def gather(t, buf):
            n, p = unpack(steps, kind, t)
            ds = ds_buf[buf]
            dv[p] += nn(p_buf[buf], head_tile(do_refs, n))
            dk[p] += nn(ds, row_tile(own_ref, n, 0))
            dq[n] += nn(lanes_at(kt, p), ds)

        walk_two(steps[kind, LIST - 1], soften, gather)

    run(0)
    run(1)

    @pl.loop(0, QT, unroll=8)
    def _(n):
        qb = (dq[n] * SCALE).astype(bf16).T
        for h in range(4):
            out_ref[:, n, :, 640 + h * HD:768 + h * HD] = qb[h * 64:(h + 1) * 64].reshape(4, 16, HD)

    @pl.loop(0, KP, unroll=8)
    def _(p):
        for first, tile in ((0, (dk[p] * SCALE).astype(bf16)), (HD, dv[p].astype(bf16))):
            for h in (0, 1):
                at = 256 * h + first
                out_ref[:, p, :, at:at + HD] = tile[64 * h:64 * h + 64].reshape(4, 16, HD)
                oth_out_ref[:, p, :, at:at + HD] = tile[128 + 64 * h:192 + 64 * h].reshape(4, 16, HD)


def fwd(steps, pos, kpos, own, oth):
    return pl.pallas_call(
        fwd_kernel,
        in_specs=[SMEM] + [VMEM] * 4,
        out_specs=[VMEM, VMEM],
        scratch_shapes=[
            pltpu.VMEM((HD, KP * 256), bf16),
            pltpu.VMEM((QT + 1, 1, 256), f32), pltpu.VMEM((QT + 1, 1, 256), f32),
            pltpu.VMEM((4, 256, 256), f32), pltpu.VMEM((4, 256, 256), bf16), pltpu.VMEM((4, 1, 256), f32),
        ],
        out_shape=[jax.ShapeDtypeStruct((QT + 1, HD, 256), f32), jax.ShapeDtypeStruct((QT, 4, 256), f32)],
        compiler_params=pltpu.CompilerParams(vmem_limit_bytes=16 << 20),
        cost_estimate=pl.CostEstimate(flops=15 * 10 ** 9, bytes_accessed=8 << 20, transcendentals=0),
        name="fwd",
    )(steps, pos, kpos, own, oth)


def delta(st, ot, dos):
    return pl.pallas_call(
        delta_kernel, in_specs=[VMEM] * 6, out_specs=VMEM, out_shape=jax.ShapeDtypeStruct((QT, 2, 256), f32),
        compiler_params=pltpu.CompilerParams(vmem_limit_bytes=12 << 20), name="delta",
    )(st, ot, *dos)


def scale(sts, st, ot):
    return pl.pallas_call(
        scale_kernel, in_specs=[VMEM] * 6, out_specs=[VMEM] * 5,
        out_shape=[jax.ShapeDtypeStruct((QT + 1, 2, 256), f32)] + [jax.ShapeDtypeStruct((4, QT, 16, HD), bf16)] * 4,
        compiler_params=pltpu.CompilerParams(vmem_limit_bytes=12 << 20), name="scale",
    )(*sts, st, ot)


def turn_kernel(own_ref, oth_ref, kt):
    @pl.loop(0, KP, unroll=8)
    def _(p):
        kt[:, pl.ds(pl.multiple_of(p * 256, 256), 256)] = key_tile(own_ref, oth_ref, p, 0).T


def turn_keys(own, oth):
    return pl.pallas_call(
        turn_kernel, in_specs=[VMEM] * 2, out_specs=VMEM, out_shape=jax.ShapeDtypeStruct((HD, KP * 256), bf16),
        cost_estimate=pl.CostEstimate(flops=10 ** 9, bytes_accessed=2 << 20, transcendentals=0),
        compiler_params=pltpu.CompilerParams(vmem_limit_bytes=12 << 20), name="turn_keys",
    )(own, oth)


def bwd(steps, pos, kpos, stat, own, oth, dos, kt):
    return pl.pallas_call(
        bwd_kernel,
        in_specs=[SMEM] + [VMEM] * 10,
        out_specs=[VMEM] * 2,
        scratch_shapes=[
            pltpu.VMEM((QT + 1, HD, 256), f32), pltpu.VMEM((KP, 256, HD), f32), pltpu.VMEM((KP, 256, HD), f32),
            pltpu.VMEM((8, 256, 256), bf16), pltpu.VMEM((8, 256, 256), bf16),
        ],
        out_shape=[jax.ShapeDtypeStruct((4, QT, 16, WIDE), bf16), jax.ShapeDtypeStruct((4, KP, 16, 512), bf16)],
        compiler_params=pltpu.CompilerParams(vmem_limit_bytes=24 << 20),
        cost_estimate=pl.CostEstimate(flops=25 * 10 ** 9, bytes_accessed=8 << 20, transcendentals=0),
        name="bwd",
    )(steps, pos, kpos, stat, own, oth, *dos, kt)


def pack_kernel(q_hbm, k_hbm, v_hbm, do_hbm, out_hbm, q_ref, k_ref, v_ref, do_ref, out_ref, in_sem, out_sem):
    loads = [pltpu.make_async_copy(src, dst, in_sem.at[i])
             for i, (src, dst) in enumerate(((q_hbm, q_ref), (k_hbm, k_ref), (v_hbm, v_ref), (do_hbm, do_ref)))]
    for load in loads:
        load.start()
    for load in loads:
        load.wait()
    stores = []
    for j in range(4):
        for u in range(8):
            for g in range(2):
                at = u * 2 + g
                tokens = slice(16 * u, 16 * u + 16)
                for r in range(4):
                    head = 512 * g + HD * ((j - r) % 4)
                    out_ref[j, at, :, r * HD:r * HD + HD] = q_ref[tokens, head:head + HD]
                head = 512 * g + HD * j
                out_ref[j, at, :, 1024:1152] = do_ref[tokens, head:head + HD]
                for h in (0, 1):
                    rows = slice(32 * j + 16 * h, 32 * j + 16 * h + 16)
                    out_ref[j, at, :, 512 + 256 * h:640 + 256 * h] = k_ref[rows, HD * g:HD * g + HD]
                    out_ref[j, at, :, 640 + 256 * h:768 + 256 * h] = v_ref[rows, HD * g:HD * g + HD]
        stores.append(pltpu.make_async_copy(out_ref.at[j], out_hbm.at[j], out_sem.at[j]))
        stores[-1].start()
    for store in stores:
        store.wait()


def pack(q, k, v, do):
    any_spec = pl.BlockSpec(memory_space=pltpu.HBM)
    return pl.pallas_call(
        pack_kernel, in_specs=[any_spec] * 4, out_specs=any_spec,
        out_shape=jax.ShapeDtypeStruct((4, 16, 16, WIDE), bf16),
        scratch_shapes=[pltpu.VMEM((128, 1024), bf16), pltpu.VMEM((128, 256), bf16), pltpu.VMEM((128, 256), bf16),
                        pltpu.VMEM((128, 1024), bf16), pltpu.VMEM((4, 16, 16, WIDE), bf16), pltpu.SemaphoreType.DMA((4,)), pltpu.SemaphoreType.DMA((4,))],
        compiler_params=pltpu.CompilerParams(vmem_limit_bytes=60 << 20), name="pack",
    )(q, k, v, do)


def gather_kernel(oth_ref, o0_ref, o1_ref, o2_ref, o3_ref, out_ref, sum_ref):
    out_ref[...] = oth_ref[...]
    total = o0_ref[...].astype(f32) + o1_ref[...].astype(f32) + o2_ref[...].astype(f32) + o3_ref[...].astype(f32)
    sum_ref[...] = total.astype(bf16)


def gather_parts(oth, heads):
    return pl.pallas_call(
        gather_kernel, in_specs=[VMEM] * 5, out_specs=[VMEM] * 2,
        out_shape=[jax.ShapeDtypeStruct(oth.shape, bf16), jax.ShapeDtypeStruct(heads[0].shape, bf16)],
        compiler_params=pltpu.CompilerParams(vmem_limit_bytes=12 << 20), name="gather_parts",
    )(oth, *heads)


def add_kernel(own_ref, other_ref, head_ref, out_ref):
    out_ref[..., :512] = (own_ref[..., :512].astype(f32) + other_ref[...].astype(f32)).astype(bf16)
    out_ref[..., 512:] = head_ref[...]


def add_parts(out, other, head):
    block = lambda columns: pl.BlockSpec((1, KP, 16, columns), lambda i: (i, 0, 0, 0))
    return pl.pallas_call(
        add_kernel, grid=(4,), in_specs=[block(640), block(512), block(HD)], out_specs=block(640),
        out_shape=jax.ShapeDtypeStruct(out.shape, bf16), input_output_aliases={0: 0},
        compiler_params=pltpu.CompilerParams(vmem_limit_bytes=12 << 20), name="add_parts",
    )(out, other, head)


def sum_kernel(in_ref, at_ref, qg_ref, kg_ref, vg_ref):
    for u in range(8):
        for g in range(2):
            rows = slice(16 * u, 16 * u + 16)
            for h in range(4):
                cols = slice(512 * g + HD * h, 512 * g + HD * h + HD)
                at_ref[rows, cols] = in_ref[h * 16 + u * 2 + g, :, 512:640]
                first = [640 + HD * ((j - h) % 4) for j in range(4)]
                parts = [in_ref[j * 16 + u * 2 + g, :, first[j]:first[j] + HD].astype(f32) for j in range(4)]
                qg_ref[rows, cols] = (parts[0] + parts[1] + parts[2] + parts[3]).astype(bf16)
    for j in range(4):
        for g in range(2):
            for h in (0, 1):
                rows, cols = slice(32 * j + 16 * h, 32 * j + 16 * h + 16), slice(HD * g, HD * g + HD)
                both = sum(in_ref[j * 16 + u * 2 + g, :, 256 * h:256 * h + 256].astype(f32) for u in range(8))
                kg_ref[rows, cols] = both[:, :HD].astype(bf16)
                vg_ref[rows, cols] = both[:, HD:].astype(bf16)


def sum_pieces(pieces):
    big, small = jax.ShapeDtypeStruct((128, 1024), bf16), jax.ShapeDtypeStruct((128, 256), bf16)
    return pl.pallas_call(
        sum_kernel, in_specs=[VMEM], out_specs=[VMEM] * 4, out_shape=[big, big, small, small],
        compiler_params=pltpu.CompilerParams(vmem_limit_bytes=12 << 20), name="sum_pieces",
    )(pieces)


def make_plan(lengths, core, u, j):
    n = jnp.arange(QT + 1, dtype=i32)[:, None, None]
    x = jnp.arange(4, dtype=i32)[None, :, None]
    t = jnp.arange(16, dtype=i32)[None, None, :]
    pos = (512 * (2 * n + core) + 128 * x + 16 * u + t).reshape(QT + 1, 64)
    docs = jnp.arange(lengths.shape[0])
    ends = jnp.sum(jnp.where(docs[:, None] <= docs[None, :], lengths[:, None], 0), axis=0)
    start = jnp.sum(jnp.where(ends[None, None, :] <= pos[:, :, None], lengths, 0), axis=-1)
    rows = jnp.stack([jnp.tile(pos, (1, 4)), jnp.tile(start, (1, 4))], axis=1).astype(i32)
    low = (start[:QT, 0] // 1024)[None, :]
    plain_low = ((start[:QT, -1] + 1023) // 1024)[None, :]
    d = jnp.arange(KP, dtype=i32)[:, None]
    m = jnp.arange(QT, dtype=i32)[None, :]
    live = (m - d >= 0) & (m - d >= low)
    plain = live & (d > 0) & (m - d >= plain_low)
    code = (m * 256 + m - d).reshape(1, QT * KP)
    order = jnp.arange(QT * KP, dtype=i32)
    earlier = order[:, None] < order[None, :]
    at = jnp.arange(LIST, dtype=i32)[:, None]

    def ranks(mask):
        return jnp.sum((earlier & mask.reshape(QT * KP, 1)).astype(i32), axis=0, keepdims=True)

    def compact(mask, rank):
        mask = mask.reshape(1, QT * KP)
        listed = QT * 256 + jnp.sum(jnp.where(mask & (rank == at), code - QT * 256, 0), axis=1)
        return jnp.where(at[:, 0] == LIST - 1, jnp.sum(mask.astype(i32)), listed)

    rank = ranks(plain)
    plain = plain & (rank.reshape(KP, QT) < jnp.sum(plain.astype(i32)) // TRIP * TRIP)
    edge = live & ~plain
    steps = jnp.stack([compact(plain, rank), compact(edge, ranks(edge))]).astype(i32)
    r = jnp.arange(256, dtype=i32)
    parity = jnp.where(r < 128, core, 1 - core)
    kpos = 512 * parity + 128 * (r % 64 // 16) + 32 * j + 16 * (r // 64 % 2) + r % 16
    return steps, rows, jnp.broadcast_to(kpos[:, None], (256, 128)).astype(i32)


PLANE = ("head", "inner", "zl")


def on_device(query_rows, key_rows, value_rows, out_grad, lengths):
    j, u, core = (lax.axis_index(name) for name in ("head", "inner", "core"))
    swap = [(0, 1), (1, 0)]
    steps, pos, kpos = make_plan(lengths, core, u, j)
    pieces = pack(query_rows.reshape(128, 1024), key_rows.reshape(128, 256), value_rows.reshape(128, 256),
                  out_grad.reshape(128, 1024))
    own = lax.all_to_all(pieces.reshape(64, 16, WIDE), PLANE, 0, 0, tiled=True).reshape(4, QT, 16, WIDE)
    own, steps, pos, kpos = lax.optimization_barrier((own, steps, pos, kpos))
    oth = lax.ppermute(own[..., 512:1024], "core", swap)

    def along(x, k):
        return lax.ppermute(x, "head", [(i, (i + k) % 4) for i in range(4)])

    def spread(arrays, sign):
        moved = {k: along(arrays[k], sign * k) for k in (3, 1, 2)}
        return [arrays[0]] + [moved[k] for k in (1, 2, 3)]

    do = own[..., 1024:]
    dos = spread([do] * 4, 1)
    ot, st = fwd(steps, pos, kpos, own, oth)
    part = delta(st, ot, dos)
    stat, *heads = scale(spread([part] * 4, 1), st, ot)
    heads = spread(heads, -1)
    out, oth_out = bwd(steps, pos, kpos, stat, own, oth, dos, turn_keys(own, oth))
    oth_out, head = gather_parts(oth_out, heads)
    out = add_parts(out, lax.ppermute(oth_out, "core", swap), head)
    out = lax.all_to_all(out.reshape(64, 16, WIDE), PLANE, 0, 0, tiled=True)
    attended, query_grad, key_grad, value_grad = sum_pieces(out)
    return (attended.reshape(1, 1, 128, 1024), query_grad.reshape(1, 1, 128, 1024),
            key_grad.reshape(1, 1, 128, 256), value_grad.reshape(1, 1, 128, 256))


def solution(mesh):
    finer = Mesh(mesh.devices.reshape(4, 8, 2, 2), ("head", "inner", "zl", "core"))
    placed = P(("inner", "zl", "core"), "head", None, None)
    return jax.shard_map(
        on_device,
        mesh=finer,
        in_specs=(placed, placed, placed, placed, P()),
        out_specs=(placed, placed, placed, placed),
        check_vma=False,
    )
```
